256 devices in a mesh: dp: 8 (over x, core), vocab: 32 (over y, z).
Axes of the slice: x: 4, y: 4, z: 8, core: 2. Of those that a mesh axis runs over, the one named last changes fastest.
Arguments:
- hidden_states: bfloat16 [1024, 5120], P('dp'), may hold values from -70 to 70, as said below
- head: bfloat16 [5120, 77824], P('dp', 'vocab'), may hold values from -2 to 2
- token_ids: int32 [1024], P('dp'), may hold values from 0 to 77823
- valid: int32 [1024], P('dp'), may hold values 0 or 1
- advantage: float32 [1024], P('dp'), may hold values from -6 to 6
Outputs:
- hidden_grad: float32 [1024, 5120], P('vocab', 'dp')
- head_grad: float32 [5120, 77824], P('dp', 'vocab')
The draws below stay inside these ranges and needn't reach their ends.
Inputs may be any that keep to these rules, and one draw needn't show every extreme that they name: `hidden_states`: hidden states of order one, some tokens larger than others.
All inputs are finite; a program needn't handle non-finite values. No bound on the sum of `valid` on one device may be relied on, other than what follows from the above.
Results may differ from the reference program's by a relative error of at most 0.0034.
Values may be sent and summed in bfloat16 or wider, within the bound.
No kernel may reach another device: no remote copies, remote signals or barrier semaphores. Data moves between devices by JAX's collectives and lax.ppermute only.
A program may use at most 128 MiB of HBM per device.

```python
import jax
import jax.numpy as jnp
from jax import lax

H = 5120
VOC_DEV = 2432
ROUNDS = 24
TOKENS = 1024
VOCAB = 77824
N_VOCAB = 32


def draw_hidden_states(key, part):
    key = jax.random.fold_in(key, 11)
    first, second = jax.random.split(key, 2)
    base = jax.random.truncated_normal(first, -4.0, 4.0, (TOKENS, H), jnp.float32)
    scales = jnp.exp(jax.random.uniform(second, (TOKENS, 1), jnp.float32, jnp.log(0.3), jnp.log(1.0)))
    values = base * scales
    return values.astype(jnp.bfloat16)


def touch_ends(drawn, stream_key, least, high):
    place = [jax.random.randint(jax.random.fold_in(stream_key, axis), (), 0, length) for axis, length in enumerate(drawn.shape)]
    longest = drawn.shape.index(max(drawn.shape))
    beside = place[:longest] + [(place[longest] + 1) % drawn.shape[longest]] + place[longest + 1:]
    return drawn.at[tuple(place)].set(least).at[tuple(beside)].set(high)


def block_levels(rng, dims, cuts, low, largest):
    level, own = 1.0, jax.random.fold_in(rng, 6)
    for dim, shards_of in cuts:
        steps = jnp.exp(jax.random.uniform(jax.random.fold_in(own, dim), (shards_of,), jnp.float32, low / len(cuts), largest / len(cuts)))
        level = level * jnp.repeat(steps, dims[dim] // shards_of).reshape([-1 if axis == dim else 1 for axis in range(len(dims))])
    return level


def gaussian(rng, shape, deviation, most, cuts=(), kind=jnp.bfloat16):
    entries = jax.random.normal(rng, shape, jnp.float32) * deviation
    if len(cuts) > 0:
        entries = block_levels(rng, shape, cuts, -0.22, 0.18) * entries
    return jnp.clip(entries, min=-most, max=most).astype(kind)


def setup_inputs(seed: int = 0) -> dict:
    arg_keys = jax.random.split(jax.random.key(seed), 6)
    return {
        "hidden_states": draw_hidden_states(jax.random.fold_in(arg_keys[5], 71), 0),
        "head": gaussian(arg_keys[1], (H, VOCAB), 0.15, 2.0, ((0, 8), (1, 32))),
        "token_ids": touch_ends(jax.random.randint(arg_keys[2], (TOKENS,), 0, VOCAB), jax.random.fold_in(arg_keys[2], 1), 0, VOCAB - 1).astype(jnp.int32),
        "valid": touch_ends((jax.random.randint(arg_keys[3], (TOKENS,), 0, 4) < 3).astype(jnp.int32), jax.random.fold_in(arg_keys[3], 1), 0, 1),
        "advantage": gaussian(arg_keys[4], (TOKENS,), 1.0, 6.0, ((0, 8),), jnp.float32),
    }


ramp_width = 0.5


def reference(hidden_states, head, token_ids, valid, advantage):
    blocks = N_VOCAB
    width = VOC_DEV
    columns_iota = jnp.arange(width, dtype=jnp.int32)

    def block_logits(index):
        start = (index * width).astype(jnp.int32)
        part = lax.dynamic_slice_in_dim(head, start, width, 1)
        logits = jnp.dot(hidden_states, part, preferred_element_type=jnp.float32)
        hit = (columns_iota[None, :] + start) == token_ids[:, None]
        return part, logits, hit

    def stats_step(carry, index):
        highest, total, moment, picked = carry
        part, logits, hit = block_logits(index)
        newest = jnp.maximum(highest, jnp.max(logits, axis=1))
        factor = jnp.exp(highest - newest)
        shifted = jnp.exp(logits - newest[:, None])
        total = total * factor + jnp.sum(shifted, axis=1)
        moment = moment * factor + jnp.sum(shifted * logits, axis=1)
        picked = picked + jnp.sum(jnp.where(hit, logits, 0.0), axis=1)
        return (newest, total, moment, picked), None

    start_carry = (jnp.full((TOKENS,), -jnp.inf, jnp.float32), jnp.zeros((TOKENS,), jnp.float32),
                   jnp.zeros((TOKENS,), jnp.float32), jnp.zeros((TOKENS,), jnp.float32))
    (highest, total, moment, picked), _ = lax.scan(stats_step, start_carry, jnp.arange(blocks, dtype=jnp.int32))
    normal = highest + jnp.log(total)
    entropy = normal - moment / total
    logprob = picked - normal

    quota = jnp.sum(valid) // 5
    low = jnp.float32(0.0)
    high = jnp.log(jnp.float32(VOCAB)) + 1.0
    for step in range(ROUNDS):
        middle = (low + high) * 0.5
        above = jnp.sum(jnp.where(entropy > middle, valid, 0))
        more = above > quota
        low, high = jnp.where(more, middle, low), jnp.where(more, high, middle)
    threshold = high
    validf = valid.astype(jnp.float32)
    gate = validf * jnp.clip((entropy - threshold) / ramp_width + 0.5, 0.0, 1.0)
    coef = -(gate * advantage)

    def grad_step(partial_h, index):
        part, logits, hit = block_logits(index)
        probs = jnp.exp(logits - normal[:, None])
        slopes = (coef[:, None] * (hit.astype(jnp.float32) - probs)).astype(jnp.bfloat16)
        grad_block = lax.dot_general(hidden_states, slopes, (((0,), (0,)), ((), ())), preferred_element_type=jnp.float32)
        partial_h = partial_h + lax.dot_general(slopes, part, (((1,), (1,)), ((), ())), preferred_element_type=jnp.float32)
        return partial_h, grad_block

    hidden_grad, grad_blocks = lax.scan(grad_step, jnp.zeros((TOKENS, H), jnp.float32), jnp.arange(blocks, dtype=jnp.int32))
    head_grad = jnp.transpose(grad_blocks, (1, 0, 2)).reshape(H, VOCAB)
    return hidden_grad, head_grad
```

```python
import functools

import jax
import jax.numpy as jnp
import numpy as np
from jax import lax
from jax.experimental import pallas as pl
from jax.experimental.pallas import tpu as pltpu
from jax.sharding import Mesh, PartitionSpec as P

ROUNDS = 24
LEVELS = 6
CAP = 16
CAP_OWNER = 48

ramp_width = 0.5
DP = ("x", "c")
VOC = ("y", "z")
f32 = jnp.float32
bf16 = jnp.bfloat16


def ring(n, shift):
    return [(i, (i + shift) % n) for i in range(n)]


SWAP = [(0, 1), (1, 0)]


def dense(hidden_states, head, token_ids, valid, advantage):
    voc_cols = head.shape[1]
    columns = lax.all_to_all(hidden_states, DP, split_axis=1, concat_axis=0, tiled=True)
    logits = lax.psum_scatter(
        jnp.dot(columns, head, preferred_element_type=f32), DP, scatter_dimension=0, tiled=True
    )
    offset = lax.axis_index(VOC) * voc_cols
    hit = jnp.arange(voc_cols, dtype=jnp.int32)[None, :] + offset == token_ids[:, None]
    highest = lax.pmax(jnp.max(logits, axis=1), VOC)
    shifted = jnp.exp(logits - highest[:, None])
    total, moment = lax.psum((jnp.sum(shifted, axis=1), jnp.sum(shifted * logits, axis=1)), VOC)
    normal = highest + jnp.log(total)
    entropy = normal - moment / total
    validf = valid.astype(f32)
    start_high = jnp.log(f32(voc_cols * lax.axis_size(VOC))) + 1.0
    counted = lax.psum(jnp.sum(validf), DP)
    quota = jnp.floor((counted + 0.5) * 0.2)

    def round_step(step, bounds):
        low, high = bounds
        middle = (low + high) * 0.5
        above = lax.psum(jnp.sum(jnp.where(entropy > middle, validf, 0.0)), DP)
        more = above > quota
        return (jnp.where(more, middle, low), jnp.where(more, high, middle))

    _, threshold = lax.fori_loop(0, ROUNDS, round_step, (f32(0.0), start_high))
    gate = validf * jnp.clip((entropy - threshold) / ramp_width + 0.5, 0.0, 1.0)
    coef = -(gate * advantage)
    probs = jnp.exp(logits - normal[:, None])
    slopes = (coef[:, None] * (hit.astype(f32) - probs)).astype(bf16)
    piece = lax.all_gather(slopes, DP, axis=0, tiled=True)
    head_grad = lax.dot_general(columns, piece, (((0,), (0,)), ((), ())), preferred_element_type=f32)
    product = lax.dot_general(piece, head, (((1,), (1,)), ((), ())), preferred_element_type=f32)
    return lax.psum_scatter(product, VOC, scatter_dimension=0, tiled=True), head_grad


def bisect(entropy, counted, start_high):
    columns = jnp.transpose(entropy)
    quota = jnp.floor((counted + 0.5) * 0.2)
    lane = lax.broadcasted_iota(jnp.int32, (1, 128), 1)
    leaves = 1 << LEVELS
    low = jnp.zeros((1, 128), f32)
    high = jnp.full((1, 128), start_high, f32)
    for _ in range(ROUNDS // LEVELS):
        for level in range(LEVELS):
            middle = (low + high) * 0.5
            bit = ((lane >> (LEVELS - 1 - level)) & 1) == 1
            low, high = jnp.where(bit, middle, low), jnp.where(bit, high, middle)
        above = jnp.zeros((128, 128), f32)
        for i in range(8):
            above = above + jnp.where(columns[:, i : i + 1] > low, 1.0, 0.0)
        above = jnp.sum(above, axis=0, keepdims=True)
        more = jnp.where(((above > quota) | (lane == 0)) & (lane < leaves), 1.0, 0.0)
        here = lane == jnp.sum(more, axis=1, keepdims=True).astype(jnp.int32) - 1
        low, high = (
            jnp.broadcast_to(jnp.sum(jnp.where(here, v, 0.0), axis=1, keepdims=True), (1, 128))
            for v in (low, high)
        )
    return high[:, :1]


def call(kernel, out, args, scratch=(), vmem=16, smem=0, **kw):
    specs = [pl.BlockSpec(memory_space=pltpu.SMEM)] * smem
    specs += [pl.BlockSpec(memory_space=pltpu.VMEM)] * (len(args) - smem)
    return pl.pallas_call(
        kernel,
        in_specs=specs,
        out_shape=out,
        scratch_shapes=list(scratch),
        compiler_params=pltpu.CompilerParams(vmem_limit_bytes=vmem << 20),
        **kw,
    )(*args)


def struct(shape, dtype):
    return jax.ShapeDtypeStruct(shape, dtype)


LN2_64 = float(np.log(2.0) / 64.0)


def partial_kernel(at, b0, b1, b2, b3, head, other, own, q1, q2, q3, mine, theirs, part):
    tokens = b0.shape[0]
    rows, cols = head.shape
    here = pl.ds(pl.multiple_of(at[1] * rows, 128), rows)
    there = pl.ds(pl.multiple_of((1 - at[1]) * rows, 128), rows)
    for s, block in enumerate((b0, b1, b2, b3)):
        mine[s * tokens : (s + 1) * tokens, :] = block[:, here]
        theirs[s * tokens : (s + 1) * tokens, :] = block[:, there]

    def tile(at_col, size):
        span = pl.ds(at_col, size)
        part[:, span] = jnp.dot(mine[...], head[:, span], preferred_element_type=f32) + jnp.dot(
            theirs[...], other[:, span], preferred_element_type=f32
        )

    wide = cols // 256

    @pl.loop(0, wide)
    def _(i):
        tile(pl.multiple_of(i * 256, 256), 256)

    if cols > wide * 256:
        tile(wide * 256, cols - wide * 256)
    own[...] = part[0:tokens, :]
    step = 32
    for s, out in ((1, q1), (2, q2), (3, q3)):

        @pl.loop(0, tokens // step)
        def _(i, s=s, out=out):
            to = pl.ds(pl.multiple_of(i * step, step), step)
            block = part[pl.ds(pl.multiple_of(s * tokens + i * step, step), step), :]
            top = jnp.maximum(jnp.max(jnp.abs(block), axis=1, keepdims=True), 1e-30)
            power = jnp.ceil(jnp.log(top) * (1.0 / LN2_64)) + 1.0
            fixed = jnp.round(block * (jnp.exp(power * -LN2_64) * 32766.0))
            out[to, 0:cols] = fixed.astype(jnp.int32).astype(jnp.int16)
            wide_power = jnp.broadcast_to(power.astype(jnp.int32), (step, 128))
            out[to, cols : cols + 128] = wide_power.astype(jnp.int16)


def total_kernel(own, q1, q2, q3, logits, sent, stats):
    tokens, cols = own.shape
    step = 16
    lane = lax.broadcasted_iota(jnp.int32, (step, 128), 1)

    @pl.loop(0, tokens // step)
    def _(i):
        at = pl.ds(pl.multiple_of(i * step, step), step)
        value = own[at, :]
        for q in (q1, q2, q3):
            power = q[at, cols : cols + 128].astype(jnp.int32).astype(f32)[:, :1]
            scale = jnp.exp(power * LN2_64) * (1.0 / 32766.0)
            value = value + q[at, 0:cols].astype(jnp.int32).astype(f32) * scale
        logits[at, :] = value
        high = jnp.max(value, axis=1, keepdims=True)
        shifted = jnp.exp(value - high)
        total = jnp.sum(shifted, axis=1, keepdims=True)
        moment = jnp.sum(shifted * value, axis=1, keepdims=True)
        stats[at, :] = jnp.where(lane == 0, high, jnp.where(lane == 1, total, moment))

    rows = jnp.transpose(stats[...])[0:8, :]
    for i in range(sent.shape[0]):
        sent[i] = rows


def merge_kernel(parts, valid, advantage, sent):
    high = parts[0, 0:1, :]
    for i in range(1, parts.shape[0]):
        high = jnp.maximum(high, parts[i, 0:1, :])
    sums = jnp.zeros((8, 128), f32)
    for i in range(parts.shape[0]):
        sums = sums + jnp.exp(parts[i, 0:1, :] - high) * parts[i]
    row = lax.broadcasted_iota(jnp.int32, (8, 128), 0)
    out = jnp.where(row == 0, high, sums)
    out = jnp.where(row == 3, valid[...].astype(f32), jnp.where(row == 4, advantage[...], out))
    for i in range(sent.shape[0]):
        sent[i] = out


def plan_kernel(start_high, cap_owner, parts, coef_out, normal_out, packed_out, slot_out, flag, rows):
    owners = 8
    ny = parts.shape[0] // owners
    for o in range(owners):
        high = parts[o * ny, 0:1, :]
        for y in range(1, ny):
            high = jnp.maximum(high, parts[o * ny + y, 0:1, :])
        sums = jnp.zeros((8, 128), f32)
        for y in range(ny):
            sums = sums + jnp.exp(parts[o * ny + y, 0:1, :] - high) * parts[o * ny + y]
        row = lax.broadcasted_iota(jnp.int32, (8, 128), 0)
        normal = high + jnp.log(sums[1:2, :])
        entropy = normal - sums[2:3, :] / sums[1:2, :]
        rows[o] = jnp.where(row == 0, normal, jnp.where(row == 1, entropy, parts[o * ny]))
    normal, entropy, valid, advantage = (
        jnp.concatenate([rows[o, k : k + 1, :] for o in range(owners)], axis=0) for k in (0, 1, 3, 4)
    )
    counted = jnp.sum(jnp.sum(valid, axis=1, keepdims=True), axis=0, keepdims=True)
    threshold = bisect(jnp.where(valid > 0.0, entropy, -jnp.inf), counted, start_high)
    gate = valid * jnp.clip((entropy - threshold) / ramp_width + 0.5, 0.0, 1.0)
    coef = -(gate * advantage)
    active = coef != 0.0
    activef = active.astype(f32)
    i = lax.broadcasted_iota(jnp.int32, (128, 128), 0)
    j = lax.broadcasted_iota(jnp.int32, (128, 128), 1)
    ahead = (i < j).astype(f32)
    group = 128 // (32 // owners)
    same = (i // group == j // group).astype(f32)
    rank_owner = jnp.dot(activef, ahead, preferred_element_type=f32)
    rank_group = jnp.dot(activef, ahead * same, preferred_element_type=f32)
    start = (lax.broadcasted_iota(jnp.int32, (8, 128), 1) // group * CAP).astype(f32)
    coef_out[...] = coef
    normal_out[...] = normal
    packed_out[...] = jnp.where(active, rank_owner, -1.0)
    slot_out[...] = jnp.where(active, rank_group + start, -1.0)
    over = jnp.where(active & ((rank_owner >= cap_owner) | (rank_group >= CAP)), 1.0, 0.0)
    flag[0, 0] = jnp.max(over).astype(jnp.int32)


def as_columns(rows):
    row = lax.broadcasted_iota(jnp.int32, (8, 128), 0)
    out = jnp.zeros((8, 128), f32)
    for k, value in enumerate(rows):
        out = jnp.where(row == k, value, out)
    return jnp.transpose(out)


def one_hot(count, slots):
    row = lax.broadcasted_iota(jnp.int32, (count, 128), 0).astype(f32)
    return (row == slots).astype(f32).astype(bf16)


def slopes_kernel(at, logits, coef_all, normal_all, packed_all, ids, out):
    me = pl.ds(at[2], 1)
    count = out.shape[0]
    columns = as_columns([coef_all[me, :], normal_all[me, :], ids[...].astype(f32)])
    coef, normal, token = columns[:, 0:1], columns[:, 1:2], columns[:, 2:3].astype(jnp.int32) - at[3]
    choose = one_hot(count, packed_all[me, :])
    lane = lax.broadcasted_iota(jnp.int32, (128, 128), 1)
    for k in range(logits.shape[1] // 128):
        span = slice(k * 128, (k + 1) * 128)
        hit = (lane + k * 128 == token).astype(f32)
        slopes = (coef * (hit - jnp.exp(logits[:, span] - normal))).astype(bf16)
        out[:, span] = jnp.dot(choose, slopes, preferred_element_type=f32).astype(bf16)


def product_kernel(nx, at, mine, theirs, head, packed_all, slot_all, out, held):
    half = mine.shape[0]
    count = half // nx
    for k, rows in enumerate((mine, theirs)):
        held[k * half : (k + 1) * half, :] = lax.dot_general(
            rows[...], head[...], (((1,), (1,)), ((), ())), preferred_element_type=f32
        ).astype(bf16)
    size = out.shape[0] // (2 * nx)
    for owner in range(2 * nx):
        to, core = owner // 2, owner % 2
        source = lax.rem(at[0] - to + nx, nx) * count + lax.rem(at[1] + core, 2) * half
        block = held[pl.ds(pl.multiple_of(source, 16), count), :]
        spread = lax.dot_general(
            one_hot(size, slot_all[owner : owner + 1, :]),
            one_hot(count, packed_all[owner : owner + 1, :]),
            (((1,), (1,)), ((), ())),
            preferred_element_type=f32,
        ).astype(bf16)
        out[owner * size : (owner + 1) * size, :] = jnp.dot(
            spread, block, preferred_element_type=f32
        ).astype(bf16)


def outer_kernel(nx, at, packed_all, hid_mine, hid_theirs, mine, theirs, out, held):
    half = mine.shape[0]
    count = half // nx
    for k, hidden in enumerate((hid_mine, hid_theirs)):
        for s in range(nx):
            owner = lax.rem(at[0] - s + nx, nx) * 2 + lax.rem(at[1] + k, 2)
            choose = one_hot(count, packed_all[pl.ds(owner, 1), :])
            to = k * half + s * count
            held[to : to + count, :] = jnp.dot(
                choose, hidden[s * 128 : (s + 1) * 128, :], preferred_element_type=f32
            ).astype(bf16)
    total = jnp.zeros(out.shape, f32)
    for k, rows in enumerate((mine, theirs)):
        total = total + lax.dot_general(
            held[k * half : (k + 1) * half, :],
            rows[...],
            (((0,), (0,)), ((), ())),
            preferred_element_type=f32,
        )
    out[...] = total


def sum_kernel(at, parts, slot_all, out, ranks):
    n_voc = parts.shape[0] // CAP
    total = parts[0:CAP, :].astype(f32)
    for i in range(1, n_voc):
        total = total + parts[i * CAP : (i + 1) * CAP, :].astype(f32)
    group = out.shape[0]
    per_owner = 128 // group
    owner, place = at[4] // per_owner, lax.rem(at[4], per_owner)
    ranks[...] = as_columns([slot_all[pl.ds(owner, 1), :]])
    rank = ranks[pl.ds(pl.multiple_of(place * group, group), group), :][:, 0:1]
    rank = rank - (place * CAP).astype(f32)
    rows = jnp.zeros(out.shape, f32)
    for r in range(CAP):
        rows = rows + jnp.where(rank == float(r), total[r : r + 1, :], 0.0)
    out[...] = rows


def shards(hidden_states, head, token_ids, valid, advantage):
    tokens, width = hidden_states.shape
    rows, voc_cols = head.shape
    nx, n_voc, n_dp = lax.axis_size("x"), lax.axis_size(VOC), lax.axis_size(DP)
    x, c, block = lax.axis_index("x"), lax.axis_index("c"), lax.axis_index(VOC)
    at = jnp.stack([x, c, x * 2 + c, block * voc_cols, block]).astype(jnp.int32)
    chip_rows = width // nx

    head_other = lax.ppermute(head, "c", SWAP)

    def block_for(to):
        return lax.dynamic_slice(hidden_states, (0, to * chip_rows), (tokens, chip_rows))

    came = {s: lax.ppermute(block_for((x + s) % nx), "x", ring(nx, s)) for s in (2, 1, 3)}
    packed = struct((tokens, voc_cols + 128), jnp.int16)
    own, q1, q2, q3, hid_mine, hid_send = call(
        partial_kernel,
        [struct((tokens, voc_cols), f32), packed, packed, packed]
        + [struct((nx * tokens, rows), bf16)] * 2,
        [at, block_for(x), came[1], came[2], came[3], head, head_other],
        [pltpu.VMEM((nx * tokens, voc_cols), f32)],
        vmem=32,
        smem=1,
    )
    sent = {s: lax.ppermute(q, "x", ring(nx, -s)) for s, q in ((2, q2), (1, q1), (3, q3))}
    hid_theirs = lax.ppermute(hid_send, "c", SWAP)
    logits, stats = call(
        total_kernel,
        [struct((tokens, voc_cols), f32), struct((lax.axis_size("z"), 8, 128), f32)],
        [own, sent[1], sent[2], sent[3]],
        [pltpu.VMEM((tokens, 128), f32)],
    )

    stats = lax.all_to_all(stats, "z", 0, 0, tiled=True)
    everyone = DP + ("y",)
    stats = call(
        merge_kernel,
        struct((lax.axis_size(everyone), 8, 128), f32),
        [stats, valid.reshape(1, tokens), advantage.reshape(1, tokens)],
    )
    stats = lax.all_to_all(stats, everyone, 0, 0, tiled=True)
    start_high = float(np.float32(np.log(np.float32(voc_cols * n_voc))) + np.float32(1.0))
    table = struct((n_dp, tokens), f32)
    coef_all, normal_all, packed_all, slot_all, flag = call(
        functools.partial(plan_kernel, start_high, CAP_OWNER),
        [table] * 4 + [struct((1, 1), jnp.int32)],
        [stats],
        [pltpu.VMEM((n_dp, 8, 128), f32)],
        out_specs=[pl.BlockSpec(memory_space=pltpu.VMEM)] * 4 + [pl.BlockSpec(memory_space=pltpu.SMEM)],
    )

    def sparse(_):
        piece = call(
            slopes_kernel,
            struct((CAP_OWNER, voc_cols), bf16),
            [at, logits, coef_all, normal_all, packed_all, token_ids.reshape(1, tokens)],
            smem=1,
        )
        pieces = {s: lax.ppermute(piece, "x", ring(nx, s)) for s in (2, 1, 3)}
        mine = jnp.concatenate([piece, pieces[1], pieces[2], pieces[3]], axis=0)
        theirs = lax.ppermute(mine, "c", SWAP)
        product = call(
            functools.partial(product_kernel, nx),
            struct((n_voc * CAP, rows), bf16),
            [at, mine, theirs, head, packed_all, slot_all],
            [pltpu.VMEM((2 * nx * CAP_OWNER, rows), bf16)],
            smem=1,
        )
        parts = lax.all_to_all(product, VOC, 0, 0, tiled=True)
        tile = 128
        head_grad = pl.pallas_call(
            functools.partial(outer_kernel, nx),
            grid=(rows // tile,),
            in_specs=[
                pl.BlockSpec(memory_space=pltpu.SMEM),
                pl.BlockSpec((n_dp, tokens), lambda i: (0, 0)),
                pl.BlockSpec((nx * tokens, tile), lambda i: (0, i)),
                pl.BlockSpec((nx * tokens, tile), lambda i: (0, i)),
                pl.BlockSpec((nx * CAP_OWNER, voc_cols), lambda i: (0, 0)),
                pl.BlockSpec((nx * CAP_OWNER, voc_cols), lambda i: (0, 0)),
            ],
            out_specs=pl.BlockSpec((tile, voc_cols), lambda i: (i, 0)),
            out_shape=struct((rows, voc_cols), f32),
            scratch_shapes=[pltpu.VMEM((2 * nx * CAP_OWNER, tile), bf16)],
            compiler_params=pltpu.CompilerParams(vmem_limit_bytes=24 << 20),
            cost_estimate=pl.CostEstimate(
                flops=4 * nx * CAP_OWNER * rows * voc_cols,
                bytes_accessed=4 * rows * voc_cols,
                transcendentals=0,
            ),
        )(at, packed_all, hid_mine, hid_theirs, mine, theirs)
        hidden_grad = call(
            sum_kernel,
            struct((tokens * n_dp // n_voc, rows), f32),
            [at, parts, slot_all],
            [pltpu.VMEM((tokens, 8), f32)],
            smem=1,
        )
        return hidden_grad, head_grad

    def whole(_):
        return dense(hidden_states, head, token_ids, valid, advantage)

    return lax.cond(flag[0, 0] != 0, whole, sparse, 0)


def solution(mesh):
    chips = Mesh(mesh.devices.reshape(4, 2, 4, 8), DP + VOC)
    placed = (P(DP, None), P(DP, VOC), P(DP), P(DP), P(DP))
    return jax.shard_map(
        shards,
        mesh=chips,
        in_specs=placed,
        out_specs=(P(VOC, DP), P(DP, VOC)),
        check_vma=False,
    )
```

```python
import functools

import jax
import jax.numpy as jnp
import numpy as np
from jax import lax
from jax.experimental import pallas as pl
from jax.experimental.pallas import tpu as pltpu
from jax.sharding import Mesh, PartitionSpec as P

ROUNDS = 24
LEVELS = 6
CAP = 16
CAP_OWNER = 48
ORDER = (0, 1, 3, 2)

ramp_width = 0.5
DP = ("x", "c")
VOC = ("y", "z")
f32 = jnp.float32
bf16 = jnp.bfloat16


def ring(n, shift):
    return [(i, (i + shift) % n) for i in range(n)]


SWAP = [(0, 1), (1, 0)]


def dense(hidden_states, head, token_ids, valid, advantage):
    voc_cols = head.shape[1]
    columns = lax.all_to_all(hidden_states, DP, split_axis=1, concat_axis=0, tiled=True)
    logits = lax.psum_scatter(
        jnp.dot(columns, head, preferred_element_type=f32), DP, scatter_dimension=0, tiled=True
    )
    offset = lax.axis_index(VOC) * voc_cols
    hit = jnp.arange(voc_cols, dtype=jnp.int32)[None, :] + offset == token_ids[:, None]
    highest = lax.pmax(jnp.max(logits, axis=1), VOC)
    shifted = jnp.exp(logits - highest[:, None])
    total, moment = lax.psum((jnp.sum(shifted, axis=1), jnp.sum(shifted * logits, axis=1)), VOC)
    normal = highest + jnp.log(total)
    entropy = normal - moment / total
    validf = valid.astype(f32)
    start_high = jnp.log(f32(voc_cols * lax.axis_size(VOC))) + 1.0
    counted = lax.psum(jnp.sum(validf), DP)
    quota = jnp.floor((counted + 0.5) * 0.2)

    def round_step(step, bounds):
        low, high = bounds
        middle = (low + high) * 0.5
        above = lax.psum(jnp.sum(jnp.where(entropy > middle, validf, 0.0)), DP)
        more = above > quota
        return (jnp.where(more, middle, low), jnp.where(more, high, middle))

    _, threshold = lax.fori_loop(0, ROUNDS, round_step, (f32(0.0), start_high))
    gate = validf * jnp.clip((entropy - threshold) / ramp_width + 0.5, 0.0, 1.0)
    coef = -(gate * advantage)
    probs = jnp.exp(logits - normal[:, None])
    slopes = (coef[:, None] * (hit.astype(f32) - probs)).astype(bf16)
    piece = lax.all_gather(slopes, DP, axis=0, tiled=True)
    head_grad = lax.dot_general(columns, piece, (((0,), (0,)), ((), ())), preferred_element_type=f32)
    product = lax.dot_general(piece, head, (((1,), (1,)), ((), ())), preferred_element_type=f32)
    return lax.psum_scatter(product, VOC, scatter_dimension=0, tiled=True), head_grad


def bisect(entropy, counted, start_high):
    columns = jnp.transpose(entropy)
    quota = jnp.floor((counted + 0.5) * 0.2)
    lane = lax.broadcasted_iota(jnp.int32, (1, 128), 1)
    leaves = 1 << LEVELS
    low = jnp.zeros((1, 128), f32)
    high = jnp.full((1, 128), start_high, f32)
    for _ in range(ROUNDS // LEVELS):
        for level in range(LEVELS):
            middle = (low + high) * 0.5
            bit = ((lane >> (LEVELS - 1 - level)) & 1) == 1
            low, high = jnp.where(bit, middle, low), jnp.where(bit, high, middle)
        above = jnp.zeros((128, 128), f32)
        for i in range(8):
            above = above + jnp.where(columns[:, i : i + 1] > low, 1.0, 0.0)
        above = jnp.sum(above, axis=0, keepdims=True)
        more = jnp.where(((above > quota) | (lane == 0)) & (lane < leaves), 1.0, 0.0)
        here = lane == jnp.sum(more, axis=1, keepdims=True).astype(jnp.int32) - 1
        low, high = (
            jnp.broadcast_to(jnp.sum(jnp.where(here, v, 0.0), axis=1, keepdims=True), (1, 128))
            for v in (low, high)
        )
    return high[:, :1]


def call(kernel, out, args, scratch=(), vmem=16, smem=0, **kw):
    specs = [pl.BlockSpec(memory_space=pltpu.SMEM)] * smem
    specs += [pl.BlockSpec(memory_space=pltpu.VMEM)] * (len(args) - smem)
    return pl.pallas_call(
        kernel,
        in_specs=specs,
        out_shape=out,
        scratch_shapes=list(scratch),
        compiler_params=pltpu.CompilerParams(vmem_limit_bytes=vmem << 20),
        **kw,
    )(*args)


def struct(shape, dtype):
    return jax.ShapeDtypeStruct(shape, dtype)


def estimate(m, k, n):
    return pl.CostEstimate(flops=2 * m * k * n, bytes_accessed=2 * k * n, transcendentals=0)


LN2_64 = float(np.log(2.0) / 64.0)


def split_kernel(at, hidden, b0, b1, b2, b3):
    chip_rows = b0.shape[1]
    nx = hidden.shape[1] // chip_rows
    for s, out in enumerate((b0, b1, b2, b3)):
        to = lax.rem(at[0] + s, nx) * chip_rows
        out[...] = hidden[:, pl.ds(pl.multiple_of(to, 128), chip_rows)]


def turn_kernel(head, kept, turned):
    kept[...] = head[...]
    for k in range(head.shape[1] // 128):
        span = slice(k * 128, (k + 1) * 128)
        turned[span, :] = jnp.transpose(head[:, span])


def pack(block, out, to):
    step, cols = block.shape
    top = jnp.maximum(jnp.max(jnp.abs(block), axis=1, keepdims=True), 1e-30)
    power = jnp.ceil(jnp.log(top) * (1.0 / LN2_64)) + 1.0
    fixed = jnp.round(block * (jnp.exp(power * -LN2_64) * 32766.0))
    out[to, 0:cols] = fixed.astype(jnp.int32).astype(jnp.int16)
    wide_power = jnp.broadcast_to(power.astype(jnp.int32), (step, 128))
    out[to, cols : cols + 128] = wide_power.astype(jnp.int16)


def unpack(ref, at):
    cols = ref.shape[1] - 128
    power = ref[at, cols : cols + 128].astype(jnp.int32).astype(f32)[:, :1]
    return ref[at, 0:cols].astype(jnp.int32).astype(f32) * (jnp.exp(power * LN2_64) * (1.0 / 32766.0))


def over_columns(cols, tile):
    wide = cols // 256

    @pl.loop(0, wide)
    def _(i):
        tile(pl.multiple_of(i * 256, 256), 256)

    if cols > wide * 256:
        tile(wide * 256, cols - wide * 256)


def halves(at, rows):
    return (
        pl.ds(pl.multiple_of(at[1] * rows, 128), rows),
        pl.ds(pl.multiple_of((1 - at[1]) * rows, 128), rows),
    )


def far_kernel(at, block, head, other, low, high, tick, part):
    tokens = block.shape[0]
    rows, cols = head.shape
    here, there = halves(at, rows)

    def tile(start, size):
        span = pl.ds(start, size)
        part[:, span] = jnp.dot(block[:, here], head[:, span], preferred_element_type=f32) + jnp.dot(
            block[:, there], other[:, span], preferred_element_type=f32
        )

    over_columns(cols, tile)
    tick[...] = jnp.zeros(tick.shape, f32)
    step = 32
    for k, out in enumerate((low, high)):

        @pl.loop(0, tokens // 2 // step)
        def _(i, k=k, out=out):
            source = pl.multiple_of(k * (tokens // 2) + i * step, step)
            pack(part[pl.ds(source, step), :], out, pl.ds(pl.multiple_of(i * step, step), step))


def near_kernel(at, tick, b0, b1, b2, b3, head, other, own, p1, p3, mine, theirs):
    tokens = b0.shape[0]
    rows, cols = head.shape
    here, there = halves(at, rows)
    for k, block in enumerate((b0, b1, b3, b2)):
        mine[k * tokens : (k + 1) * tokens, :] = block[:, here]
        theirs[k * tokens : (k + 1) * tokens, :] = block[:, there]

    def tile(start, size):
        span = pl.ds(start, size)
        part = jnp.dot(mine[0 : 3 * tokens, :], head[:, span], preferred_element_type=f32) + jnp.dot(
            theirs[0 : 3 * tokens, :], other[:, span], preferred_element_type=f32
        )
        own[:, span] = part[0:tokens, :]
        p1[:, span] = part[tokens : 2 * tokens, :]
        p3[:, span] = part[2 * tokens :, :]

    over_columns(cols, tile)


def relay_kernel(p1, p3, low, high, q1, q3):
    tokens = p1.shape[0]
    half, step = tokens // 2, 32

    @pl.loop(0, half // step)
    def _(i):
        near = pl.ds(pl.multiple_of(i * step, step), step)
        far = pl.ds(pl.multiple_of(half + i * step, step), step)
        pack(p1[near, :] + unpack(low, near), q1, near)
        pack(p1[far, :], q1, far)
        pack(p3[near, :], q3, near)
        pack(p3[far, :] + unpack(high, near), q3, far)


def total_kernel(own, q1, q3, logits, sent, stats):
    tokens = own.shape[0]
    step = 16
    lane = lax.broadcasted_iota(jnp.int32, (step, 128), 1)

    @pl.loop(0, tokens // step)
    def _(i):
        at = pl.ds(pl.multiple_of(i * step, step), step)
        value = own[at, :]
        value = value + unpack(q1, at) + unpack(q3, at)
        logits[at, :] = value
        high = jnp.max(value, axis=1, keepdims=True)
        shifted = jnp.exp(value - high)
        total = jnp.sum(shifted, axis=1, keepdims=True)
        moment = jnp.sum(shifted * value, axis=1, keepdims=True)
        stats[at, :] = jnp.where(lane == 0, high, jnp.where(lane == 1, total, moment))

    rows = jnp.transpose(stats[...])[0:8, :]
    for i in range(sent.shape[0]):
        sent[i] = rows


def merge_kernel(parts, valid, advantage, sent):
    high = parts[0, 0:1, :]
    for i in range(1, parts.shape[0]):
        high = jnp.maximum(high, parts[i, 0:1, :])
    sums = jnp.zeros((8, 128), f32)
    for i in range(parts.shape[0]):
        sums = sums + jnp.exp(parts[i, 0:1, :] - high) * parts[i]
    row = lax.broadcasted_iota(jnp.int32, (8, 128), 0)
    out = jnp.where(row == 0, high, sums)
    out = jnp.where(row == 3, valid[...].astype(f32), jnp.where(row == 4, advantage[...], out))
    for i in range(sent.shape[0]):
        sent[i] = out


def plan_kernel(start_high, cap_owner, parts, coef_out, normal_out, packed_out, slot_out, flag, rows):
    owners = 8
    ny = parts.shape[0] // owners
    for o in range(owners):
        high = parts[o * ny, 0:1, :]
        for y in range(1, ny):
            high = jnp.maximum(high, parts[o * ny + y, 0:1, :])
        sums = jnp.zeros((8, 128), f32)
        for y in range(ny):
            sums = sums + jnp.exp(parts[o * ny + y, 0:1, :] - high) * parts[o * ny + y]
        row = lax.broadcasted_iota(jnp.int32, (8, 128), 0)
        normal = high + jnp.log(sums[1:2, :])
        entropy = normal - sums[2:3, :] / sums[1:2, :]
        rows[o] = jnp.where(row == 0, normal, jnp.where(row == 1, entropy, parts[o * ny]))
    normal, entropy, valid, advantage = (
        jnp.concatenate([rows[o, k : k + 1, :] for o in range(owners)], axis=0) for k in (0, 1, 3, 4)
    )
    counted = jnp.sum(jnp.sum(valid, axis=1, keepdims=True), axis=0, keepdims=True)
    threshold = bisect(jnp.where(valid > 0.0, entropy, -jnp.inf), counted, start_high)
    gate = valid * jnp.clip((entropy - threshold) / ramp_width + 0.5, 0.0, 1.0)
    coef = -(gate * advantage)
    active = coef != 0.0
    activef = active.astype(f32)
    i = lax.broadcasted_iota(jnp.int32, (128, 128), 0)
    j = lax.broadcasted_iota(jnp.int32, (128, 128), 1)
    ahead = (i < j).astype(f32)
    group = 128 // (32 // owners)
    same = (i // group == j // group).astype(f32)
    rank_owner = jnp.dot(activef, ahead, preferred_element_type=f32)
    rank_group = jnp.dot(activef, ahead * same, preferred_element_type=f32)
    start = (lax.broadcasted_iota(jnp.int32, (8, 128), 1) // group * CAP).astype(f32)
    coef_out[...] = coef
    normal_out[...] = normal
    packed_out[...] = jnp.where(active, rank_owner, -1.0)
    slot_out[...] = jnp.where(active, rank_group + start, -1.0)
    over = jnp.where(active & ((rank_owner >= cap_owner) | (rank_group >= CAP)), 1.0, 0.0)
    flag[0, 0] = jnp.max(over).astype(jnp.int32)


def as_columns(rows):
    row = lax.broadcasted_iota(jnp.int32, (8, 128), 0)
    out = jnp.zeros((8, 128), f32)
    for k, value in enumerate(rows):
        out = jnp.where(row == k, value, out)
    return jnp.transpose(out)


def one_hot(count, slots):
    row = lax.broadcasted_iota(jnp.int32, (count, 128), 0).astype(f32)
    return (row == slots).astype(f32).astype(bf16)


def slopes_kernel(at, logits, coef_all, normal_all, packed_all, ids, out):
    me = pl.ds(at[2], 1)
    count = out.shape[0]
    columns = as_columns([coef_all[me, :], normal_all[me, :], ids[...].astype(f32)])
    coef, normal, token = columns[:, 0:1], columns[:, 1:2], columns[:, 2:3].astype(jnp.int32) - at[3]
    choose = one_hot(count, packed_all[me, :])
    lane = lax.broadcasted_iota(jnp.int32, (128, 128), 1)
    for k in range(logits.shape[1] // 128):
        span = slice(k * 128, (k + 1) * 128)
        hit = (lane + k * 128 == token).astype(f32)
        slopes = (coef * (hit - jnp.exp(logits[:, span] - normal))).astype(bf16)
        out[:, span] = jnp.dot(choose, slopes, preferred_element_type=f32).astype(bf16)


def product_kernel(nx, at, mine, theirs, turned, packed_all, slot_all, out, held):
    half = mine.shape[0]
    count = half // nx
    for k, rows in enumerate((mine, theirs)):
        held[k * half : (k + 1) * half, :] = lax.dot_general(
            rows[...], turned[...], (((1,), (0,)), ((), ())), preferred_element_type=f32
        ).astype(bf16)
    size = out.shape[0] // (2 * nx)
    for owner in range(2 * nx):
        to, core = owner // 2, owner % 2
        source = lax.rem(at[0] - to + nx, nx) * count + lax.rem(at[1] + core, 2) * half
        block = held[pl.ds(pl.multiple_of(source, 16), count), :]
        spread = lax.dot_general(
            one_hot(size, slot_all[owner : owner + 1, :]),
            one_hot(count, packed_all[owner : owner + 1, :]),
            (((1,), (1,)), ((), ())),
            preferred_element_type=f32,
        ).astype(bf16)
        out[owner * size : (owner + 1) * size, :] = jnp.dot(
            spread, block, preferred_element_type=f32
        ).astype(bf16)


def outer_kernel(nx, at, packed_all, hid_mine, hid_theirs, mine, theirs, out, held):
    half = mine.shape[0]
    count = half // nx
    for k, hidden in enumerate((hid_mine, hid_theirs)):
        for s in range(nx):
            owner = lax.rem(at[0] - s + nx, nx) * 2 + lax.rem(at[1] + k, 2)
            choose = one_hot(count, packed_all[pl.ds(owner, 1), :])
            to = k * half + s * count
            held[to : to + count, :] = jnp.dot(
                choose, hidden[ORDER[s] * 128 : (ORDER[s] + 1) * 128, :], preferred_element_type=f32
            ).astype(bf16)
    total = jnp.zeros(out.shape, f32)
    for k, rows in enumerate((mine, theirs)):
        total = total + lax.dot_general(
            held[k * half : (k + 1) * half, :],
            rows[...],
            (((0,), (0,)), ((), ())),
            preferred_element_type=f32,
        )
    out[...] = total


def sum_kernel(at, parts, slot_all, out, ranks):
    n_voc = parts.shape[0] // CAP
    total = parts[0:CAP, :].astype(f32)
    for i in range(1, n_voc):
        total = total + parts[i * CAP : (i + 1) * CAP, :].astype(f32)
    group = out.shape[0]
    per_owner = 128 // group
    owner, place = at[4] // per_owner, lax.rem(at[4], per_owner)
    ranks[...] = as_columns([slot_all[pl.ds(owner, 1), :]])
    rank = ranks[pl.ds(pl.multiple_of(place * group, group), group), :][:, 0:1]
    rank = rank - (place * CAP).astype(f32)
    rows = jnp.zeros(out.shape, f32)
    for r in range(CAP):
        rows = rows + jnp.where(rank == float(r), total[r : r + 1, :], 0.0)
    out[...] = rows


def shards(hidden_states, head, token_ids, valid, advantage):
    tokens, width = hidden_states.shape
    rows, voc_cols = head.shape
    nx, n_voc, n_dp = lax.axis_size("x"), lax.axis_size(VOC), lax.axis_size(DP)
    x, c, block = lax.axis_index("x"), lax.axis_index("c"), lax.axis_index(VOC)
    at = jnp.stack([x, c, x * 2 + c, block * voc_cols, block]).astype(jnp.int32)
    chip_rows = width // nx

    head_other = lax.ppermute(head, "c", SWAP)

    block_shape = struct((tokens, chip_rows), bf16)
    b0, *leave = call(split_kernel, [block_shape] * 4, [at, hidden_states], smem=1)
    came = {s: lax.ppermute(leave[s - 1], "x", ring(nx, s)) for s in (2, 1, 3)}
    kept, turned = call(
        turn_kernel, [struct((rows, voc_cols), bf16), struct((voc_cols, rows), bf16)], [head]
    )
    half = struct((tokens // 2, voc_cols + 128), jnp.int16)
    low, high, tick = call(
        far_kernel,
        [half, half, struct((8, 128), f32)],
        [at, came[2], kept, head_other],
        [pltpu.VMEM((tokens, voc_cols), f32)],
        smem=1,
        cost_estimate=estimate(tokens, chip_rows, voc_cols),
    )
    low, high = lax.ppermute(low, "x", ring(nx, -1)), lax.ppermute(high, "x", ring(nx, 1))
    partial = struct((tokens, voc_cols), f32)
    own, p1, p3, hid_mine, hid_send = call(
        near_kernel,
        [partial] * 3 + [struct((nx * tokens, rows), bf16)] * 2,
        [at, tick, b0, came[1], came[2], came[3], kept, head_other],
        vmem=24,
        smem=1,
        cost_estimate=estimate(3 * tokens, chip_rows, voc_cols),
    )
    packed = struct((tokens, voc_cols + 128), jnp.int16)
    q1, q3 = call(relay_kernel, [packed] * 2, [p1, p3, low, high])
    q1, q3 = lax.ppermute(q1, "x", ring(nx, -1)), lax.ppermute(q3, "x", ring(nx, 1))
    hid_theirs = lax.ppermute(hid_send, "c", SWAP)
    logits, stats = call(
        total_kernel,
        [partial, struct((lax.axis_size("z"), 8, 128), f32)],
        [own, q1, q3],
        [pltpu.VMEM((tokens, 128), f32)],
    )

    stats = lax.all_to_all(stats, "z", 0, 0, tiled=True)
    everyone = DP + ("y",)
    stats = call(
        merge_kernel,
        struct((lax.axis_size(everyone), 8, 128), f32),
        [stats, valid.reshape(1, tokens), advantage.reshape(1, tokens)],
    )
    stats = lax.all_to_all(stats, everyone, 0, 0, tiled=True)
    start_high = float(np.float32(np.log(np.float32(voc_cols * n_voc))) + np.float32(1.0))
    table = struct((n_dp, tokens), f32)
    coef_all, normal_all, packed_all, slot_all, flag = call(
        functools.partial(plan_kernel, start_high, CAP_OWNER),
        [table] * 4 + [struct((1, 1), jnp.int32)],
        [stats],
        [pltpu.VMEM((n_dp, 8, 128), f32)],
        out_specs=[pl.BlockSpec(memory_space=pltpu.VMEM)] * 4 + [pl.BlockSpec(memory_space=pltpu.SMEM)],
    )

    def sparse(_):
        piece = call(
            slopes_kernel,
            struct((CAP_OWNER, voc_cols), bf16),
            [at, logits, coef_all, normal_all, packed_all, token_ids.reshape(1, tokens)],
            smem=1,
        )
        pieces = {s: lax.ppermute(piece, "x", ring(nx, s)) for s in (2, 1, 3)}
        mine = jnp.concatenate([piece, pieces[1], pieces[2], pieces[3]], axis=0)
        theirs = lax.ppermute(mine, "c", SWAP)
        product = call(
            functools.partial(product_kernel, nx),
            struct((n_voc * CAP, rows), bf16),
            [at, mine, theirs, turned, packed_all, slot_all],
            [pltpu.VMEM((2 * nx * CAP_OWNER, rows), bf16)],
            smem=1,
        )
        parts = lax.all_to_all(product, VOC, 0, 0, tiled=True)
        tile = 128
        head_grad = pl.pallas_call(
            functools.partial(outer_kernel, nx),
            grid=(rows // tile,),
            in_specs=[
                pl.BlockSpec(memory_space=pltpu.SMEM),
                pl.BlockSpec((n_dp, tokens), lambda i: (0, 0)),
                pl.BlockSpec((nx * tokens, tile), lambda i: (0, i)),
                pl.BlockSpec((nx * tokens, tile), lambda i: (0, i)),
                pl.BlockSpec((nx * CAP_OWNER, voc_cols), lambda i: (0, 0)),
                pl.BlockSpec((nx * CAP_OWNER, voc_cols), lambda i: (0, 0)),
            ],
            out_specs=pl.BlockSpec((tile, voc_cols), lambda i: (i, 0)),
            out_shape=struct((rows, voc_cols), f32),
            scratch_shapes=[pltpu.VMEM((2 * nx * CAP_OWNER, tile), bf16)],
            compiler_params=pltpu.CompilerParams(vmem_limit_bytes=24 << 20),
            cost_estimate=pl.CostEstimate(
                flops=4 * nx * CAP_OWNER * rows * voc_cols,
                bytes_accessed=4 * rows * voc_cols,
                transcendentals=0,
            ),
        )(at, packed_all, hid_mine, hid_theirs, mine, theirs)
        hidden_grad = call(
            sum_kernel,
            struct((tokens * n_dp // n_voc, rows), f32),
            [at, parts, slot_all],
            [pltpu.VMEM((tokens, 8), f32)],
            smem=1,
        )
        return hidden_grad, head_grad

    def whole(_):
        return dense(hidden_states, head, token_ids, valid, advantage)

    return lax.cond(flag[0, 0] != 0, whole, sparse, 0)


def solution(mesh):
    chips = Mesh(mesh.devices.reshape(4, 2, 4, 8), DP + VOC)
    placed = (P(DP, None), P(DP, VOC), P(DP), P(DP), P(DP))
    return jax.shard_map(
        shards,
        mesh=chips,
        in_specs=placed,
        out_specs=(P(VOC, DP), P(DP, VOC)),
        check_vma=False,
    )
```

```python
import functools

import jax
import jax.numpy as jnp
import numpy as np
from jax import lax
from jax.experimental import pallas as pl
from jax.experimental.pallas import tpu as pltpu
from jax.sharding import Mesh, PartitionSpec as P

ROUNDS = 24
LEVELS = 6
CAP = 16
CAP_PAIR = 64
ORDER = (0, 1, 3, 2)
NX = 4

ramp_width = 0.5
DP = ("x", "c")
VOC = ("y", "z")
f32 = jnp.float32
bf16 = jnp.bfloat16


def ring(n, shift):
    return [(i, (i + shift) % n) for i in range(n)]


SWAP = [(0, 1), (1, 0)]


def dense(hidden_states, head, token_ids, valid, advantage):
    voc_cols = head.shape[1]
    columns = lax.all_to_all(hidden_states, DP, split_axis=1, concat_axis=0, tiled=True)
    logits = lax.psum_scatter(
        jnp.dot(columns, head, preferred_element_type=f32), DP, scatter_dimension=0, tiled=True
    )
    offset = lax.axis_index(VOC) * voc_cols
    hit = jnp.arange(voc_cols, dtype=jnp.int32)[None, :] + offset == token_ids[:, None]
    highest = lax.pmax(jnp.max(logits, axis=1), VOC)
    shifted = jnp.exp(logits - highest[:, None])
    total, moment = lax.psum((jnp.sum(shifted, axis=1), jnp.sum(shifted * logits, axis=1)), VOC)
    normal = highest + jnp.log(total)
    entropy = normal - moment / total
    validf = valid.astype(f32)
    start_high = jnp.log(f32(voc_cols * lax.axis_size(VOC))) + 1.0
    counted = lax.psum(jnp.sum(validf), DP)
    quota = jnp.floor((counted + 0.5) * 0.2)

    def round_step(step, bounds):
        low, high = bounds
        middle = (low + high) * 0.5
        above = lax.psum(jnp.sum(jnp.where(entropy > middle, validf, 0.0)), DP)
        more = above > quota
        return (jnp.where(more, middle, low), jnp.where(more, high, middle))

    _, threshold = lax.fori_loop(0, ROUNDS, round_step, (f32(0.0), start_high))
    gate = validf * jnp.clip((entropy - threshold) / ramp_width + 0.5, 0.0, 1.0)
    coef = -(gate * advantage)
    probs = jnp.exp(logits - normal[:, None])
    slopes = (coef[:, None] * (hit.astype(f32) - probs)).astype(bf16)
    piece = lax.all_gather(slopes, DP, axis=0, tiled=True)
    head_grad = lax.dot_general(columns, piece, (((0,), (0,)), ((), ())), preferred_element_type=f32)
    product = lax.dot_general(piece, head, (((1,), (1,)), ((), ())), preferred_element_type=f32)
    return lax.psum_scatter(product, VOC, scatter_dimension=0, tiled=True), head_grad


def bisect(entropy, counted, start_high):
    columns = jnp.transpose(entropy)
    quota = jnp.floor((counted + 0.5) * 0.2)
    lane = lax.broadcasted_iota(jnp.int32, (1, 128), 1)
    leaves = 1 << LEVELS
    low = jnp.zeros((1, 128), f32)
    high = jnp.full((1, 128), start_high, f32)
    for _ in range(ROUNDS // LEVELS):
        for level in range(LEVELS):
            middle = (low + high) * 0.5
            bit = ((lane >> (LEVELS - 1 - level)) & 1) == 1
            low, high = jnp.where(bit, middle, low), jnp.where(bit, high, middle)
        above = jnp.zeros((128, 128), f32)
        for i in range(8):
            above = above + jnp.where(columns[:, i : i + 1] > low, 1.0, 0.0)
        above = jnp.sum(above, axis=0, keepdims=True)
        more = jnp.where(((above > quota) | (lane == 0)) & (lane < leaves), 1.0, 0.0)
        here = lane == jnp.sum(more, axis=1, keepdims=True).astype(jnp.int32) - 1
        low, high = (
            jnp.broadcast_to(jnp.sum(jnp.where(here, v, 0.0), axis=1, keepdims=True), (1, 128))
            for v in (low, high)
        )
    return high[:, :1]


def call(kernel, out, args, scratch=(), vmem=16, smem=0, **kw):
    specs = [pl.BlockSpec(memory_space=pltpu.SMEM)] * smem
    specs += [pl.BlockSpec(memory_space=pltpu.VMEM)] * (len(args) - smem)
    return pl.pallas_call(
        kernel,
        in_specs=specs,
        out_shape=out,
        scratch_shapes=list(scratch),
        compiler_params=pltpu.CompilerParams(vmem_limit_bytes=vmem << 20),
        **kw,
    )(*args)


def struct(shape, dtype):
    return jax.ShapeDtypeStruct(shape, dtype)


def estimate(m, k, n):
    return pl.CostEstimate(flops=2 * m * k * n, bytes_accessed=2 * k * n, transcendentals=0)


LN2_64 = float(np.log(2.0) / 64.0)


def split_kernel(at, hidden, b0, b1, b2, b3):
    chip_rows = b0.shape[1]
    nx = hidden.shape[1] // chip_rows
    for s, out in enumerate((b0, b1, b2, b3)):
        to = lax.rem(at[0] + s, nx) * chip_rows
        out[...] = hidden[:, pl.ds(pl.multiple_of(to, 128), chip_rows)]


def turn_kernel(head, kept, turned):
    kept[...] = head[...]
    for k in range(head.shape[1] // 128):
        span = slice(k * 128, (k + 1) * 128)
        turned[span, :] = jnp.transpose(head[:, span])


def pack(block, out, to):
    step, cols = block.shape
    top = jnp.maximum(jnp.max(jnp.abs(block), axis=1, keepdims=True), 1e-30)
    power = jnp.ceil(jnp.log(top) * (1.0 / LN2_64)) + 1.0
    fixed = jnp.round(block * (jnp.exp(power * -LN2_64) * 32766.0))
    out[to, 0:cols] = fixed.astype(jnp.int32).astype(jnp.int16)
    wide_power = jnp.broadcast_to(power.astype(jnp.int32), (step, 128))
    out[to, cols : cols + 128] = wide_power.astype(jnp.int16)


def unpack(ref, at):
    cols = ref.shape[1] - 128
    power = ref[at, cols : cols + 128].astype(jnp.int32).astype(f32)[:, :1]
    return ref[at, 0:cols].astype(jnp.int32).astype(f32) * (jnp.exp(power * LN2_64) * (1.0 / 32766.0))


def over_columns(cols, tile):
    wide = cols // 256

    @pl.loop(0, wide)
    def _(i):
        tile(pl.multiple_of(i * 256, 256), 256)

    if cols > wide * 256:
        tile(wide * 256, cols - wide * 256)


def halves(at, rows):
    return (
        pl.ds(pl.multiple_of(at[1] * rows, 128), rows),
        pl.ds(pl.multiple_of((1 - at[1]) * rows, 128), rows),
    )


def far_kernel(at, block, head, other, low, high, tick, part):
    tokens = block.shape[0]
    rows, cols = head.shape
    here, there = halves(at, rows)

    def tile(start, size):
        span = pl.ds(start, size)
        part[:, span] = jnp.dot(block[:, here], head[:, span], preferred_element_type=f32) + jnp.dot(
            block[:, there], other[:, span], preferred_element_type=f32
        )

    over_columns(cols, tile)
    tick[...] = jnp.zeros(tick.shape, f32)
    step = 32
    for k, out in enumerate((low, high)):

        @pl.loop(0, tokens // 2 // step)
        def _(i, k=k, out=out):
            source = pl.multiple_of(k * (tokens // 2) + i * step, step)
            pack(part[pl.ds(source, step), :], out, pl.ds(pl.multiple_of(i * step, step), step))


def near_kernel(at, tick, b0, b1, b2, b3, head, other, own, p1, p3, mine, theirs):
    tokens = b0.shape[0]
    rows, cols = head.shape
    here, there = halves(at, rows)
    for k, block in enumerate((b0, b1, b3, b2)):
        mine[k * tokens : (k + 1) * tokens, :] = block[:, here]
        theirs[k * tokens : (k + 1) * tokens, :] = block[:, there]

    def tile(start, size):
        span = pl.ds(start, size)
        part = jnp.dot(mine[0 : 3 * tokens, :], head[:, span], preferred_element_type=f32) + jnp.dot(
            theirs[0 : 3 * tokens, :], other[:, span], preferred_element_type=f32
        )
        own[:, span] = part[0:tokens, :]
        p1[:, span] = part[tokens : 2 * tokens, :]
        p3[:, span] = part[2 * tokens :, :]

    over_columns(cols, tile)


def relay_kernel(p1, p3, low, high, q1, q3):
    tokens = p1.shape[0]
    half, step = tokens // 2, 32

    @pl.loop(0, half // step)
    def _(i):
        near = pl.ds(pl.multiple_of(i * step, step), step)
        far = pl.ds(pl.multiple_of(half + i * step, step), step)
        pack(p1[near, :] + unpack(low, near), q1, near)
        pack(p1[far, :], q1, far)
        pack(p3[near, :], q3, near)
        pack(p3[far, :] + unpack(high, near), q3, far)


def total_kernel(own, q1, q3, packed, sent, stats):
    tokens = own.shape[0]
    step = 16
    lane = lax.broadcasted_iota(jnp.int32, (step, 128), 1)

    @pl.loop(0, tokens // step)
    def _(i):
        at = pl.ds(pl.multiple_of(i * step, step), step)
        value = own[at, :]
        value = value + unpack(q1, at) + unpack(q3, at)
        pack(value, packed, at)
        high = jnp.max(value, axis=1, keepdims=True)
        shifted = jnp.exp(value - high)
        total = jnp.sum(shifted, axis=1, keepdims=True)
        moment = jnp.sum(shifted * value, axis=1, keepdims=True)
        stats[at, :] = jnp.where(lane == 0, high, jnp.where(lane == 1, total, moment))

    rows = jnp.transpose(stats[...])[0:8, :]
    for i in range(sent.shape[0]):
        sent[i] = rows


def merge_kernel(parts, valid, advantage, ids, sent):
    high = parts[0, 0:1, :]
    for i in range(1, parts.shape[0]):
        high = jnp.maximum(high, parts[i, 0:1, :])
    sums = jnp.zeros((8, 128), f32)
    for i in range(parts.shape[0]):
        sums = sums + jnp.exp(parts[i, 0:1, :] - high) * parts[i]
    row = lax.broadcasted_iota(jnp.int32, (8, 128), 0)
    out = jnp.where(row == 0, high, sums)
    out = jnp.where(row == 3, valid[...].astype(f32), jnp.where(row == 4, advantage[...], out))
    out = jnp.where(row == 5, ids[...].astype(f32), out)
    for i in range(sent.shape[0]):
        sent[i] = out


def plan_kernel(start_high, parts, coef_out, normal_out, id_out, packed_out, slot_out, flag, rows):
    owners = 8
    ny = parts.shape[0] // owners
    for o in range(owners):
        high = parts[o * ny, 0:1, :]
        for y in range(1, ny):
            high = jnp.maximum(high, parts[o * ny + y, 0:1, :])
        sums = jnp.zeros((8, 128), f32)
        for y in range(ny):
            sums = sums + jnp.exp(parts[o * ny + y, 0:1, :] - high) * parts[o * ny + y]
        row = lax.broadcasted_iota(jnp.int32, (8, 128), 0)
        normal = high + jnp.log(sums[1:2, :])
        entropy = normal - sums[2:3, :] / sums[1:2, :]
        rows[o] = jnp.where(row == 0, normal, jnp.where(row == 1, entropy, parts[o * ny]))
    normal, entropy, valid, advantage, ids = (
        jnp.concatenate([rows[o, k : k + 1, :] for o in range(owners)], axis=0) for k in (0, 1, 3, 4, 5)
    )
    counted = jnp.sum(jnp.sum(valid, axis=1, keepdims=True), axis=0, keepdims=True)
    threshold = bisect(jnp.where(valid > 0.0, entropy, -jnp.inf), counted, start_high)
    gate = valid * jnp.clip((entropy - threshold) / ramp_width + 0.5, 0.0, 1.0)
    coef = -(gate * advantage)
    active = coef != 0.0
    activef = active.astype(f32)
    i = lax.broadcasted_iota(jnp.int32, (128, 128), 0)
    j = lax.broadcasted_iota(jnp.int32, (128, 128), 1)
    ahead = (i < j).astype(f32)
    group = 128 // (32 // owners)
    same = (i // group == j // group).astype(f32)
    rank_pair = jnp.dot(activef, ahead, preferred_element_type=f32)
    i = lax.broadcasted_iota(jnp.int32, (8, 8), 0)
    j = lax.broadcasted_iota(jnp.int32, (8, 8), 1)
    first = ((j == i - 1) & (i % 2 == 1)).astype(f32)
    counts = jnp.broadcast_to(jnp.sum(activef, axis=1, keepdims=True), (8, 128))
    rank_pair = rank_pair + jnp.dot(first, counts, preferred_element_type=f32)
    rank_group = jnp.dot(activef, ahead * same, preferred_element_type=f32)
    start = (lax.broadcasted_iota(jnp.int32, (8, 128), 1) // group * CAP).astype(f32)
    coef_out[...] = coef
    normal_out[...] = normal
    id_out[...] = ids
    packed_out[...] = jnp.where(active, rank_pair, -1.0)
    slot_out[...] = jnp.where(active, rank_group + start, -1.0)
    over = jnp.where(active & ((rank_pair >= CAP_PAIR) | (rank_group >= CAP)), 1.0, 0.0)
    flag[0, 0] = jnp.max(over).astype(jnp.int32)


def as_columns(rows):
    row = lax.broadcasted_iota(jnp.int32, (8, 128), 0)
    out = jnp.zeros((8, 128), f32)
    for k, value in enumerate(rows):
        out = jnp.where(row == k, value, out)
    return jnp.transpose(out)


def one_hot(count, slots):
    row = lax.broadcasted_iota(jnp.int32, (count, 128), 0).astype(f32)
    return (row == slots).astype(f32).astype(bf16)


def owner_of(at, s, k):
    return lax.rem(at[0] - s + NX, NX) * 2 + lax.rem(at[1] + k, 2)


def slopes_kernel(at, coef_all, normal_all, id_all, packed_all, m0, m1, m2, m3, out):
    cols = out.shape[1]
    for s, ref in enumerate((m0, m1, m2, m3)):
        me = pl.ds(owner_of(at, s, 0), 1)
        column = as_columns([coef_all[me, :], normal_all[me, :], id_all[me, :]])
        power = ref[:, cols : cols + 128].astype(jnp.int32).astype(f32)[:, :1]
        scale = jnp.exp(power * LN2_64) * (1.0 / 32766.0)
        choose = one_hot(CAP_PAIR, packed_all[me, :])

        def tile(start, size, s=s, ref=ref, column=column, scale=scale, choose=choose):
            span = pl.ds(start, size)
            lane = lax.broadcasted_iota(jnp.int32, (128, size), 1)
            token = column[:, 2:3].astype(jnp.int32) - (at[3] + start)
            logits = ref[:, span].astype(jnp.int32).astype(f32) * scale
            hit = jnp.where(lane == token, 1.0, 0.0)
            slopes = (column[:, 0:1] * (hit - jnp.exp(logits - column[:, 1:2]))).astype(bf16)
            out[s * CAP_PAIR : (s + 1) * CAP_PAIR, span] = jnp.dot(
                choose, slopes, preferred_element_type=f32
            ).astype(bf16)

        over_columns(cols, tile)


def product_kernel(at, mine, theirs, turned, slopes, o0, o1, o2, o3, held):
    slopes[...] = (mine[...].astype(f32) + theirs[...].astype(f32)).astype(bf16)
    held[...] = jnp.dot(slopes[...], turned[...], preferred_element_type=f32).astype(bf16)
    for k, out in enumerate((o0, o1, o2, o3)):
        source = lax.rem(at[0] - at[5] - k + 2 * NX, NX) * CAP_PAIR
        out[...] = held[pl.ds(pl.multiple_of(source, CAP_PAIR), CAP_PAIR), :]


def outer_kernel(at, packed_all, hid_mine, hid_theirs, slopes, out, held):
    for s in range(NX):
        rows = jnp.zeros((CAP_PAIR, out.shape[0]), f32)
        for k, hidden in enumerate((hid_mine, hid_theirs)):
            choose = one_hot(CAP_PAIR, packed_all[pl.ds(owner_of(at, s, k), 1), :])
            rows = rows + jnp.dot(
                choose, hidden[ORDER[s] * 128 : (ORDER[s] + 1) * 128, :], preferred_element_type=f32
            )
        held[s * CAP_PAIR : (s + 1) * CAP_PAIR, :] = rows.astype(bf16)
    out[...] = lax.dot_general(
        held[...], slopes[...], (((0,), (0,)), ((), ())), preferred_element_type=f32
    )


def spread_kernel(at, r0, r1, r2, r3, packed_all, slot_all, out):
    size = out.shape[0]
    spread = jnp.zeros((size, CAP_PAIR), f32)
    for k in range(2):
        me = pl.ds(at[5] * 2 + k, 1)
        slot = slot_all[me, :]
        slot = jnp.where(slot >= 0.0, slot + float(k * size // 2), -1.0)
        spread = spread + lax.dot_general(
            one_hot(size, slot),
            one_hot(CAP_PAIR, packed_all[me, :]),
            (((1,), (1,)), ((), ())),
            preferred_element_type=f32,
        )
    spread = spread.astype(bf16)
    total = jnp.zeros(out.shape, f32)
    for r in (r0, r1, r2, r3):
        total = total + jnp.dot(spread, r[...], preferred_element_type=f32)
    out[...] = total


def sum_kernel(at, parts, slot_all, out, ranks):
    total = parts[0:CAP, :]
    for i in range(1, parts.shape[0] // CAP):
        total = total + parts[i * CAP : (i + 1) * CAP, :]
    group = out.shape[0]
    per_owner = 128 // group
    owner, place = at[4] // per_owner, lax.rem(at[4], per_owner)
    ranks[...] = as_columns([slot_all[pl.ds(owner, 1), :]])
    rank = ranks[pl.ds(pl.multiple_of(place * group, group), group), :][:, 0:1]
    rank = rank - (place * CAP).astype(f32)
    rows = jnp.zeros(out.shape, f32)
    for r in range(CAP):
        rows = rows + jnp.where(rank == float(r), total[r : r + 1, :], 0.0)
    out[...] = rows


def shards(hidden_states, head, token_ids, valid, advantage):
    tokens, width = hidden_states.shape
    rows, voc_cols = head.shape
    nx, n_voc, n_dp = lax.axis_size("x"), lax.axis_size(VOC), lax.axis_size(DP)
    x, c, block = lax.axis_index("x"), lax.axis_index("c"), lax.axis_index(VOC)
    at = jnp.stack([x, c, x * 2 + c, block * voc_cols, block, lax.axis_index("y")]).astype(jnp.int32)
    chip_rows = width // nx

    head_other = lax.ppermute(head, "c", SWAP)

    block_shape = struct((tokens, chip_rows), bf16)
    b0, *leave = call(split_kernel, [block_shape] * 4, [at, hidden_states], smem=1)
    came = {s: lax.ppermute(leave[s - 1], "x", ring(nx, s)) for s in (2, 1, 3)}
    kept, turned = call(
        turn_kernel, [struct((rows, voc_cols), bf16), struct((voc_cols, rows), bf16)], [head]
    )
    half = struct((tokens // 2, voc_cols + 128), jnp.int16)
    low, high, tick = call(
        far_kernel,
        [half, half, struct((8, 128), f32)],
        [at, came[2], kept, head_other],
        [pltpu.VMEM((tokens, voc_cols), f32)],
        smem=1,
        cost_estimate=estimate(tokens, chip_rows, voc_cols),
    )
    low, high = lax.ppermute(low, "x", ring(nx, -1)), lax.ppermute(high, "x", ring(nx, 1))
    partial = struct((tokens, voc_cols), f32)
    own, p1, p3, hid_mine, hid_send = call(
        near_kernel,
        [partial] * 3 + [struct((nx * tokens, rows), bf16)] * 2,
        [at, tick, b0, came[1], came[2], came[3], kept, head_other],
        vmem=24,
        smem=1,
        cost_estimate=estimate(3 * tokens, chip_rows, voc_cols),
    )
    packed = struct((tokens, voc_cols + 128), jnp.int16)
    q1, q3 = call(relay_kernel, [packed] * 2, [p1, p3, low, high])
    q1, q3 = lax.ppermute(q1, "x", ring(nx, -1)), lax.ppermute(q3, "x", ring(nx, 1))
    hid_theirs = lax.ppermute(hid_send, "c", SWAP)
    logits, stats = call(
        total_kernel,
        [packed, struct((lax.axis_size("z"), 8, 128), f32)],
        [own, q1, q3],
        [pltpu.VMEM((tokens, 128), f32)],
    )
    mine = {s: lax.ppermute(logits, "x", ring(nx, s)) for s in (2, 1, 3)}
    mine[0] = logits

    stats = lax.all_to_all(stats, "z", 0, 0, tiled=True)
    everyone = DP + ("y",)
    stats = call(
        merge_kernel,
        struct((lax.axis_size(everyone), 8, 128), f32),
        [stats] + [v.reshape(1, tokens) for v in (valid, advantage, token_ids)],
    )
    stats = lax.all_to_all(stats, everyone, 0, 0, tiled=True)
    start_high = float(np.float32(np.log(np.float32(voc_cols * n_voc))) + np.float32(1.0))
    table = struct((n_dp, tokens), f32)
    coef_all, normal_all, id_all, packed_all, slot_all, flag = call(
        functools.partial(plan_kernel, start_high),
        [table] * 5 + [struct((1, 1), jnp.int32)],
        [stats],
        [pltpu.VMEM((n_dp, 8, 128), f32)],
        out_specs=[pl.BlockSpec(memory_space=pltpu.VMEM)] * 5 + [pl.BlockSpec(memory_space=pltpu.SMEM)],
    )

    def sparse(_):
        slopes = struct((nx * CAP_PAIR, voc_cols), bf16)
        kept_rows = call(
            slopes_kernel,
            slopes,
            [at, coef_all, normal_all, id_all, packed_all] + [mine[s] for s in range(nx)],
            smem=1,
        )
        slopes, *parts = call(
            product_kernel,
            [slopes] + [struct((CAP_PAIR, rows), bf16)] * nx,
            [at, kept_rows, lax.ppermute(kept_rows, "c", SWAP), turned],
            [pltpu.VMEM((nx * CAP_PAIR, rows), bf16)],
            smem=1,
        )
        parts = [parts[0]] + [lax.ppermute(parts[k], "y", ring(nx, k)) for k in range(1, nx)]
        tile = 128
        head_grad = pl.pallas_call(
            outer_kernel,
            grid=(rows // tile,),
            in_specs=[
                pl.BlockSpec(memory_space=pltpu.SMEM),
                pl.BlockSpec((n_dp, tokens), lambda i: (0, 0)),
                pl.BlockSpec((nx * tokens, tile), lambda i: (0, i)),
                pl.BlockSpec((nx * tokens, tile), lambda i: (0, i)),
                pl.BlockSpec((nx * CAP_PAIR, voc_cols), lambda i: (0, 0)),
            ],
            out_specs=pl.BlockSpec((tile, voc_cols), lambda i: (i, 0)),
            out_shape=struct((rows, voc_cols), f32),
            scratch_shapes=[pltpu.VMEM((nx * CAP_PAIR, tile), bf16)],
            compiler_params=pltpu.CompilerParams(vmem_limit_bytes=24 << 20),
            cost_estimate=estimate(rows, nx * CAP_PAIR, voc_cols),
        )(at, packed_all, hid_mine, hid_theirs, slopes)
        spread = call(
            spread_kernel,
            struct((n_voc * CAP // nx, rows), f32),
            [at, *parts, packed_all, slot_all],
            smem=1,
        )
        spread = lax.all_to_all(spread, "z", 0, 0, tiled=True)
        hidden_grad = call(
            sum_kernel,
            struct((tokens * n_dp // n_voc, rows), f32),
            [at, spread, slot_all],
            [pltpu.VMEM((tokens, 8), f32)],
            smem=1,
        )
        return hidden_grad, head_grad

    def whole(_):
        return dense(hidden_states, head, token_ids, valid, advantage)

    return lax.cond(flag[0, 0] != 0, whole, sparse, 0)


def solution(mesh):
    chips = Mesh(mesh.devices.reshape(4, 2, 4, 8), DP + VOC)
    placed = (P(DP, None), P(DP, VOC), P(DP), P(DP), P(DP))
    return jax.shard_map(
        shards,
        mesh=chips,
        in_specs=placed,
        out_specs=(P(VOC, DP), P(DP, VOC)),
        check_vma=False,
    )
```

```python
import functools

import jax
import jax.numpy as jnp
import numpy as np
from jax import lax
from jax.experimental import pallas as pl
from jax.experimental.pallas import tpu as pltpu
from jax.sharding import Mesh, PartitionSpec as P

ROUNDS = 24
LEVELS = 6
CAP = 16
CAP_SMALL = 32
ORDER = (2, 0, 3, 1)
NX = 4

ramp_width = 0.5
DP = ("x", "c")
VOC = ("y", "z")
f32 = jnp.float32
bf16 = jnp.bfloat16


def ring(n, shift):
    return [(i, (i + shift) % n) for i in range(n)]


SWAP = [(0, 1), (1, 0)]


def dense(hidden_states, head, token_ids, valid, advantage):
    voc_cols = head.shape[1]
    columns = lax.all_to_all(hidden_states, DP, split_axis=1, concat_axis=0, tiled=True)
    logits = lax.psum_scatter(
        jnp.dot(columns, head, preferred_element_type=f32), DP, scatter_dimension=0, tiled=True
    )
    offset = lax.axis_index(VOC) * voc_cols
    hit = jnp.arange(voc_cols, dtype=jnp.int32)[None, :] + offset == token_ids[:, None]
    highest = lax.pmax(jnp.max(logits, axis=1), VOC)
    shifted = jnp.exp(logits - highest[:, None])
    total, moment = lax.psum((jnp.sum(shifted, axis=1), jnp.sum(shifted * logits, axis=1)), VOC)
    normal = highest + jnp.log(total)
    entropy = normal - moment / total
    validf = valid.astype(f32)
    start_high = jnp.log(f32(voc_cols * lax.axis_size(VOC))) + 1.0
    counted = lax.psum(jnp.sum(validf), DP)
    quota = jnp.floor((counted + 0.5) * 0.2)

    def round_step(step, bounds):
        low, high = bounds
        middle = (low + high) * 0.5
        above = lax.psum(jnp.sum(jnp.where(entropy > middle, validf, 0.0)), DP)
        more = above > quota
        return (jnp.where(more, middle, low), jnp.where(more, high, middle))

    _, threshold = lax.fori_loop(0, ROUNDS, round_step, (f32(0.0), start_high))
    gate = validf * jnp.clip((entropy - threshold) / ramp_width + 0.5, 0.0, 1.0)
    coef = -(gate * advantage)
    probs = jnp.exp(logits - normal[:, None])
    slopes = (coef[:, None] * (hit.astype(f32) - probs)).astype(bf16)
    piece = lax.all_gather(slopes, DP, axis=0, tiled=True)
    head_grad = lax.dot_general(columns, piece, (((0,), (0,)), ((), ())), preferred_element_type=f32)
    product = lax.dot_general(piece, head, (((1,), (1,)), ((), ())), preferred_element_type=f32)
    return lax.psum_scatter(product, VOC, scatter_dimension=0, tiled=True), head_grad


def bisect(entropy, counted, start_high):
    columns = jnp.transpose(entropy)
    quota = jnp.floor((counted + 0.5) * 0.2)
    lane = lax.broadcasted_iota(jnp.int32, (1, 128), 1)
    leaves = 1 << LEVELS
    low = jnp.zeros((1, 128), f32)
    high = jnp.full((1, 128), start_high, f32)
    for _ in range(ROUNDS // LEVELS):
        for level in range(LEVELS):
            middle = (low + high) * 0.5
            bit = ((lane >> (LEVELS - 1 - level)) & 1) == 1
            low, high = jnp.where(bit, middle, low), jnp.where(bit, high, middle)
        above = jnp.zeros((128, 128), f32)
        for i in range(8):
            above = above + jnp.where(columns[:, i : i + 1] > low, 1.0, 0.0)
        above = jnp.sum(above, axis=0, keepdims=True)
        more = jnp.where(((above > quota) | (lane == 0)) & (lane < leaves), 1.0, 0.0)
        here = lane == jnp.sum(more, axis=1, keepdims=True).astype(jnp.int32) - 1
        low, high = (
            jnp.broadcast_to(jnp.sum(jnp.where(here, v, 0.0), axis=1, keepdims=True), (1, 128))
            for v in (low, high)
        )
    return high[:, :1]


def call(kernel, out, args, scratch=(), vmem=16, smem=0, **kw):
    specs = [pl.BlockSpec(memory_space=pltpu.SMEM)] * smem
    specs += [pl.BlockSpec(memory_space=pltpu.VMEM)] * (len(args) - smem)
    return pl.pallas_call(
        kernel,
        in_specs=specs,
        out_shape=out,
        scratch_shapes=list(scratch),
        compiler_params=pltpu.CompilerParams(vmem_limit_bytes=vmem << 20),
        **kw,
    )(*args)


def struct(shape, dtype):
    return jax.ShapeDtypeStruct(shape, dtype)


def estimate(m, k, n):
    return pl.CostEstimate(flops=2 * m * k * n, bytes_accessed=2 * k * n, transcendentals=0)


LN2_64 = float(np.log(2.0) / 64.0)


def split_kernel(at, hidden, b0, b1, b2, b3):
    chip_rows = b0.shape[1]
    nx = hidden.shape[1] // chip_rows
    for s, out in enumerate((b0, b1, b2, b3)):
        to = lax.rem(at[0] + s, nx) * chip_rows
        out[...] = hidden[:, pl.ds(pl.multiple_of(to, 128), chip_rows)]


def turn_kernel(tick, head, turned):
    for k in range(head.shape[1] // 128):
        span = slice(k * 128, (k + 1) * 128)
        turned[span, :] = jnp.transpose(head[:, span])


def pack(block, out, to):
    step, cols = block.shape
    top = jnp.maximum(jnp.max(jnp.abs(block), axis=1, keepdims=True), 1e-30)
    power = jnp.ceil(jnp.log(top) * (1.0 / LN2_64)) + 1.0
    fixed = jnp.round(block * (jnp.exp(power * -LN2_64) * 32766.0))
    out[to, 0:cols] = fixed.astype(jnp.int32).astype(jnp.int16)
    wide_power = jnp.broadcast_to(power.astype(jnp.int32), (step, 128))
    out[to, cols : cols + 128] = wide_power.astype(jnp.int16)


def unpack(ref, at):
    cols = ref.shape[1] - 128
    power = ref[at, cols : cols + 128].astype(jnp.int32).astype(f32)[:, :1]
    return ref[at, 0:cols].astype(jnp.int32).astype(f32) * (jnp.exp(power * LN2_64) * (1.0 / 32766.0))


def over_columns(cols, tile):
    for start in range(0, cols, 256):
        tile(slice(start, min(start + 256, cols)))


def halves(at, rows):
    return (
        pl.ds(pl.multiple_of(at[1] * rows, 128), rows),
        pl.ds(pl.multiple_of((1 - at[1]) * rows, 128), rows),
    )


def own_kernel(at, block, head, other, own, kept):
    kept[...] = head[...]
    here, there = halves(at, head.shape[0])

    def tile(span):
        own[:, span] = jnp.dot(block[:, here], head[:, span], preferred_element_type=f32) + jnp.dot(
            block[:, there], other[:, span], preferred_element_type=f32
        )

    over_columns(head.shape[1], tile)


def far_kernel(at, block, head, other, low, high, tick, part):
    tokens = block.shape[0]
    rows, cols = head.shape
    here, there = halves(at, rows)

    def tile(span):
        part[:, span] = jnp.dot(block[:, here], head[:, span], preferred_element_type=f32) + jnp.dot(
            block[:, there], other[:, span], preferred_element_type=f32
        )

    over_columns(cols, tile)
    tick[...] = jnp.zeros(tick.shape, f32)
    step = 32
    for k, out in enumerate((low, high)):

        @pl.loop(0, tokens // 2 // step)
        def _(i, k=k, out=out):
            source = pl.multiple_of(k * (tokens // 2) + i * step, step)
            pack(part[pl.ds(source, step), :], out, pl.ds(pl.multiple_of(i * step, step), step))


def near_kernel(at, tick, b0, b1, b2, b3, head, other, p1, p3, mine, theirs):
    tokens = b0.shape[0]
    rows, cols = head.shape
    here, there = halves(at, rows)
    for k, block in enumerate((b1, b3, b0, b2)):
        mine[k * tokens : (k + 1) * tokens, :] = block[:, here]
        theirs[k * tokens : (k + 1) * tokens, :] = block[:, there]

    def tile(span):
        part = jnp.dot(mine[0 : 2 * tokens, :], head[:, span], preferred_element_type=f32) + jnp.dot(
            theirs[0 : 2 * tokens, :], other[:, span], preferred_element_type=f32
        )
        p1[:, span] = part[0:tokens, :]
        p3[:, span] = part[tokens:, :]

    over_columns(cols, tile)


def relay_kernel(p1, p3, low, high, q1, q3, tick):
    tokens = p1.shape[0]
    half, step = tokens // 2, 32
    tick[...] = jnp.zeros(tick.shape, f32)

    @pl.loop(0, half // step)
    def _(i):
        near = pl.ds(pl.multiple_of(i * step, step), step)
        far = pl.ds(pl.multiple_of(half + i * step, step), step)
        pack(p1[near, :] + unpack(low, near), q1, near)
        pack(p1[far, :], q1, far)
        pack(p3[near, :], q3, near)
        pack(p3[far, :] + unpack(high, near), q3, far)


def total_kernel(own, q1, q3, logits, sent, stats):
    tokens = own.shape[0]
    step = 16
    lane = lax.broadcasted_iota(jnp.int32, (step, 128), 1)

    @pl.loop(0, tokens // step)
    def _(i):
        at = pl.ds(pl.multiple_of(i * step, step), step)
        value = own[at, :]
        value = value + unpack(q1, at) + unpack(q3, at)
        logits[at, :] = value
        high = jnp.max(value, axis=1, keepdims=True)
        shifted = jnp.exp(value - high)
        total = jnp.sum(shifted, axis=1, keepdims=True)
        moment = jnp.sum(shifted * value, axis=1, keepdims=True)
        stats[at, :] = jnp.where(lane == 0, high, jnp.where(lane == 1, total, moment))

    rows = jnp.transpose(stats[...])[0:8, :]
    for i in range(sent.shape[0]):
        sent[i] = rows


def merge_kernel(parts, valid, advantage, sent):
    high = parts[0, 0:1, :]
    for i in range(1, parts.shape[0]):
        high = jnp.maximum(high, parts[i, 0:1, :])
    sums = jnp.zeros((8, 128), f32)
    for i in range(parts.shape[0]):
        sums = sums + jnp.exp(parts[i, 0:1, :] - high) * parts[i]
    row = lax.broadcasted_iota(jnp.int32, (8, 128), 0)
    out = jnp.where(row == 0, high, sums)
    out = jnp.where(row == 3, valid[...].astype(f32), jnp.where(row == 4, advantage[...], out))
    for i in range(sent.shape[0]):
        sent[i] = out


def plan_kernel(start_high, parts, coef_out, normal_out, packed_out, slot_out, flag, rows):
    owners = 8
    ny = parts.shape[0] // owners
    for o in range(owners):
        high = parts[o * ny, 0:1, :]
        for y in range(1, ny):
            high = jnp.maximum(high, parts[o * ny + y, 0:1, :])
        sums = jnp.zeros((8, 128), f32)
        for y in range(ny):
            sums = sums + jnp.exp(parts[o * ny + y, 0:1, :] - high) * parts[o * ny + y]
        row = lax.broadcasted_iota(jnp.int32, (8, 128), 0)
        normal = high + jnp.log(sums[1:2, :])
        entropy = normal - sums[2:3, :] / sums[1:2, :]
        rows[o] = jnp.where(row == 0, normal, jnp.where(row == 1, entropy, parts[o * ny]))
    normal, entropy, valid, advantage = (
        jnp.concatenate([rows[o, k : k + 1, :] for o in range(owners)], axis=0) for k in (0, 1, 3, 4)
    )
    counted = jnp.sum(jnp.sum(valid, axis=1, keepdims=True), axis=0, keepdims=True)
    threshold = bisect(jnp.where(valid > 0.0, entropy, -jnp.inf), counted, start_high)
    gate = valid * jnp.clip((entropy - threshold) / ramp_width + 0.5, 0.0, 1.0)
    coef = -(gate * advantage)
    active = coef != 0.0
    activef = active.astype(f32)
    i = lax.broadcasted_iota(jnp.int32, (128, 128), 0)
    j = lax.broadcasted_iota(jnp.int32, (128, 128), 1)
    ahead = (i < j).astype(f32)
    group = 128 // (32 // owners)
    same = (i // group == j // group).astype(f32)
    rank_owner = jnp.dot(activef, ahead, preferred_element_type=f32)
    rank_group = jnp.dot(activef, ahead * same, preferred_element_type=f32)
    start = (lax.broadcasted_iota(jnp.int32, (8, 128), 1) // group * CAP).astype(f32)
    coef_out[...] = coef
    normal_out[...] = normal
    packed_out[...] = jnp.where(active, rank_owner, -1.0)
    slot_out[...] = jnp.where(active, rank_group + start, -1.0)
    over = jnp.where(active & (rank_owner >= CAP_SMALL), 1.0, 0.0)
    over = jnp.where(active & (rank_group >= CAP), 2.0, over)
    flag[0, 0] = jnp.max(over).astype(jnp.int32)


def as_columns(rows):
    row = lax.broadcasted_iota(jnp.int32, (8, 128), 0)
    out = jnp.zeros((8, 128), f32)
    for k, value in enumerate(rows):
        out = jnp.where(row == k, value, out)
    return jnp.transpose(out)


def one_hot(count, slots):
    row = lax.broadcasted_iota(jnp.int32, (count, 128), 0).astype(f32)
    return (row == slots).astype(f32).astype(bf16)


def slopes_kernel(at, logits, coef_all, normal_all, packed_all, ids, out):
    me = pl.ds(at[2], 1)
    count = out.shape[0]
    columns = as_columns([coef_all[me, :], normal_all[me, :], ids[...].astype(f32)])
    coef, normal, token = columns[:, 0:1], columns[:, 1:2], columns[:, 2:3].astype(jnp.int32) - at[3]
    choose = one_hot(count, packed_all[me, :])
    lane = lax.broadcasted_iota(jnp.int32, (128, 128), 1)
    for k in range(logits.shape[1] // 128):
        span = slice(k * 128, (k + 1) * 128)
        hit = (lane + k * 128 == token).astype(f32)
        slopes = (coef * (hit - jnp.exp(logits[:, span] - normal))).astype(bf16)
        out[:, span] = jnp.dot(choose, slopes, preferred_element_type=f32).astype(bf16)


def owner_of(at, s, k):
    return lax.rem(at[0] - s + NX, NX) * 2 + lax.rem(at[1] + k, 2)


def product_kernel(at, mine, theirs, turned, o0, o1, o2, o3, held):
    cap = mine.shape[0] // NX
    for k, rows in enumerate((mine, theirs)):
        held[k * NX * cap : (k + 1) * NX * cap, :] = jnp.dot(
            rows[...], turned[...], preferred_element_type=f32
        ).astype(bf16)
    for step, out in enumerate((o0, o1, o2, o3)):
        source = lax.rem(at[0] - at[5] - step + 2 * NX, NX) * cap
        for k in range(2):
            rows = pl.ds(pl.multiple_of(source + k * NX * cap, cap), cap)
            out[k * cap : (k + 1) * cap, :] = held[rows, :]


def outer_kernel(at, packed_all, hid_mine, hid_theirs, mine, theirs, out, tick, held):
    half = mine.shape[0]
    cap = half // NX
    tick[...] = jnp.zeros(tick.shape, f32)
    for k, hidden in enumerate((hid_mine, hid_theirs)):
        for s in range(NX):
            choose = one_hot(cap, packed_all[pl.ds(owner_of(at, s, k), 1), :])
            to = k * half + s * cap
            held[to : to + cap, :] = jnp.dot(
                choose, hidden[ORDER[s] * 128 : (ORDER[s] + 1) * 128, :], preferred_element_type=f32
            ).astype(bf16)
    slopes = jnp.concatenate([mine[...], theirs[...]], axis=0)
    out[...] = lax.dot_general(held[...], slopes, (((0,), (0,)), ((), ())), preferred_element_type=f32)


def spread_kernel(at, tick, r0, r1, r2, r3, packed_all, slot_all, out):
    size = out.shape[0]
    cap = r0.shape[0] // 2
    total = jnp.zeros(out.shape, f32)
    for k in range(2):
        core = lax.rem(at[1] + k, 2)
        me = pl.ds(at[5] * 2 + core, 1)
        slot = slot_all[me, :]
        slot = jnp.where(slot >= 0.0, slot + (core * (size // 2)).astype(f32), -1.0)
        spread = lax.dot_general(
            one_hot(size, slot),
            one_hot(cap, packed_all[me, :]),
            (((1,), (1,)), ((), ())),
            preferred_element_type=f32,
        ).astype(bf16)
        for r in (r0, r1, r2, r3):
            total = total + jnp.dot(spread, r[k * cap : (k + 1) * cap, :], preferred_element_type=f32)
    out[...] = total


def sum_kernel(at, parts, slot_all, out, ranks):
    total = parts[0:CAP, :]
    for i in range(1, parts.shape[0] // CAP):
        total = total + parts[i * CAP : (i + 1) * CAP, :]
    group = out.shape[0]
    per_owner = 128 // group
    owner, place = at[4] // per_owner, lax.rem(at[4], per_owner)
    ranks[...] = as_columns([slot_all[pl.ds(owner, 1), :]])
    rank = ranks[pl.ds(pl.multiple_of(place * group, group), group), :][:, 0:1]
    rank = rank - (place * CAP).astype(f32)
    rows = jnp.zeros(out.shape, f32)
    for r in range(CAP):
        rows = rows + jnp.where(rank == float(r), total[r : r + 1, :], 0.0)
    out[...] = rows


def shards(hidden_states, head, token_ids, valid, advantage):
    tokens, width = hidden_states.shape
    rows, voc_cols = head.shape
    nx, n_voc, n_dp = lax.axis_size("x"), lax.axis_size(VOC), lax.axis_size(DP)
    x, c, block = lax.axis_index("x"), lax.axis_index("c"), lax.axis_index(VOC)
    at = jnp.stack([x, c, x * 2 + c, block * voc_cols, block, lax.axis_index("y")]).astype(jnp.int32)
    chip_rows = width // nx

    head_other = lax.ppermute(head, "c", SWAP)

    block_shape = struct((tokens, chip_rows), bf16)
    b0, *leave = call(split_kernel, [block_shape] * 4, [at, hidden_states], smem=1)
    came = {s: lax.ppermute(leave[s - 1], "x", ring(nx, s)) for s in (2, 1, 3)}
    partial = struct((tokens, voc_cols), f32)
    tick_shape = struct((8, 128), f32)
    own, kept = call(
        own_kernel,
        [partial, struct((rows, voc_cols), bf16)],
        [at, b0, head, head_other],
        smem=1,
        cost_estimate=estimate(tokens, chip_rows, voc_cols),
    )
    half = struct((tokens // 2, voc_cols + 128), jnp.int16)
    low, high, tick = call(
        far_kernel,
        [half, half, tick_shape],
        [at, came[2], kept, head_other],
        [pltpu.VMEM((tokens, voc_cols), f32)],
        smem=1,
        cost_estimate=estimate(tokens, chip_rows, voc_cols),
    )
    low, high = lax.ppermute(low, "x", ring(nx, -1)), lax.ppermute(high, "x", ring(nx, 1))
    p1, p3, hid_mine, hid_send = call(
        near_kernel,
        [partial] * 2 + [struct((nx * tokens, rows), bf16)] * 2,
        [at, tick, b0, came[1], came[2], came[3], kept, head_other],
        vmem=24,
        smem=1,
        cost_estimate=estimate(2 * tokens, chip_rows, voc_cols),
    )
    packed = struct((tokens, voc_cols + 128), jnp.int16)
    q1, q3, tick = call(relay_kernel, [packed] * 2 + [tick_shape], [p1, p3, low, high])
    q1, q3 = lax.ppermute(q1, "x", ring(nx, -1)), lax.ppermute(q3, "x", ring(nx, 1))
    turned = call(turn_kernel, struct((voc_cols, rows), bf16), [tick, kept])
    hid_theirs = lax.ppermute(hid_send, "c", SWAP)
    logits, stats = call(
        total_kernel,
        [partial, struct((lax.axis_size("z"), 8, 128), f32)],
        [own, q1, q3],
        [pltpu.VMEM((tokens, 128), f32)],
    )

    stats = lax.all_to_all(stats, "z", 0, 0, tiled=True)
    everyone = DP + ("y",)
    stats = call(
        merge_kernel,
        struct((lax.axis_size(everyone), 8, 128), f32),
        [stats, valid.reshape(1, tokens), advantage.reshape(1, tokens)],
    )
    stats = lax.all_to_all(stats, everyone, 0, 0, tiled=True)
    start_high = float(np.float32(np.log(np.float32(voc_cols * n_voc))) + np.float32(1.0))
    table = struct((n_dp, tokens), f32)
    coef_all, normal_all, packed_all, slot_all, flag = call(
        functools.partial(plan_kernel, start_high),
        [table] * 4 + [struct((1, 1), jnp.int32)],
        [stats],
        [pltpu.VMEM((n_dp, 8, 128), f32)],
        out_specs=[pl.BlockSpec(memory_space=pltpu.VMEM)] * 4 + [pl.BlockSpec(memory_space=pltpu.SMEM)],
    )

    def sparse(cap, _):
        piece = call(
            slopes_kernel,
            struct((cap, voc_cols), bf16),
            [at, logits, coef_all, normal_all, packed_all, token_ids.reshape(1, tokens)],
            smem=1,
        )
        pieces = {s: lax.ppermute(piece, "x", ring(nx, s)) for s in (2, 1, 3)}
        mine = jnp.concatenate([piece, pieces[1], pieces[2], pieces[3]], axis=0)
        theirs = lax.ppermute(mine, "c", SWAP)
        parts = call(
            product_kernel,
            [struct((2 * cap, rows), bf16)] * nx,
            [at, mine, theirs, turned],
            [pltpu.VMEM((2 * nx * cap, rows), bf16)],
            smem=1,
        )
        parts = [parts[0]] + [lax.ppermute(parts[k], "y", ring(nx, k)) for k in range(1, nx)]
        tile = 128
        whole_block = lambda i: (0, 0)
        head_grad, tick = pl.pallas_call(
            outer_kernel,
            grid=(rows // tile,),
            in_specs=[
                pl.BlockSpec(memory_space=pltpu.SMEM),
                pl.BlockSpec((n_dp, tokens), whole_block),
                pl.BlockSpec((nx * tokens, tile), lambda i: (0, i)),
                pl.BlockSpec((nx * tokens, tile), lambda i: (0, i)),
                pl.BlockSpec((nx * cap, voc_cols), whole_block),
                pl.BlockSpec((nx * cap, voc_cols), whole_block),
            ],
            out_specs=[pl.BlockSpec((tile, voc_cols), lambda i: (i, 0)), pl.BlockSpec((8, 128), whole_block)],
            out_shape=[struct((rows, voc_cols), f32), tick_shape],
            scratch_shapes=[pltpu.VMEM((2 * nx * cap, tile), bf16)],
            compiler_params=pltpu.CompilerParams(vmem_limit_bytes=24 << 20),
            cost_estimate=estimate(rows, 2 * nx * cap, voc_cols),
        )(at, packed_all, hid_mine, hid_theirs, mine, theirs)
        spread = call(
            spread_kernel,
            struct((n_voc * CAP // nx, rows), f32),
            [at, tick, *parts, packed_all, slot_all],
            smem=1,
        )
        spread = lax.all_to_all(spread, "z", 0, 0, tiled=True)
        hidden_grad = call(
            sum_kernel,
            struct((tokens * n_dp // n_voc, rows), f32),
            [at, spread, slot_all],
            [pltpu.VMEM((tokens, 8), f32)],
            smem=1,
        )
        return hidden_grad, head_grad

    def whole(_):
        return dense(hidden_states, head, token_ids, valid, advantage)

    small = functools.partial(sparse, CAP_SMALL)
    large = functools.partial(sparse, CAP * n_voc // n_dp)
    return lax.switch(flag[0, 0], [small, large, whole], 0)


def solution(mesh):
    chips = Mesh(mesh.devices.reshape(4, 2, 4, 8), DP + VOC)
    placed = (P(DP, None), P(DP, VOC), P(DP), P(DP), P(DP))
    return jax.shard_map(
        shards,
        mesh=chips,
        in_specs=placed,
        out_specs=(P(VOC, DP), P(DP, VOC)),
        check_vma=False,
    )
```

```python
import functools

import jax
import jax.numpy as jnp
import numpy as np
from jax import lax
from jax.experimental import pallas as pl
from jax.experimental.pallas import tpu as pltpu
from jax.sharding import Mesh, PartitionSpec as P

ROUNDS = 24
LEVELS = 6
CAP = 16
CAP_SMALL = 32
ORDER = (2, 0, 3, 1)
NX = 4

ramp_width = 0.5
DP = ("x", "c")
VOC = ("y", "z")
f32 = jnp.float32
bf16 = jnp.bfloat16


def ring(n, shift):
    return [(i, (i + shift) % n) for i in range(n)]


SWAP = [(0, 1), (1, 0)]


def dense(hidden_states, head, token_ids, valid, advantage):
    voc_cols = head.shape[1]
    columns = lax.all_to_all(hidden_states, DP, split_axis=1, concat_axis=0, tiled=True)
    logits = lax.psum_scatter(
        jnp.dot(columns, head, preferred_element_type=f32), DP, scatter_dimension=0, tiled=True
    )
    offset = lax.axis_index(VOC) * voc_cols
    hit = jnp.arange(voc_cols, dtype=jnp.int32)[None, :] + offset == token_ids[:, None]
    highest = lax.pmax(jnp.max(logits, axis=1), VOC)
    shifted = jnp.exp(logits - highest[:, None])
    total, moment = lax.psum((jnp.sum(shifted, axis=1), jnp.sum(shifted * logits, axis=1)), VOC)
    normal = highest + jnp.log(total)
    entropy = normal - moment / total
    validf = valid.astype(f32)
    start_high = jnp.log(f32(voc_cols * lax.axis_size(VOC))) + 1.0
    counted = lax.psum(jnp.sum(validf), DP)
    quota = jnp.floor((counted + 0.5) * 0.2)

    def round_step(step, bounds):
        low, high = bounds
        middle = (low + high) * 0.5
        above = lax.psum(jnp.sum(jnp.where(entropy > middle, validf, 0.0)), DP)
        more = above > quota
        return (jnp.where(more, middle, low), jnp.where(more, high, middle))

    _, threshold = lax.fori_loop(0, ROUNDS, round_step, (f32(0.0), start_high))
    gate = validf * jnp.clip((entropy - threshold) / ramp_width + 0.5, 0.0, 1.0)
    coef = -(gate * advantage)
    probs = jnp.exp(logits - normal[:, None])
    slopes = (coef[:, None] * (hit.astype(f32) - probs)).astype(bf16)
    piece = lax.all_gather(slopes, DP, axis=0, tiled=True)
    head_grad = lax.dot_general(columns, piece, (((0,), (0,)), ((), ())), preferred_element_type=f32)
    product = lax.dot_general(piece, head, (((1,), (1,)), ((), ())), preferred_element_type=f32)
    return lax.psum_scatter(product, VOC, scatter_dimension=0, tiled=True), head_grad


def bisect(entropy, counted, start_high):
    columns = jnp.transpose(entropy)
    quota = jnp.floor((counted + 0.5) * 0.2)
    lane = lax.broadcasted_iota(jnp.int32, (1, 128), 1)
    leaves = 1 << LEVELS
    low = jnp.zeros((1, 128), f32)
    high = jnp.full((1, 128), start_high, f32)
    for _ in range(ROUNDS // LEVELS):
        for level in range(LEVELS):
            middle = (low + high) * 0.5
            bit = ((lane >> (LEVELS - 1 - level)) & 1) == 1
            low, high = jnp.where(bit, middle, low), jnp.where(bit, high, middle)
        above = jnp.zeros((128, 128), f32)
        for i in range(8):
            above = above + jnp.where(columns[:, i : i + 1] > low, 1.0, 0.0)
        above = jnp.sum(above, axis=0, keepdims=True)
        more = jnp.where(((above > quota) | (lane == 0)) & (lane < leaves), 1.0, 0.0)
        here = lane == jnp.sum(more, axis=1, keepdims=True).astype(jnp.int32) - 1
        low, high = (
            jnp.broadcast_to(jnp.sum(jnp.where(here, v, 0.0), axis=1, keepdims=True), (1, 128))
            for v in (low, high)
        )
    return high[:, :1]


def call(kernel, out, args, scratch=(), vmem=16, smem=0, loose=0, **kw):
    specs = [pl.BlockSpec(memory_space=pltpu.SMEM)] * smem
    specs += [pl.BlockSpec(memory_space=pltpu.VMEM)] * (len(args) - smem - loose)
    specs += [pl.BlockSpec(memory_space=pl.ANY)] * loose
    return pl.pallas_call(
        kernel,
        in_specs=specs,
        out_shape=out,
        scratch_shapes=list(scratch),
        compiler_params=pltpu.CompilerParams(vmem_limit_bytes=vmem << 20),
        **kw,
    )(*args)


def struct(shape, dtype):
    return jax.ShapeDtypeStruct(shape, dtype)


def estimate(m, k, n):
    return pl.CostEstimate(flops=2 * m * k * n, bytes_accessed=2 * k * n, transcendentals=0)


LN2_64 = float(np.log(2.0) / 64.0)


def split_kernel(at, hidden, b0, b1, b2, b3):
    chip_rows = b0.shape[1]
    nx = hidden.shape[1] // chip_rows
    for s, out in enumerate((b0, b1, b2, b3)):
        to = lax.rem(at[0] + s, nx) * chip_rows
        out[...] = hidden[:, pl.ds(pl.multiple_of(to, 128), chip_rows)]


def turn_kernel(tick, head, turned):
    for k in range(head.shape[1] // 128):
        span = slice(k * 128, (k + 1) * 128)
        turned[span, :] = jnp.transpose(head[:, span])


def pack(block, out, to):
    step, cols = block.shape
    top = jnp.maximum(jnp.max(jnp.abs(block), axis=1, keepdims=True), 1e-30)
    power = jnp.ceil(jnp.log(top) * (1.0 / LN2_64)) + 1.0
    fixed = jnp.round(block * (jnp.exp(power * -LN2_64) * 32766.0))
    out[to, 0:cols] = fixed.astype(jnp.int32).astype(jnp.int16)
    wide_power = jnp.broadcast_to(power.astype(jnp.int32), (step, 128))
    out[to, cols : cols + 128] = wide_power.astype(jnp.int16)


def unpack(ref, at):
    cols = ref.shape[1] - 128
    power = ref[at, cols : cols + 128].astype(jnp.int32).astype(f32)[:, :1]
    return ref[at, 0:cols].astype(jnp.int32).astype(f32) * (jnp.exp(power * LN2_64) * (1.0 / 32766.0))


def over_columns(cols, tile):
    for start in range(0, cols, 256):
        tile(slice(start, min(start + 256, cols)))


def halves(at, rows):
    return (
        pl.ds(pl.multiple_of(at[1] * rows, 128), rows),
        pl.ds(pl.multiple_of((1 - at[1]) * rows, 128), rows),
    )


def own_kernel(at, block, head, other, own, kept):
    kept[...] = head[...]
    here, there = halves(at, head.shape[0])

    def tile(span):
        own[:, span] = jnp.dot(block[:, here], head[:, span], preferred_element_type=f32) + jnp.dot(
            block[:, there], other[:, span], preferred_element_type=f32
        )

    over_columns(head.shape[1], tile)


def far_kernel(at, block, head, other, low, high, tick, part):
    tokens = block.shape[0]
    rows, cols = head.shape
    here, there = halves(at, rows)

    def tile(span):
        part[:, span] = jnp.dot(block[:, here], head[:, span], preferred_element_type=f32) + jnp.dot(
            block[:, there], other[:, span], preferred_element_type=f32
        )

    over_columns(cols, tile)
    tick[...] = jnp.zeros(tick.shape, f32)
    step = 32
    for k, out in enumerate((low, high)):

        @pl.loop(0, tokens // 2 // step)
        def _(i, k=k, out=out):
            source = pl.multiple_of(k * (tokens // 2) + i * step, step)
            pack(part[pl.ds(source, step), :], out, pl.ds(pl.multiple_of(i * step, step), step))


def near_kernel(at, tick, b0, b1, b2, b3, head, other, p1, p3, mine, theirs):
    tokens = b0.shape[0]
    rows, cols = head.shape
    here, there = halves(at, rows)
    for k, block in enumerate((b1, b3, b0, b2)):
        mine[k * tokens : (k + 1) * tokens, :] = block[:, here]
        theirs[k * tokens : (k + 1) * tokens, :] = block[:, there]

    def tile(span):
        part = jnp.dot(mine[0 : 2 * tokens, :], head[:, span], preferred_element_type=f32) + jnp.dot(
            theirs[0 : 2 * tokens, :], other[:, span], preferred_element_type=f32
        )
        p1[:, span] = part[0:tokens, :]
        p3[:, span] = part[tokens:, :]

    over_columns(cols, tile)


def relay_kernel(p1, p3, low, high, q1, q3, tick):
    tokens = p1.shape[0]
    half, step = tokens // 2, 32
    tick[...] = jnp.zeros(tick.shape, f32)

    @pl.loop(0, half // step)
    def _(i):
        near = pl.ds(pl.multiple_of(i * step, step), step)
        far = pl.ds(pl.multiple_of(half + i * step, step), step)
        pack(p1[near, :] + unpack(low, near), q1, near)
        pack(p1[far, :], q1, far)
        pack(p3[near, :], q3, near)
        pack(p3[far, :] + unpack(high, near), q3, far)


def total_kernel(own, q1, q3, turned, theirs, logits, sent, stats):
    tokens = own.shape[0]
    step = 16
    lane = lax.broadcasted_iota(jnp.int32, (step, 128), 1)
    for start in range(0, tokens, step):
        at = slice(start, start + step)
        value = own[at, :] + unpack(q1, at) + unpack(q3, at)
        logits[at, :] = value
        high = jnp.max(value, axis=1, keepdims=True)
        shifted = jnp.exp(value - high)
        total = jnp.sum(shifted, axis=1, keepdims=True)
        moment = jnp.sum(shifted * value, axis=1, keepdims=True)
        stats[at, :] = jnp.where(lane == 0, high, jnp.where(lane == 1, total, moment))

    rows = jnp.transpose(stats[...])[0:8, :]
    for i in range(sent.shape[0]):
        sent[i] = rows


def merge_kernel(parts, valid, advantage, sent):
    high = parts[0, 0:1, :]
    for i in range(1, parts.shape[0]):
        high = jnp.maximum(high, parts[i, 0:1, :])
    sums = jnp.zeros((8, 128), f32)
    for i in range(parts.shape[0]):
        sums = sums + jnp.exp(parts[i, 0:1, :] - high) * parts[i]
    row = lax.broadcasted_iota(jnp.int32, (8, 128), 0)
    out = jnp.where(row == 0, high, sums)
    out = jnp.where(row == 3, valid[...].astype(f32), jnp.where(row == 4, advantage[...], out))
    for i in range(sent.shape[0]):
        sent[i] = out


def plan_kernel(start_high, parts, coef_out, normal_out, packed_out, slot_out, flag, rows):
    owners = 8
    ny = parts.shape[0] // owners
    for o in range(owners):
        high = parts[o * ny, 0:1, :]
        for y in range(1, ny):
            high = jnp.maximum(high, parts[o * ny + y, 0:1, :])
        sums = jnp.zeros((8, 128), f32)
        for y in range(ny):
            sums = sums + jnp.exp(parts[o * ny + y, 0:1, :] - high) * parts[o * ny + y]
        row = lax.broadcasted_iota(jnp.int32, (8, 128), 0)
        normal = high + jnp.log(sums[1:2, :])
        entropy = normal - sums[2:3, :] / sums[1:2, :]
        rows[o] = jnp.where(row == 0, normal, jnp.where(row == 1, entropy, parts[o * ny]))
    normal, entropy, valid, advantage = (
        jnp.concatenate([rows[o, k : k + 1, :] for o in range(owners)], axis=0) for k in (0, 1, 3, 4)
    )
    counted = jnp.sum(jnp.sum(valid, axis=1, keepdims=True), axis=0, keepdims=True)
    threshold = bisect(jnp.where(valid > 0.0, entropy, -jnp.inf), counted, start_high)
    gate = valid * jnp.clip((entropy - threshold) / ramp_width + 0.5, 0.0, 1.0)
    coef = -(gate * advantage)
    active = coef != 0.0
    activef = active.astype(f32)
    i = lax.broadcasted_iota(jnp.int32, (128, 128), 0)
    j = lax.broadcasted_iota(jnp.int32, (128, 128), 1)
    ahead = (i < j).astype(f32)
    group = 128 // (32 // owners)
    same = (i // group == j // group).astype(f32)
    rank_owner = jnp.dot(activef, ahead, preferred_element_type=f32)
    rank_group = jnp.dot(activef, ahead * same, preferred_element_type=f32)
    start = (lax.broadcasted_iota(jnp.int32, (8, 128), 1) // group * CAP).astype(f32)
    coef_out[...] = coef
    normal_out[...] = normal
    packed_out[...] = jnp.where(active, rank_owner, -1.0)
    slot_out[...] = jnp.where(active, rank_group + start, -1.0)
    over = jnp.where(active & (rank_owner >= CAP_SMALL), 1.0, 0.0)
    over = jnp.where(active & (rank_group >= CAP), 2.0, over)
    flag[0, 0] = jnp.max(over).astype(jnp.int32)


def as_columns(rows):
    row = lax.broadcasted_iota(jnp.int32, (8, 128), 0)
    out = jnp.zeros((8, 128), f32)
    for k, value in enumerate(rows):
        out = jnp.where(row == k, value, out)
    return jnp.transpose(out)


def one_hot(count, slots):
    row = lax.broadcasted_iota(jnp.int32, (count, 128), 0).astype(f32)
    return (row == slots).astype(f32).astype(bf16)


def slopes_kernel(at, logits, coef_all, normal_all, packed_all, ids, out):
    me = pl.ds(at[2], 1)
    count = out.shape[0]
    columns = as_columns([coef_all[me, :], normal_all[me, :], ids[...].astype(f32)])
    coef, normal, token = columns[:, 0:1], columns[:, 1:2], columns[:, 2:3].astype(jnp.int32) - at[3]
    choose = one_hot(count, packed_all[me, :])
    lane = lax.broadcasted_iota(jnp.int32, (128, 128), 1)
    for k in range(logits.shape[1] // 128):
        span = slice(k * 128, (k + 1) * 128)
        hit = (lane + k * 128 == token).astype(f32)
        slopes = (coef * (hit - jnp.exp(logits[:, span] - normal))).astype(bf16)
        out[:, span] = jnp.dot(choose, slopes, preferred_element_type=f32).astype(bf16)


def owner_of(at, s, k):
    return lax.rem(at[0] - s + NX, NX) * 2 + lax.rem(at[1] + k, 2)


def product_kernel(at, mine, theirs, turned, slopes, o0, o1, o2, o3, held):
    half = mine.shape[0]
    cap = half // NX
    slopes[0:half, :] = mine[...]
    slopes[half:, :] = theirs[...]
    held[...] = jnp.dot(slopes[...], turned[...], preferred_element_type=f32).astype(bf16)
    for step, out in enumerate((o0, o1, o2, o3)):
        source = lax.rem(at[0] - at[5] - step + 2 * NX, NX) * cap
        for k in range(2):
            rows = pl.ds(pl.multiple_of(source + k * half, cap), cap)
            out[k * cap : (k + 1) * cap, :] = held[rows, :]


def outer_kernel(at, packed_all, hid_mine, hid_theirs, slopes, above, after, out, tick, held):
    half = slopes.shape[0] // 2
    cap = half // NX
    tick[...] = jnp.zeros(tick.shape, f32)
    for k, hidden in enumerate((hid_mine, hid_theirs)):
        for s in range(NX):
            choose = one_hot(cap, packed_all[pl.ds(owner_of(at, s, k), 1), :])
            to = k * half + s * cap
            held[to : to + cap, :] = jnp.dot(
                choose, hidden[ORDER[s] * 128 : (ORDER[s] + 1) * 128, :], preferred_element_type=f32
            ).astype(bf16)
    out[...] = lax.dot_general(
        held[...], slopes[...], (((0,), (0,)), ((), ())), preferred_element_type=f32
    )


def outer(at, packed_all, hid_mine, hid_theirs, slopes, first, count, above, after):
    (tokens, rows), (depth, cols) = hid_mine.shape, slopes.shape
    tile = 128
    whole_block = lambda i: (0, 0)
    in_specs = [
        pl.BlockSpec(memory_space=pltpu.SMEM),
        pl.BlockSpec(packed_all.shape, whole_block),
        pl.BlockSpec((tokens, tile), lambda i: (0, i + first)),
        pl.BlockSpec((tokens, tile), lambda i: (0, i + first)),
        pl.BlockSpec((depth, cols), whole_block),
        pl.BlockSpec(memory_space=pl.ANY),
        pl.BlockSpec(memory_space=pl.ANY),
    ]
    aliases = {5: 0} if above.shape == (rows, cols) else {}
    return pl.pallas_call(
        outer_kernel,
        grid=(count,),
        in_specs=in_specs,
        out_specs=[pl.BlockSpec((tile, cols), lambda i: (i + first, 0)), pl.BlockSpec((8, 128), whole_block)],
        out_shape=[struct((rows, cols), f32), struct((8, 128), f32)],
        scratch_shapes=[pltpu.VMEM((depth, tile), bf16)],
        input_output_aliases=aliases,
        compiler_params=pltpu.CompilerParams(vmem_limit_bytes=24 << 20),
        cost_estimate=estimate(count * tile, depth, cols),
    )(at, packed_all, hid_mine, hid_theirs, slopes, above, after)


def spread_kernel(at, before, r0, r1, r2, r3, packed_all, slot_all, out, tick):
    size = out.shape[0]
    cap = r0.shape[0] // 2
    tick[...] = jnp.zeros(tick.shape, f32)
    total = jnp.zeros(out.shape, f32)
    for k in range(2):
        core = lax.rem(at[1] + k, 2)
        me = pl.ds(at[5] * 2 + core, 1)
        slot = slot_all[me, :]
        slot = jnp.where(slot >= 0.0, slot + (core * (size // 2)).astype(f32), -1.0)
        spread = lax.dot_general(
            one_hot(size, slot),
            one_hot(cap, packed_all[me, :]),
            (((1,), (1,)), ((), ())),
            preferred_element_type=f32,
        ).astype(bf16)
        for r in (r0, r1, r2, r3):
            total = total + jnp.dot(spread, r[k * cap : (k + 1) * cap, :], preferred_element_type=f32)
    out[...] = total


def sum_kernel(at, parts, slot_all, out, ranks):
    total = parts[0:CAP, :]
    for i in range(1, parts.shape[0] // CAP):
        total = total + parts[i * CAP : (i + 1) * CAP, :]
    group = out.shape[0]
    per_owner = 128 // group
    owner, place = at[4] // per_owner, lax.rem(at[4], per_owner)
    ranks[...] = as_columns([slot_all[pl.ds(owner, 1), :]])
    rank = ranks[pl.ds(pl.multiple_of(place * group, group), group), :][:, 0:1]
    rank = rank - (place * CAP).astype(f32)
    rows = jnp.zeros(out.shape, f32)
    for r in range(CAP):
        rows = rows + jnp.where(rank == float(r), total[r : r + 1, :], 0.0)
    out[...] = rows


def shards(hidden_states, head, token_ids, valid, advantage):
    tokens, width = hidden_states.shape
    rows, voc_cols = head.shape
    nx, n_voc, n_dp = lax.axis_size("x"), lax.axis_size(VOC), lax.axis_size(DP)
    x, c, block = lax.axis_index("x"), lax.axis_index("c"), lax.axis_index(VOC)
    at = jnp.stack([x, c, x * 2 + c, block * voc_cols, block, lax.axis_index("y")]).astype(jnp.int32)
    chip_rows = width // nx

    head_other = lax.ppermute(head, "c", SWAP)

    block_shape = struct((tokens, chip_rows), bf16)
    b0, *leave = call(split_kernel, [block_shape] * 4, [at, hidden_states], smem=1)
    came = {s: lax.ppermute(leave[s - 1], "x", ring(nx, s)) for s in (2, 1, 3)}
    partial = struct((tokens, voc_cols), f32)
    tick_shape = struct((8, 128), f32)
    own, kept = call(
        own_kernel,
        [partial, struct((rows, voc_cols), bf16)],
        [at, b0, head, head_other],
        smem=1,
        cost_estimate=estimate(tokens, chip_rows, voc_cols),
    )
    half = struct((tokens // 2, voc_cols + 128), jnp.int16)
    low, high, tick = call(
        far_kernel,
        [half, half, tick_shape],
        [at, came[2], kept, head_other],
        [pltpu.VMEM((tokens, voc_cols), f32)],
        smem=1,
        cost_estimate=estimate(tokens, chip_rows, voc_cols),
    )
    low, high = lax.ppermute(low, "x", ring(nx, -1)), lax.ppermute(high, "x", ring(nx, 1))
    p1, p3, hid_mine, hid_send = call(
        near_kernel,
        [partial] * 2 + [struct((nx * tokens, rows), bf16)] * 2,
        [at, tick, b0, came[1], came[2], came[3], kept, head_other],
        vmem=24,
        smem=1,
        cost_estimate=estimate(2 * tokens, chip_rows, voc_cols),
    )
    packed = struct((tokens, voc_cols + 128), jnp.int16)
    q1, q3, tick = call(relay_kernel, [packed] * 2 + [tick_shape], [p1, p3, low, high])
    q1, q3 = lax.ppermute(q1, "x", ring(nx, -1)), lax.ppermute(q3, "x", ring(nx, 1))
    turned = call(turn_kernel, struct((voc_cols, rows), bf16), [tick, kept])
    hid_theirs = lax.ppermute(hid_send, "c", SWAP)
    logits, stats = call(
        total_kernel,
        [partial, struct((lax.axis_size("z"), 8, 128), f32)],
        [own, q1, q3, turned, hid_theirs],
        [pltpu.VMEM((tokens, 128), f32)],
        loose=2,
    )

    stats = lax.all_to_all(stats, "z", 0, 0, tiled=True)
    everyone = DP + ("y",)
    stats = call(
        merge_kernel,
        struct((lax.axis_size(everyone), 8, 128), f32),
        [stats, valid.reshape(1, tokens), advantage.reshape(1, tokens)],
    )
    stats = lax.all_to_all(stats, everyone, 0, 0, tiled=True)
    start_high = float(np.float32(np.log(np.float32(voc_cols * n_voc))) + np.float32(1.0))
    table = struct((n_dp, tokens), f32)
    coef_all, normal_all, packed_all, slot_all, flag = call(
        functools.partial(plan_kernel, start_high),
        [table] * 4 + [struct((1, 1), jnp.int32)],
        [stats],
        [pltpu.VMEM((n_dp, 8, 128), f32)],
        out_specs=[pl.BlockSpec(memory_space=pltpu.VMEM)] * 4 + [pl.BlockSpec(memory_space=pltpu.SMEM)],
    )

    def backward(cap):
        piece = call(
            slopes_kernel,
            struct((cap, voc_cols), bf16),
            [at, logits, coef_all, normal_all, packed_all, token_ids.reshape(1, tokens)],
            smem=1,
        )
        pieces = {s: lax.ppermute(piece, "x", ring(nx, s)) for s in (2, 1, 3)}
        mine = jnp.concatenate([piece, pieces[1], pieces[2], pieces[3]], axis=0)
        theirs = lax.ppermute(mine, "c", SWAP)
        return call(
            product_kernel,
            [struct((2 * nx * cap, voc_cols), bf16)] + [struct((2 * cap, rows), bf16)] * nx,
            [at, mine, theirs, turned],
            [pltpu.VMEM((2 * nx * cap, rows), bf16)],
            smem=1,
        )

    def finish(slopes, *parts):
        parts = [parts[0]] + [lax.ppermute(parts[k], "y", ring(nx, k)) for k in range(1, nx)]
        sides = (at, packed_all, hid_mine, hid_theirs, slopes)
        blocks = rows // 128
        early = (blocks + 1) // 2
        head_grad, tick = outer(*sides, 0, early, packed_all, packed_all)
        spread, tick = call(
            spread_kernel,
            [struct((n_voc * CAP // nx, rows), f32), tick_shape],
            [at, tick, *parts, packed_all, slot_all],
            smem=1,
        )
        spread = lax.all_to_all(spread, "z", 0, 0, tiled=True)
        head_grad, _ = outer(*sides, early, blocks - early, head_grad, tick)
        hidden_grad = call(
            sum_kernel,
            struct((tokens * n_dp // n_voc, rows), f32),
            [at, spread, slot_all],
            [pltpu.VMEM((tokens, 8), f32)],
            smem=1,
        )
        return hidden_grad, head_grad

    def whole(_):
        return dense(hidden_states, head, token_ids, valid, advantage)

    packed_rows = backward(CAP_SMALL)

    def small(_):
        return finish(*packed_rows)

    def large(_):
        return finish(*backward(CAP * n_voc // n_dp))

    return lax.switch(flag[0, 0], [small, large, whole], 0)


def solution(mesh):
    chips = Mesh(mesh.devices.reshape(4, 2, 4, 8), DP + VOC)
    placed = (P(DP, None), P(DP, VOC), P(DP), P(DP), P(DP))
    return jax.shard_map(
        shards,
        mesh=chips,
        in_specs=placed,
        out_specs=(P(VOC, DP), P(DP, VOC)),
        check_vma=False,
    )
```

```python
import functools

import jax
import jax.numpy as jnp
import numpy as np
from jax import lax
from jax.experimental import pallas as pl
from jax.experimental.pallas import tpu as pltpu
from jax.sharding import Mesh, PartitionSpec as P

ROUNDS = 24
LEVELS = 6
CAP = 16
CAP_SMALL = 32
ORDER = (2, 0, 3, 1)
NX = 4

ramp_width = 0.5
DP = ("x", "c")
VOC = ("y", "z")
f32 = jnp.float32
bf16 = jnp.bfloat16


def ring(n, shift):
    return [(i, (i + shift) % n) for i in range(n)]


SWAP = [(0, 1), (1, 0)]


def dense(hidden_states, head, token_ids, valid, advantage):
    voc_cols = head.shape[1]
    columns = lax.all_to_all(hidden_states, DP, split_axis=1, concat_axis=0, tiled=True)
    logits = lax.psum_scatter(
        jnp.dot(columns, head, preferred_element_type=f32), DP, scatter_dimension=0, tiled=True
    )
    offset = lax.axis_index(VOC) * voc_cols
    hit = jnp.arange(voc_cols, dtype=jnp.int32)[None, :] + offset == token_ids[:, None]
    highest = lax.pmax(jnp.max(logits, axis=1), VOC)
    shifted = jnp.exp(logits - highest[:, None])
    total, moment = lax.psum((jnp.sum(shifted, axis=1), jnp.sum(shifted * logits, axis=1)), VOC)
    normal = highest + jnp.log(total)
    entropy = normal - moment / total
    validf = valid.astype(f32)
    start_high = jnp.log(f32(voc_cols * lax.axis_size(VOC))) + 1.0
    counted = lax.psum(jnp.sum(validf), DP)
    quota = jnp.floor((counted + 0.5) * 0.2)

    def round_step(step, bounds):
        low, high = bounds
        middle = (low + high) * 0.5
        above = lax.psum(jnp.sum(jnp.where(entropy > middle, validf, 0.0)), DP)
        more = above > quota
        return (jnp.where(more, middle, low), jnp.where(more, high, middle))

    _, threshold = lax.fori_loop(0, ROUNDS, round_step, (f32(0.0), start_high))
    gate = validf * jnp.clip((entropy - threshold) / ramp_width + 0.5, 0.0, 1.0)
    coef = -(gate * advantage)
    probs = jnp.exp(logits - normal[:, None])
    slopes = (coef[:, None] * (hit.astype(f32) - probs)).astype(bf16)
    piece = lax.all_gather(slopes, DP, axis=0, tiled=True)
    head_grad = lax.dot_general(columns, piece, (((0,), (0,)), ((), ())), preferred_element_type=f32)
    product = lax.dot_general(piece, head, (((1,), (1,)), ((), ())), preferred_element_type=f32)
    return lax.psum_scatter(product, VOC, scatter_dimension=0, tiled=True), head_grad


def bisect(entropy, counted, start_high):
    columns = jnp.transpose(entropy)
    quota = jnp.floor((counted + 0.5) * 0.2)
    lane = lax.broadcasted_iota(jnp.int32, (1, 128), 1)
    leaves = 1 << LEVELS
    low = jnp.zeros((1, 128), f32)
    high = jnp.full((1, 128), start_high, f32)
    for _ in range(ROUNDS // LEVELS):
        for level in range(LEVELS):
            middle = (low + high) * 0.5
            bit = ((lane >> (LEVELS - 1 - level)) & 1) == 1
            low, high = jnp.where(bit, middle, low), jnp.where(bit, high, middle)
        above = jnp.zeros((128, 128), f32)
        for i in range(8):
            above = above + jnp.where(columns[:, i : i + 1] > low, 1.0, 0.0)
        above = jnp.sum(above, axis=0, keepdims=True)
        more = jnp.where(((above > quota) | (lane == 0)) & (lane < leaves), 1.0, 0.0)
        here = lane == jnp.sum(more, axis=1, keepdims=True).astype(jnp.int32) - 1
        low, high = (
            jnp.broadcast_to(jnp.sum(jnp.where(here, v, 0.0), axis=1, keepdims=True), (1, 128))
            for v in (low, high)
        )
    return high[:, :1]


def call(kernel, out, args, scratch=(), vmem=16, smem=0, loose=0, **kw):
    specs = [pl.BlockSpec(memory_space=pltpu.SMEM)] * smem
    specs += [pl.BlockSpec(memory_space=pltpu.VMEM)] * (len(args) - smem - loose)
    specs += [pl.BlockSpec(memory_space=pl.ANY)] * loose
    return pl.pallas_call(
        kernel,
        in_specs=specs,
        out_shape=out,
        scratch_shapes=list(scratch),
        compiler_params=pltpu.CompilerParams(vmem_limit_bytes=vmem << 20),
        **kw,
    )(*args)


def struct(shape, dtype):
    return jax.ShapeDtypeStruct(shape, dtype)


def estimate(m, k, n):
    return pl.CostEstimate(flops=2 * m * k * n, bytes_accessed=2 * k * n, transcendentals=0)


LN2_64 = float(np.log(2.0) / 64.0)


def split_kernel(at, hidden, b0, b1, b2, b3):
    chip_rows = b0.shape[1]
    nx = hidden.shape[1] // chip_rows
    for s, out in enumerate((b0, b1, b2, b3)):
        to = lax.rem(at[0] + s, nx) * chip_rows
        out[...] = hidden[:, pl.ds(pl.multiple_of(to, 128), chip_rows)]


def turn_kernel(tick, head, turned):
    for k in range(head.shape[1] // 128):
        span = slice(k * 128, (k + 1) * 128)
        turned[span, :] = jnp.transpose(head[:, span])


def pack(block, out, to):
    step, cols = block.shape
    top = jnp.maximum(jnp.max(jnp.abs(block), axis=1, keepdims=True), 1e-30)
    power = jnp.ceil(jnp.log(top) * (1.0 / LN2_64)) + 1.0
    fixed = jnp.round(block * (jnp.exp(power * -LN2_64) * 32766.0))
    out[to, 0:cols] = fixed.astype(jnp.int32).astype(jnp.int16)
    wide_power = jnp.broadcast_to(power.astype(jnp.int32), (step, 128))
    out[to, cols : cols + 128] = wide_power.astype(jnp.int16)


def pack_rows(part, start, out):
    step = 16
    for row in range(0, out.shape[0], step):
        pack(part[start + row : start + row + step, :], out, slice(row, row + step))


def unpack(ref, at):
    cols = ref.shape[1] - 128
    power = ref[at, cols : cols + 128].astype(jnp.int32).astype(f32)[:, :1]
    return ref[at, 0:cols].astype(jnp.int32).astype(f32) * (jnp.exp(power * LN2_64) * (1.0 / 32766.0))


def over_columns(cols, tile):
    for start in range(0, cols, 256):
        tile(slice(start, min(start + 256, cols)))


def halves(at, rows):
    return (
        pl.ds(pl.multiple_of(at[1] * rows, 128), rows),
        pl.ds(pl.multiple_of((1 - at[1]) * rows, 128), rows),
    )


def own_kernel(at, block, head, other, own, kept):
    kept[...] = head[...]
    here, there = halves(at, head.shape[0])

    def tile(span):
        own[:, span] = jnp.dot(block[:, here], head[:, span], preferred_element_type=f32) + jnp.dot(
            block[:, there], other[:, span], preferred_element_type=f32
        )

    over_columns(head.shape[1], tile)


def far_kernel(at, block, head, other, low, high, tick, part):
    tokens = block.shape[0]
    rows, cols = head.shape
    here, there = halves(at, rows)

    def tile(span):
        part[:, span] = jnp.dot(block[:, here], head[:, span], preferred_element_type=f32) + jnp.dot(
            block[:, there], other[:, span], preferred_element_type=f32
        )

    over_columns(cols, tile)
    tick[...] = jnp.zeros(tick.shape, f32)
    half = tokens // 2
    pack_rows(part, 0, low)
    pack_rows(part, half, high)


def near_kernel(at, tick, b0, b1, b2, b3, head, other, p1, p3, q1, q3, mine, theirs, part):
    tokens = b0.shape[0]
    half = tokens // 2
    rows, cols = head.shape
    here, there = halves(at, rows)
    for k, block in enumerate((b1, b3, b0, b2)):
        mine[k * tokens : (k + 1) * tokens, :] = block[:, here]
        theirs[k * tokens : (k + 1) * tokens, :] = block[:, there]

    def tile(span):
        both = jnp.dot(mine[0 : 2 * tokens, :], head[:, span], preferred_element_type=f32) + jnp.dot(
            theirs[0 : 2 * tokens, :], other[:, span], preferred_element_type=f32
        )
        p1[:, span] = both[0:half, :]
        part[:, span] = both[half : tokens + half, :]
        p3[:, span] = both[tokens + half :, :]

    over_columns(cols, tile)
    pack_rows(part, 0, q1)
    pack_rows(part, half, q3)


def relay_kernel(p1, p3, low, high, q1, q3, tick):
    step = 16
    tick[...] = jnp.zeros(tick.shape, f32)
    for start in range(0, p1.shape[0], step):
        at = slice(start, start + step)
        pack(p1[at, :] + unpack(low, at), q1, at)
        pack(p3[at, :] + unpack(high, at), q3, at)


def total_kernel(own, q1_low, q1_high, q3_low, q3_high, turned, theirs, logits, sent, stats):
    tokens = own.shape[0]
    step = 16
    lane = lax.broadcasted_iota(jnp.int32, (step, 128), 1)
    for start in range(0, tokens, step):
        at = slice(start, start + step)
        q1, q3 = (q1_low, q3_low) if start < tokens // 2 else (q1_high, q3_high)
        part = slice(start % (tokens // 2), start % (tokens // 2) + step)
        value = own[at, :] + unpack(q1, part) + unpack(q3, part)
        logits[at, :] = value
        high = jnp.max(value, axis=1, keepdims=True)
        shifted = jnp.exp(value - high)
        total = jnp.sum(shifted, axis=1, keepdims=True)
        moment = jnp.sum(shifted * value, axis=1, keepdims=True)
        stats[at, :] = jnp.where(lane == 0, high, jnp.where(lane == 1, total, moment))

    rows = jnp.transpose(stats[...])[0:8, :]
    for i in range(sent.shape[0]):
        sent[i] = rows


def merge_kernel(parts, valid, advantage, sent):
    high = parts[0, 0:1, :]
    for i in range(1, parts.shape[0]):
        high = jnp.maximum(high, parts[i, 0:1, :])
    sums = jnp.zeros((8, 128), f32)
    for i in range(parts.shape[0]):
        sums = sums + jnp.exp(parts[i, 0:1, :] - high) * parts[i]
    row = lax.broadcasted_iota(jnp.int32, (8, 128), 0)
    out = jnp.where(row == 0, high, sums)
    out = jnp.where(row == 3, valid[...].astype(f32), jnp.where(row == 4, advantage[...], out))
    for i in range(sent.shape[0]):
        sent[i] = out


def plan_kernel(start_high, parts, coef_out, normal_out, packed_out, slot_out, flag, rows):
    owners = 8
    ny = parts.shape[0] // owners
    for o in range(owners):
        high = parts[o * ny, 0:1, :]
        for y in range(1, ny):
            high = jnp.maximum(high, parts[o * ny + y, 0:1, :])
        sums = jnp.zeros((8, 128), f32)
        for y in range(ny):
            sums = sums + jnp.exp(parts[o * ny + y, 0:1, :] - high) * parts[o * ny + y]
        row = lax.broadcasted_iota(jnp.int32, (8, 128), 0)
        normal = high + jnp.log(sums[1:2, :])
        entropy = normal - sums[2:3, :] / sums[1:2, :]
        rows[o] = jnp.where(row == 0, normal, jnp.where(row == 1, entropy, parts[o * ny]))
    normal, entropy, valid, advantage = (
        jnp.concatenate([rows[o, k : k + 1, :] for o in range(owners)], axis=0) for k in (0, 1, 3, 4)
    )
    counted = jnp.sum(jnp.sum(valid, axis=1, keepdims=True), axis=0, keepdims=True)
    threshold = bisect(jnp.where(valid > 0.0, entropy, -jnp.inf), counted, start_high)
    gate = valid * jnp.clip((entropy - threshold) / ramp_width + 0.5, 0.0, 1.0)
    coef = -(gate * advantage)
    active = coef != 0.0
    activef = active.astype(f32)
    i = lax.broadcasted_iota(jnp.int32, (128, 128), 0)
    j = lax.broadcasted_iota(jnp.int32, (128, 128), 1)
    ahead = (i < j).astype(f32)
    group = 128 // (32 // owners)
    same = (i // group == j // group).astype(f32)
    rank_owner = jnp.dot(activef, ahead, preferred_element_type=f32)
    rank_group = jnp.dot(activef, ahead * same, preferred_element_type=f32)
    start = (lax.broadcasted_iota(jnp.int32, (8, 128), 1) // group * CAP).astype(f32)
    coef_out[...] = coef
    normal_out[...] = normal
    packed_out[...] = jnp.where(active, rank_owner, -1.0)
    slot_out[...] = jnp.where(active, rank_group + start, -1.0)
    over = jnp.where(active & (rank_owner >= CAP_SMALL), 1.0, 0.0)
    over = jnp.where(active & (rank_group >= CAP), 2.0, over)
    flag[0, 0] = jnp.max(over).astype(jnp.int32)


def as_columns(rows):
    row = lax.broadcasted_iota(jnp.int32, (8, 128), 0)
    out = jnp.zeros((8, 128), f32)
    for k, value in enumerate(rows):
        out = jnp.where(row == k, value, out)
    return jnp.transpose(out)


def one_hot(count, slots):
    row = lax.broadcasted_iota(jnp.int32, (count, 128), 0).astype(f32)
    return (row == slots).astype(f32).astype(bf16)


def slopes_kernel(at, logits, coef_all, normal_all, packed_all, ids, out):
    me = pl.ds(at[2], 1)
    count = out.shape[0]
    columns = as_columns([coef_all[me, :], normal_all[me, :], ids[...].astype(f32)])
    coef, normal, token = columns[:, 0:1], columns[:, 1:2], columns[:, 2:3].astype(jnp.int32) - at[3]
    choose = one_hot(count, packed_all[me, :])
    lane = lax.broadcasted_iota(jnp.int32, (128, 128), 1)
    for k in range(logits.shape[1] // 128):
        span = slice(k * 128, (k + 1) * 128)
        hit = (lane + k * 128 == token).astype(f32)
        slopes = (coef * (hit - jnp.exp(logits[:, span] - normal))).astype(bf16)
        out[:, span] = jnp.dot(choose, slopes, preferred_element_type=f32).astype(bf16)


def owner_of(at, s, k):
    return lax.rem(at[0] - s + NX, NX) * 2 + lax.rem(at[1] + k, 2)


def product_kernel(at, mine, theirs, turned, slopes, o0, o1, o2, o3, held):
    half = mine.shape[0]
    cap = half // NX
    slopes[0:half, :] = mine[...]
    slopes[half:, :] = theirs[...]
    held[...] = jnp.dot(slopes[...], turned[...], preferred_element_type=f32).astype(bf16)
    for step, out in enumerate((o0, o1, o2, o3)):
        source = lax.rem(at[0] - at[5] - step + 2 * NX, NX) * cap
        for k in range(2):
            rows = pl.ds(pl.multiple_of(source + k * half, cap), cap)
            out[k * cap : (k + 1) * cap, :] = held[rows, :]


def outer_kernel(at, packed_all, hid_mine, hid_theirs, slopes, above, after, out, tick, held):
    half = slopes.shape[0] // 2
    cap = half // NX
    tick[...] = jnp.zeros(tick.shape, f32)
    for k, hidden in enumerate((hid_mine, hid_theirs)):
        for s in range(NX):
            choose = one_hot(cap, packed_all[pl.ds(owner_of(at, s, k), 1), :])
            to = k * half + s * cap
            held[to : to + cap, :] = jnp.dot(
                choose, hidden[ORDER[s] * 128 : (ORDER[s] + 1) * 128, :], preferred_element_type=f32
            ).astype(bf16)
    out[...] = lax.dot_general(
        held[...], slopes[...], (((0,), (0,)), ((), ())), preferred_element_type=f32
    )


def outer(at, packed_all, hid_mine, hid_theirs, slopes, first, count, above, after):
    (tokens, rows), (depth, cols) = hid_mine.shape, slopes.shape
    tile = 128
    whole_block = lambda i: (0, 0)
    in_specs = [
        pl.BlockSpec(memory_space=pltpu.SMEM),
        pl.BlockSpec(packed_all.shape, whole_block),
        pl.BlockSpec((tokens, tile), lambda i: (0, i + first)),
        pl.BlockSpec((tokens, tile), lambda i: (0, i + first)),
        pl.BlockSpec((depth, cols), whole_block),
        pl.BlockSpec(memory_space=pl.ANY),
        pl.BlockSpec(memory_space=pl.ANY),
    ]
    aliases = {5: 0} if above.shape == (rows, cols) else {}
    return pl.pallas_call(
        outer_kernel,
        grid=(count,),
        in_specs=in_specs,
        out_specs=[pl.BlockSpec((tile, cols), lambda i: (i + first, 0)), pl.BlockSpec((8, 128), whole_block)],
        out_shape=[struct((rows, cols), f32), struct((8, 128), f32)],
        scratch_shapes=[pltpu.VMEM((depth, tile), bf16)],
        input_output_aliases=aliases,
        compiler_params=pltpu.CompilerParams(vmem_limit_bytes=24 << 20),
        cost_estimate=estimate(count * tile, depth, cols),
    )(at, packed_all, hid_mine, hid_theirs, slopes, above, after)


def spread_kernel(at, before, r0, r1, r2, r3, packed_all, slot_all, out, tick):
    size = out.shape[0]
    cap = r0.shape[0] // 2
    tick[...] = jnp.zeros(tick.shape, f32)
    spread = []
    for k in range(2):
        core = lax.rem(at[1] + k, 2)
        me = pl.ds(at[5] * 2 + core, 1)
        slot = slot_all[me, :]
        slot = jnp.where(slot >= 0.0, slot + (core * (size // 2)).astype(f32), -1.0)
        part = lax.dot_general(
            one_hot(size, slot),
            one_hot(cap, packed_all[me, :]),
            (((1,), (1,)), ((), ())),
            preferred_element_type=f32,
        )
        spread.append(part.astype(bf16))
    spread = jnp.concatenate(spread, axis=1)
    total = jnp.zeros(out.shape, f32)
    for r in (r0, r1, r2, r3):
        total = total + jnp.dot(spread, r[...], preferred_element_type=f32)
    out[...] = total


def sum_kernel(at, parts, slot_all, out, ranks):
    total = parts[0:CAP, :]
    for i in range(1, parts.shape[0] // CAP):
        total = total + parts[i * CAP : (i + 1) * CAP, :]
    group = out.shape[0]
    per_owner = 128 // group
    owner, place = at[4] // per_owner, lax.rem(at[4], per_owner)
    ranks[...] = as_columns([slot_all[pl.ds(owner, 1), :]])
    rank = ranks[pl.ds(pl.multiple_of(place * group, group), group), :][:, 0:1]
    rank = rank - (place * CAP).astype(f32)
    rows = jnp.zeros(out.shape, f32)
    for r in range(CAP):
        rows = rows + jnp.where(rank == float(r), total[r : r + 1, :], 0.0)
    out[...] = rows


def shards(hidden_states, head, token_ids, valid, advantage):
    tokens, width = hidden_states.shape
    rows, voc_cols = head.shape
    nx, n_voc, n_dp = lax.axis_size("x"), lax.axis_size(VOC), lax.axis_size(DP)
    x, c, block = lax.axis_index("x"), lax.axis_index("c"), lax.axis_index(VOC)
    at = jnp.stack([x, c, x * 2 + c, block * voc_cols, block, lax.axis_index("y")]).astype(jnp.int32)
    chip_rows = width // nx

    head_other = lax.ppermute(head, "c", SWAP)

    block_shape = struct((tokens, chip_rows), bf16)
    b0, *leave = call(split_kernel, [block_shape] * 4, [at, hidden_states], smem=1)
    came = {s: lax.ppermute(leave[s - 1], "x", ring(nx, s)) for s in (2, 1, 3)}
    partial = struct((tokens, voc_cols), f32)
    tick_shape = struct((8, 128), f32)
    own, kept = call(
        own_kernel,
        [partial, struct((rows, voc_cols), bf16)],
        [at, b0, head, head_other],
        smem=1,
        cost_estimate=estimate(tokens, chip_rows, voc_cols),
    )
    half = struct((tokens // 2, voc_cols + 128), jnp.int16)
    low, high, tick = call(
        far_kernel,
        [half, half, tick_shape],
        [at, came[2], kept, head_other],
        [pltpu.VMEM((tokens, voc_cols), f32)],
        smem=1,
        cost_estimate=estimate(tokens, chip_rows, voc_cols),
    )
    low, high = lax.ppermute(low, "x", ring(nx, -1)), lax.ppermute(high, "x", ring(nx, 1))
    half_partial = struct((tokens // 2, voc_cols), f32)
    p1, p3, q1_high, q3_low, hid_mine, hid_send = call(
        near_kernel,
        [half_partial] * 2 + [half] * 2 + [struct((nx * tokens, rows), bf16)] * 2,
        [at, tick, b0, came[1], came[2], came[3], kept, head_other],
        [pltpu.VMEM((tokens, voc_cols), f32)],
        vmem=24,
        smem=1,
        cost_estimate=estimate(2 * tokens, chip_rows, voc_cols),
    )
    q1_high, q3_low = lax.ppermute(q1_high, "x", ring(nx, -1)), lax.ppermute(q3_low, "x", ring(nx, 1))
    q1_low, q3_high, tick = call(relay_kernel, [half] * 2 + [tick_shape], [p1, p3, low, high])
    q1_low, q3_high = lax.ppermute(q1_low, "x", ring(nx, -1)), lax.ppermute(q3_high, "x", ring(nx, 1))
    turned = call(turn_kernel, struct((voc_cols, rows), bf16), [tick, kept])
    hid_theirs = lax.ppermute(hid_send, "c", SWAP)
    logits, stats = call(
        total_kernel,
        [partial, struct((lax.axis_size("z"), 8, 128), f32)],
        [own, q1_low, q1_high, q3_low, q3_high, turned, hid_theirs],
        [pltpu.VMEM((tokens, 128), f32)],
        loose=2,
    )

    stats = lax.all_to_all(stats, "z", 0, 0, tiled=True)
    everyone = DP + ("y",)
    stats = call(
        merge_kernel,
        struct((lax.axis_size(everyone), 8, 128), f32),
        [stats, valid.reshape(1, tokens), advantage.reshape(1, tokens)],
    )
    stats = lax.all_to_all(stats, everyone, 0, 0, tiled=True)
    start_high = float(np.float32(np.log(np.float32(voc_cols * n_voc))) + np.float32(1.0))
    table = struct((n_dp, tokens), f32)
    coef_all, normal_all, packed_all, slot_all, flag = call(
        functools.partial(plan_kernel, start_high),
        [table] * 4 + [struct((1, 1), jnp.int32)],
        [stats],
        [pltpu.VMEM((n_dp, 8, 128), f32)],
        out_specs=[pl.BlockSpec(memory_space=pltpu.VMEM)] * 4 + [pl.BlockSpec(memory_space=pltpu.SMEM)],
    )

    def backward(cap):
        piece = call(
            slopes_kernel,
            struct((cap, voc_cols), bf16),
            [at, logits, coef_all, normal_all, packed_all, token_ids.reshape(1, tokens)],
            smem=1,
        )
        pieces = {s: lax.ppermute(piece, "x", ring(nx, s)) for s in (2, 1, 3)}
        mine = jnp.concatenate([piece, pieces[1], pieces[2], pieces[3]], axis=0)
        theirs = lax.ppermute(mine, "c", SWAP)
        return call(
            product_kernel,
            [struct((2 * nx * cap, voc_cols), bf16)] + [struct((2 * cap, rows), bf16)] * nx,
            [at, mine, theirs, turned],
            [pltpu.VMEM((2 * nx * cap, rows), bf16)],
            smem=1,
        )

    def finish(slopes, *parts):
        parts = [parts[0]] + [lax.ppermute(parts[k], "y", ring(nx, k)) for k in range(1, nx)]
        sides = (at, packed_all, hid_mine, hid_theirs, slopes)
        blocks = rows // 128
        early = (blocks + 1) // 2
        head_grad, tick = outer(*sides, 0, early, packed_all, packed_all)
        spread, tick = call(
            spread_kernel,
            [struct((n_voc * CAP // nx, rows), f32), tick_shape],
            [at, tick, *parts, packed_all, slot_all],
            smem=1,
        )
        spread = lax.all_to_all(spread, "z", 0, 0, tiled=True)
        head_grad, _ = outer(*sides, early, blocks - early, head_grad, tick)
        hidden_grad = call(
            sum_kernel,
            struct((tokens * n_dp // n_voc, rows), f32),
            [at, spread, slot_all],
            [pltpu.VMEM((tokens, 8), f32)],
            smem=1,
        )
        return hidden_grad, head_grad

    def whole(_):
        return dense(hidden_states, head, token_ids, valid, advantage)

    packed_rows = backward(CAP_SMALL)

    def small(_):
        return finish(*packed_rows)

    def large(_):
        return finish(*backward(CAP * n_voc // n_dp))

    return lax.switch(flag[0, 0], [small, large, whole], 0)


def solution(mesh):
    chips = Mesh(mesh.devices.reshape(4, 2, 4, 8), DP + VOC)
    placed = (P(DP, None), P(DP, VOC), P(DP), P(DP), P(DP))
    return jax.shard_map(
        shards,
        mesh=chips,
        in_specs=placed,
        out_specs=(P(VOC, DP), P(DP, VOC)),
        check_vma=False,
    )
```

```python
import functools

import jax
import jax.numpy as jnp
import numpy as np
from jax import lax
from jax.experimental import pallas as pl
from jax.experimental.pallas import tpu as pltpu
from jax.sharding import Mesh, PartitionSpec as P

ROUNDS = 24
LEVELS = 6
CAP = 16
CAP_SMALL = 32
ORDER = (2, 0, 3, 1)
NX = 4

ramp_width = 0.5
DP = ("x", "c")
VOC = ("y", "z")
f32 = jnp.float32
bf16 = jnp.bfloat16


def ring(n, shift):
    return [(i, (i + shift) % n) for i in range(n)]


SWAP = [(0, 1), (1, 0)]


def dense(hidden_states, head, token_ids, valid, advantage):
    voc_cols = head.shape[1]
    columns = lax.all_to_all(hidden_states, DP, split_axis=1, concat_axis=0, tiled=True)
    logits = lax.psum_scatter(
        jnp.dot(columns, head, preferred_element_type=f32), DP, scatter_dimension=0, tiled=True
    )
    offset = lax.axis_index(VOC) * voc_cols
    hit = jnp.arange(voc_cols, dtype=jnp.int32)[None, :] + offset == token_ids[:, None]
    highest = lax.pmax(jnp.max(logits, axis=1), VOC)
    shifted = jnp.exp(logits - highest[:, None])
    total, moment = lax.psum((jnp.sum(shifted, axis=1), jnp.sum(shifted * logits, axis=1)), VOC)
    normal = highest + jnp.log(total)
    entropy = normal - moment / total
    validf = valid.astype(f32)
    start_high = jnp.log(f32(voc_cols * lax.axis_size(VOC))) + 1.0
    counted = lax.psum(jnp.sum(validf), DP)
    quota = jnp.floor((counted + 0.5) * 0.2)

    def round_step(step, bounds):
        low, high = bounds
        middle = (low + high) * 0.5
        above = lax.psum(jnp.sum(jnp.where(entropy > middle, validf, 0.0)), DP)
        more = above > quota
        return (jnp.where(more, middle, low), jnp.where(more, high, middle))

    _, threshold = lax.fori_loop(0, ROUNDS, round_step, (f32(0.0), start_high))
    gate = validf * jnp.clip((entropy - threshold) / ramp_width + 0.5, 0.0, 1.0)
    coef = -(gate * advantage)
    probs = jnp.exp(logits - normal[:, None])
    slopes = (coef[:, None] * (hit.astype(f32) - probs)).astype(bf16)
    piece = lax.all_gather(slopes, DP, axis=0, tiled=True)
    head_grad = lax.dot_general(columns, piece, (((0,), (0,)), ((), ())), preferred_element_type=f32)
    product = lax.dot_general(piece, head, (((1,), (1,)), ((), ())), preferred_element_type=f32)
    return lax.psum_scatter(product, VOC, scatter_dimension=0, tiled=True), head_grad


def bisect(entropy, counted, start_high):
    columns = jnp.transpose(entropy)
    quota = jnp.floor((counted + 0.5) * 0.2)
    lane = lax.broadcasted_iota(jnp.int32, (1, 128), 1)
    leaves = 1 << LEVELS
    low = jnp.zeros((1, 128), f32)
    high = jnp.full((1, 128), start_high, f32)
    for _ in range(ROUNDS // LEVELS):
        for level in range(LEVELS):
            middle = (low + high) * 0.5
            bit = ((lane >> (LEVELS - 1 - level)) & 1) == 1
            low, high = jnp.where(bit, middle, low), jnp.where(bit, high, middle)
        above = jnp.zeros((128, 128), f32)
        for i in range(8):
            above = above + jnp.where(columns[:, i : i + 1] > low, 1.0, 0.0)
        above = jnp.sum(above, axis=0, keepdims=True)
        more = jnp.where(((above > quota) | (lane == 0)) & (lane < leaves), 1.0, 0.0)
        here = lane == jnp.sum(more, axis=1, keepdims=True).astype(jnp.int32) - 1
        low, high = (
            jnp.broadcast_to(jnp.sum(jnp.where(here, v, 0.0), axis=1, keepdims=True), (1, 128))
            for v in (low, high)
        )
    return high[:, :1]


def call(kernel, out, args, scratch=(), vmem=16, smem=0, loose=0, **kw):
    specs = [pl.BlockSpec(memory_space=pltpu.SMEM)] * smem
    specs += [pl.BlockSpec(memory_space=pltpu.VMEM)] * (len(args) - smem - loose)
    specs += [pl.BlockSpec(memory_space=pl.ANY)] * loose
    return pl.pallas_call(
        kernel,
        in_specs=specs,
        out_shape=out,
        scratch_shapes=list(scratch),
        compiler_params=pltpu.CompilerParams(vmem_limit_bytes=vmem << 20),
        **kw,
    )(*args)


def struct(shape, dtype):
    return jax.ShapeDtypeStruct(shape, dtype)


def estimate(m, k, n):
    return pl.CostEstimate(flops=2 * m * k * n, bytes_accessed=2 * k * n, transcendentals=0)


LN2_64 = float(np.log(2.0) / 64.0)


def split_kernel(at, hidden, b0, b1, b2, b3, sems):
    chip_rows = b0.shape[1]
    copies = []
    for s, out in enumerate((b0, b1, b2, b3)):
        to = lax.rem(at[0] + s, NX) * chip_rows
        block = hidden.at[:, pl.ds(pl.multiple_of(to, 128), chip_rows)]
        copies.append(pltpu.make_async_copy(block, out, sems.at[s]))
    for copy in copies:
        copy.start()
    for copy in copies:
        copy.wait()


def turn_kernel(tick, head, turned):
    for k in range(head.shape[1] // 128):
        span = slice(k * 128, (k + 1) * 128)
        turned[span, :] = jnp.transpose(head[:, span])


def pack(block, out, to):
    step, cols = block.shape
    top = jnp.maximum(jnp.max(jnp.abs(block), axis=1, keepdims=True), 1e-30)
    power = jnp.ceil(jnp.log(top) * (1.0 / LN2_64)) + 1.0
    fixed = jnp.round(block * (jnp.exp(power * -LN2_64) * 32766.0))
    out[to, 0:cols] = fixed.astype(jnp.int32).astype(jnp.int16)
    wide_power = jnp.broadcast_to(power.astype(jnp.int32), (step, 128))
    out[to, cols : cols + 128] = wide_power.astype(jnp.int16)


def pack_rows(part, start, out):
    step = 16
    for row in range(0, out.shape[0], step):
        pack(part[start + row : start + row + step, :], out, slice(row, row + step))


def unpack(ref, at):
    cols = ref.shape[1] - 128
    power = ref[at, cols : cols + 128].astype(jnp.int32).astype(f32)[:, :1]
    return ref[at, 0:cols].astype(jnp.int32).astype(f32) * (jnp.exp(power * LN2_64) * (1.0 / 32766.0))


def over_columns(cols, tile):
    for start in range(0, cols, 256):
        tile(slice(start, min(start + 256, cols)))


def halves(at, rows):
    return (
        pl.ds(pl.multiple_of(at[1] * rows, 128), rows),
        pl.ds(pl.multiple_of((1 - at[1]) * rows, 128), rows),
    )


def own_kernel(at, block, head, other, own, kept):
    kept[...] = head[...]
    here, there = halves(at, head.shape[0])

    def tile(span):
        own[:, span] = jnp.dot(block[:, here], head[:, span], preferred_element_type=f32) + jnp.dot(
            block[:, there], other[:, span], preferred_element_type=f32
        )

    over_columns(head.shape[1], tile)


def far_kernel(at, block, head, other, low, high, tick, part):
    tokens = block.shape[0]
    rows, cols = head.shape
    here, there = halves(at, rows)

    def tile(span):
        part[:, span] = jnp.dot(block[:, here], head[:, span], preferred_element_type=f32) + jnp.dot(
            block[:, there], other[:, span], preferred_element_type=f32
        )

    over_columns(cols, tile)
    tick[...] = jnp.zeros(tick.shape, f32)
    half = tokens // 2
    pack_rows(part, 0, low)
    pack_rows(part, half, high)


def near_kernel(at, tick, b0, b1, b2, b3, head, other, p1, p3, q1, q3, mine, theirs, part):
    tokens = b0.shape[0]
    half = tokens // 2
    rows, cols = head.shape
    here, there = halves(at, rows)
    for k, block in enumerate((b1, b3, b0, b2)):
        mine[k * tokens : (k + 1) * tokens, :] = block[:, here]
        theirs[k * tokens : (k + 1) * tokens, :] = block[:, there]

    def tile(span):
        both = jnp.dot(mine[0 : 2 * tokens, :], head[:, span], preferred_element_type=f32) + jnp.dot(
            theirs[0 : 2 * tokens, :], other[:, span], preferred_element_type=f32
        )
        p1[:, span] = both[0:half, :]
        part[:, span] = both[half : tokens + half, :]
        p3[:, span] = both[tokens + half :, :]

    over_columns(cols, tile)
    pack_rows(part, 0, q1)
    pack_rows(part, half, q3)


def relay_kernel(p1, p3, low, high, q1, q3, tick):
    step = 16
    tick[...] = jnp.zeros(tick.shape, f32)
    for start in range(0, p1.shape[0], step):
        at = slice(start, start + step)
        pack(p1[at, :] + unpack(low, at), q1, at)
        pack(p3[at, :] + unpack(high, at), q3, at)


def total_kernel(own, q1_low, q1_high, q3_low, q3_high, turned, theirs, logits, sent, stats):
    tokens = own.shape[0]
    step = 16
    lane = lax.broadcasted_iota(jnp.int32, (step, 128), 1)
    for start in range(0, tokens, step):
        at = slice(start, start + step)
        q1, q3 = (q1_low, q3_low) if start < tokens // 2 else (q1_high, q3_high)
        part = slice(start % (tokens // 2), start % (tokens // 2) + step)
        value = own[at, :] + unpack(q1, part) + unpack(q3, part)
        logits[at, :] = value
        high = jnp.max(value, axis=1, keepdims=True)
        shifted = jnp.exp(value - high)
        total = jnp.sum(shifted, axis=1, keepdims=True)
        moment = jnp.sum(shifted * value, axis=1, keepdims=True)
        stats[at, :] = jnp.where(lane == 0, high, jnp.where(lane == 1, total, moment))

    rows = jnp.transpose(stats[...])[0:8, :]
    for i in range(sent.shape[0]):
        sent[i] = rows


def merge_kernel(parts, valid, advantage, sent):
    high = parts[0, 0:1, :]
    for i in range(1, parts.shape[0]):
        high = jnp.maximum(high, parts[i, 0:1, :])
    sums = jnp.zeros((8, 128), f32)
    for i in range(parts.shape[0]):
        sums = sums + jnp.exp(parts[i, 0:1, :] - high) * parts[i]
    row = lax.broadcasted_iota(jnp.int32, (8, 128), 0)
    out = jnp.where(row == 0, high, sums)
    out = jnp.where(row == 3, valid[...].astype(f32), jnp.where(row == 4, advantage[...], out))
    for i in range(sent.shape[0]):
        sent[i] = out


def plan_kernel(start_high, parts, coef_out, normal_out, packed_out, slot_out, flag, rows):
    owners = 8
    ny = parts.shape[0] // owners
    for o in range(owners):
        high = parts[o * ny, 0:1, :]
        for y in range(1, ny):
            high = jnp.maximum(high, parts[o * ny + y, 0:1, :])
        sums = jnp.zeros((8, 128), f32)
        for y in range(ny):
            sums = sums + jnp.exp(parts[o * ny + y, 0:1, :] - high) * parts[o * ny + y]
        row = lax.broadcasted_iota(jnp.int32, (8, 128), 0)
        normal = high + jnp.log(sums[1:2, :])
        entropy = normal - sums[2:3, :] / sums[1:2, :]
        rows[o] = jnp.where(row == 0, normal, jnp.where(row == 1, entropy, parts[o * ny]))
    normal, entropy, valid, advantage = (
        jnp.concatenate([rows[o, k : k + 1, :] for o in range(owners)], axis=0) for k in (0, 1, 3, 4)
    )
    counted = jnp.sum(jnp.sum(valid, axis=1, keepdims=True), axis=0, keepdims=True)
    threshold = bisect(jnp.where(valid > 0.0, entropy, -jnp.inf), counted, start_high)
    gate = valid * jnp.clip((entropy - threshold) / ramp_width + 0.5, 0.0, 1.0)
    coef = -(gate * advantage)
    active = coef != 0.0
    activef = active.astype(f32)
    i = lax.broadcasted_iota(jnp.int32, (128, 128), 0)
    j = lax.broadcasted_iota(jnp.int32, (128, 128), 1)
    ahead = (i < j).astype(f32)
    group = 128 // (32 // owners)
    same = (i // group == j // group).astype(f32)
    rank_owner = jnp.dot(activef, ahead, preferred_element_type=f32)
    rank_group = jnp.dot(activef, ahead * same, preferred_element_type=f32)
    start = (lax.broadcasted_iota(jnp.int32, (8, 128), 1) // group * CAP).astype(f32)
    coef_out[...] = coef
    normal_out[...] = normal
    packed_out[...] = jnp.where(active, rank_owner, -1.0)
    slot_out[...] = jnp.where(active, rank_group + start, -1.0)
    over = jnp.where(active & (rank_owner >= CAP_SMALL), 1.0, 0.0)
    over = jnp.where(active & (rank_group >= CAP), 2.0, over)
    flag[0, 0] = jnp.max(over).astype(jnp.int32)


def as_columns(rows):
    row = lax.broadcasted_iota(jnp.int32, (8, 128), 0)
    out = jnp.zeros((8, 128), f32)
    for k, value in enumerate(rows):
        out = jnp.where(row == k, value, out)
    return jnp.transpose(out)


def one_hot(count, slots):
    row = lax.broadcasted_iota(jnp.int32, (count, 128), 0).astype(f32)
    return (row == slots).astype(f32).astype(bf16)


def slopes_kernel(at, logits, coef_all, normal_all, packed_all, ids, out):
    me = pl.ds(at[2], 1)
    count = out.shape[0]
    columns = as_columns([coef_all[me, :], normal_all[me, :], ids[...].astype(f32)])
    coef, normal, token = columns[:, 0:1], columns[:, 1:2], columns[:, 2:3].astype(jnp.int32) - at[3]
    choose = one_hot(count, packed_all[me, :])
    lane = lax.broadcasted_iota(jnp.int32, (128, 128), 1)
    for k in range(logits.shape[1] // 128):
        span = slice(k * 128, (k + 1) * 128)
        hit = (lane + k * 128 == token).astype(f32)
        slopes = (coef * (hit - jnp.exp(logits[:, span] - normal))).astype(bf16)
        out[:, span] = jnp.dot(choose, slopes, preferred_element_type=f32).astype(bf16)


def owner_of(at, s, k):
    return lax.rem(at[0] - s + NX, NX) * 2 + lax.rem(at[1] + k, 2)


def product_kernel(at, mine, theirs, turned, slopes, o0, o1, o2, o3, held):
    half = mine.shape[0]
    cap = half // NX
    slopes[0:half, :] = mine[...]
    slopes[half:, :] = theirs[...]
    held[...] = jnp.dot(slopes[...], turned[...], preferred_element_type=f32).astype(bf16)
    for step, out in enumerate((o0, o1, o2, o3)):
        source = lax.rem(at[0] - at[5] - step + 2 * NX, NX) * cap
        for k in range(2):
            rows = pl.ds(pl.multiple_of(source + k * half, cap), cap)
            out[k * cap : (k + 1) * cap, :] = held[rows, :]


def outer_kernel(at, packed_all, hid_mine, hid_theirs, slopes, above, after, out, tick, held):
    half = slopes.shape[0] // 2
    cap = half // NX
    tick[...] = jnp.zeros(tick.shape, f32)
    for k, hidden in enumerate((hid_mine, hid_theirs)):
        for s in range(NX):
            choose = one_hot(cap, packed_all[pl.ds(owner_of(at, s, k), 1), :])
            to = k * half + s * cap
            held[to : to + cap, :] = jnp.dot(
                choose, hidden[ORDER[s] * 128 : (ORDER[s] + 1) * 128, :], preferred_element_type=f32
            ).astype(bf16)
    out[...] = lax.dot_general(
        held[...], slopes[...], (((0,), (0,)), ((), ())), preferred_element_type=f32
    )


def outer(at, packed_all, hid_mine, hid_theirs, slopes, first, count, above, after):
    (tokens, rows), (depth, cols) = hid_mine.shape, slopes.shape
    tile = 128
    whole_block = lambda i: (0, 0)
    in_specs = [
        pl.BlockSpec(memory_space=pltpu.SMEM),
        pl.BlockSpec(packed_all.shape, whole_block),
        pl.BlockSpec((tokens, tile), lambda i: (0, i + first)),
        pl.BlockSpec((tokens, tile), lambda i: (0, i + first)),
        pl.BlockSpec((depth, cols), whole_block),
        pl.BlockSpec(memory_space=pl.ANY),
        pl.BlockSpec(memory_space=pl.ANY),
    ]
    aliases = {5: 0} if above.shape == (rows, cols) else {}
    return pl.pallas_call(
        outer_kernel,
        grid=(count,),
        in_specs=in_specs,
        out_specs=[pl.BlockSpec((tile, cols), lambda i: (i + first, 0)), pl.BlockSpec((8, 128), whole_block)],
        out_shape=[struct((rows, cols), f32), struct((8, 128), f32)],
        scratch_shapes=[pltpu.VMEM((depth, tile), bf16)],
        input_output_aliases=aliases,
        compiler_params=pltpu.CompilerParams(vmem_limit_bytes=24 << 20),
        cost_estimate=estimate(count * tile, depth, cols),
    )(at, packed_all, hid_mine, hid_theirs, slopes, above, after)


def spread_kernel(at, before, r0, r1, r2, r3, packed_all, slot_all, out, tick):
    size = out.shape[0]
    cap = r0.shape[0] // 2
    tick[...] = jnp.zeros(tick.shape, f32)
    spread = []
    for k in range(2):
        core = lax.rem(at[1] + k, 2)
        me = pl.ds(at[5] * 2 + core, 1)
        slot = slot_all[me, :]
        slot = jnp.where(slot >= 0.0, slot + (core * (size // 2)).astype(f32), -1.0)
        part = lax.dot_general(
            one_hot(size, slot),
            one_hot(cap, packed_all[me, :]),
            (((1,), (1,)), ((), ())),
            preferred_element_type=f32,
        )
        spread.append(part.astype(bf16))
    spread = jnp.concatenate(spread, axis=1)
    total = jnp.zeros((size, r0.shape[1]), f32)
    for r in (r0, r1, r2, r3):
        total = total + jnp.dot(spread, r[...], preferred_element_type=f32)
    pack(total, out, slice(0, size))


def sum_kernel(at, parts, slot_all, out, ranks):
    total = unpack(parts, slice(0, CAP))
    for i in range(1, parts.shape[0] // CAP):
        total = total + unpack(parts, slice(i * CAP, (i + 1) * CAP))
    group = out.shape[0]
    per_owner = 128 // group
    owner, place = at[4] // per_owner, lax.rem(at[4], per_owner)
    ranks[...] = as_columns([slot_all[pl.ds(owner, 1), :]])
    rank = ranks[pl.ds(pl.multiple_of(place * group, group), group), :][:, 0:1]
    rank = rank - (place * CAP).astype(f32)
    rows = jnp.zeros(out.shape, f32)
    for r in range(CAP):
        rows = rows + jnp.where(rank == float(r), total[r : r + 1, :], 0.0)
    out[...] = rows


def shards(hidden_states, head, token_ids, valid, advantage):
    tokens, width = hidden_states.shape
    rows, voc_cols = head.shape
    nx, n_voc, n_dp = lax.axis_size("x"), lax.axis_size(VOC), lax.axis_size(DP)
    x, c, block = lax.axis_index("x"), lax.axis_index("c"), lax.axis_index(VOC)
    at = jnp.stack([x, c, x * 2 + c, block * voc_cols, block, lax.axis_index("y")]).astype(jnp.int32)
    chip_rows = width // nx

    head_other = lax.ppermute(head, "c", SWAP)

    block_shape = struct((tokens, chip_rows), bf16)
    b0, *leave = call(
        split_kernel,
        [block_shape] * 4,
        [at, hidden_states],
        [pltpu.SemaphoreType.DMA((nx,))],
        smem=1,
        loose=1,
        out_specs=[pl.BlockSpec(memory_space=pltpu.VMEM)] * 4,
    )
    came = {s: lax.ppermute(leave[s - 1], "x", ring(nx, s)) for s in (2, 1, 3)}
    partial = struct((tokens, voc_cols), f32)
    tick_shape = struct((8, 128), f32)
    own, kept = call(
        own_kernel,
        [partial, struct((rows, voc_cols), bf16)],
        [at, b0, head, head_other],
        smem=1,
        cost_estimate=estimate(tokens, chip_rows, voc_cols),
    )
    half = struct((tokens // 2, voc_cols + 128), jnp.int16)
    low, high, tick = call(
        far_kernel,
        [half, half, tick_shape],
        [at, came[2], kept, head_other],
        [pltpu.VMEM((tokens, voc_cols), f32)],
        smem=1,
        cost_estimate=estimate(tokens, chip_rows, voc_cols),
    )
    low, high = lax.ppermute(low, "x", ring(nx, -1)), lax.ppermute(high, "x", ring(nx, 1))
    half_partial = struct((tokens // 2, voc_cols), f32)
    p1, p3, q1_high, q3_low, hid_mine, hid_send = call(
        near_kernel,
        [half_partial] * 2 + [half] * 2 + [struct((nx * tokens, rows), bf16)] * 2,
        [at, tick, b0, came[1], came[2], came[3], kept, head_other],
        [pltpu.VMEM((tokens, voc_cols), f32)],
        vmem=24,
        smem=1,
        cost_estimate=estimate(2 * tokens, chip_rows, voc_cols),
    )
    q1_high, q3_low = lax.ppermute(q1_high, "x", ring(nx, -1)), lax.ppermute(q3_low, "x", ring(nx, 1))
    q1_low, q3_high, tick = call(relay_kernel, [half] * 2 + [tick_shape], [p1, p3, low, high])
    q1_low, q3_high = lax.ppermute(q1_low, "x", ring(nx, -1)), lax.ppermute(q3_high, "x", ring(nx, 1))
    turned = call(turn_kernel, struct((voc_cols, rows), bf16), [tick, kept])
    hid_theirs = lax.ppermute(hid_send, "c", SWAP)
    logits, stats = call(
        total_kernel,
        [partial, struct((lax.axis_size("z"), 8, 128), f32)],
        [own, q1_low, q1_high, q3_low, q3_high, turned, hid_theirs],
        [pltpu.VMEM((tokens, 128), f32)],
        loose=2,
    )

    stats = lax.all_to_all(stats, "z", 0, 0, tiled=True)
    everyone = DP + ("y",)
    stats = call(
        merge_kernel,
        struct((lax.axis_size(everyone), 8, 128), f32),
        [stats, valid.reshape(1, tokens), advantage.reshape(1, tokens)],
    )
    stats = lax.all_to_all(stats, everyone, 0, 0, tiled=True)
    start_high = float(np.float32(np.log(np.float32(voc_cols * n_voc))) + np.float32(1.0))
    table = struct((n_dp, tokens), f32)
    coef_all, normal_all, packed_all, slot_all, flag = call(
        functools.partial(plan_kernel, start_high),
        [table] * 4 + [struct((1, 1), jnp.int32)],
        [stats],
        [pltpu.VMEM((n_dp, 8, 128), f32)],
        out_specs=[pl.BlockSpec(memory_space=pltpu.VMEM)] * 4 + [pl.BlockSpec(memory_space=pltpu.SMEM)],
    )

    def backward(cap):
        piece = call(
            slopes_kernel,
            struct((cap, voc_cols), bf16),
            [at, logits, coef_all, normal_all, packed_all, token_ids.reshape(1, tokens)],
            smem=1,
        )
        pieces = {s: lax.ppermute(piece, "x", ring(nx, s)) for s in (2, 1, 3)}
        mine = jnp.concatenate([piece, pieces[1], pieces[2], pieces[3]], axis=0)
        theirs = lax.ppermute(mine, "c", SWAP)
        return call(
            product_kernel,
            [struct((2 * nx * cap, voc_cols), bf16)] + [struct((2 * cap, rows), bf16)] * nx,
            [at, mine, theirs, turned],
            [pltpu.VMEM((2 * nx * cap, rows), bf16)],
            smem=1,
        )

    def finish(slopes, *parts):
        parts = [parts[0]] + [lax.ppermute(parts[k], "y", ring(nx, k)) for k in range(1, nx)]
        sides = (at, packed_all, hid_mine, hid_theirs, slopes)
        blocks = rows // 128
        early = (blocks + 1) // 2
        head_grad, tick = outer(*sides, 0, early, packed_all, packed_all)
        spread, tick = call(
            spread_kernel,
            [struct((n_voc * CAP // nx, rows + 128), jnp.int16), tick_shape],
            [at, tick, *parts, packed_all, slot_all],
            smem=1,
        )
        spread = lax.all_to_all(spread, "z", 0, 0, tiled=True)
        head_grad, _ = outer(*sides, early, blocks - early, head_grad, tick)
        hidden_grad = call(
            sum_kernel,
            struct((tokens * n_dp // n_voc, rows), f32),
            [at, spread, slot_all],
            [pltpu.VMEM((tokens, 8), f32)],
            smem=1,
        )
        return hidden_grad, head_grad

    def whole(_):
        return dense(hidden_states, head, token_ids, valid, advantage)

    packed_rows = backward(CAP_SMALL)

    def small(_):
        return finish(*packed_rows)

    def large(_):
        return finish(*backward(CAP * n_voc // n_dp))

    return lax.switch(flag[0, 0], [small, large, whole], 0)


def solution(mesh):
    chips = Mesh(mesh.devices.reshape(4, 2, 4, 8), DP + VOC)
    placed = (P(DP, None), P(DP, VOC), P(DP), P(DP), P(DP))
    return jax.shard_map(
        shards,
        mesh=chips,
        in_specs=placed,
        out_specs=(P(VOC, DP), P(DP, VOC)),
        check_vma=False,
    )
```

```python
import functools

import jax
import jax.numpy as jnp
import numpy as np
from jax import lax
from jax.experimental import pallas as pl
from jax.experimental.pallas import tpu as pltpu
from jax.sharding import Mesh, PartitionSpec as P

ROUNDS = 24
LEVELS = 6
CAP = 16
CAP_SMALL = 32
VALID = 112
LOW = 64
ORDER = (2, 0, 3, 1)
NX = 4

ramp_width = 0.5
DP = ("x", "c")
VOC = ("y", "z")
f32 = jnp.float32
bf16 = jnp.bfloat16


def ring(n, shift):
    return [(i, (i + shift) % n) for i in range(n)]


SWAP = [(0, 1), (1, 0)]


def dense(hidden_states, head, token_ids, valid, advantage):
    voc_cols = head.shape[1]
    columns = lax.all_to_all(hidden_states, DP, split_axis=1, concat_axis=0, tiled=True)
    logits = lax.psum_scatter(
        jnp.dot(columns, head, preferred_element_type=f32), DP, scatter_dimension=0, tiled=True
    )
    offset = lax.axis_index(VOC) * voc_cols
    hit = jnp.arange(voc_cols, dtype=jnp.int32)[None, :] + offset == token_ids[:, None]
    highest = lax.pmax(jnp.max(logits, axis=1), VOC)
    shifted = jnp.exp(logits - highest[:, None])
    total, moment = lax.psum((jnp.sum(shifted, axis=1), jnp.sum(shifted * logits, axis=1)), VOC)
    normal = highest + jnp.log(total)
    entropy = normal - moment / total
    validf = valid.astype(f32)
    start_high = jnp.log(f32(voc_cols * lax.axis_size(VOC))) + 1.0
    counted = lax.psum(jnp.sum(validf), DP)
    quota = jnp.floor((counted + 0.5) * 0.2)

    def round_step(step, bounds):
        low, high = bounds
        middle = (low + high) * 0.5
        above = lax.psum(jnp.sum(jnp.where(entropy > middle, validf, 0.0)), DP)
        more = above > quota
        return (jnp.where(more, middle, low), jnp.where(more, high, middle))

    _, threshold = lax.fori_loop(0, ROUNDS, round_step, (f32(0.0), start_high))
    gate = validf * jnp.clip((entropy - threshold) / ramp_width + 0.5, 0.0, 1.0)
    coef = -(gate * advantage)
    probs = jnp.exp(logits - normal[:, None])
    slopes = (coef[:, None] * (hit.astype(f32) - probs)).astype(bf16)
    piece = lax.all_gather(slopes, DP, axis=0, tiled=True)
    head_grad = lax.dot_general(columns, piece, (((0,), (0,)), ((), ())), preferred_element_type=f32)
    product = lax.dot_general(piece, head, (((1,), (1,)), ((), ())), preferred_element_type=f32)
    return lax.psum_scatter(product, VOC, scatter_dimension=0, tiled=True), head_grad


def bisect(entropy, counted, start_high):
    columns = jnp.transpose(entropy)
    quota = jnp.floor((counted + 0.5) * 0.2)
    lane = lax.broadcasted_iota(jnp.int32, (1, 128), 1)
    leaves = 1 << LEVELS
    low = jnp.zeros((1, 128), f32)
    high = jnp.full((1, 128), start_high, f32)
    for _ in range(ROUNDS // LEVELS):
        for level in range(LEVELS):
            middle = (low + high) * 0.5
            bit = ((lane >> (LEVELS - 1 - level)) & 1) == 1
            low, high = jnp.where(bit, middle, low), jnp.where(bit, high, middle)
        above = jnp.zeros((128, 128), f32)
        for i in range(8):
            above = above + jnp.where(columns[:, i : i + 1] > low, 1.0, 0.0)
        above = jnp.sum(above, axis=0, keepdims=True)
        more = jnp.where(((above > quota) | (lane == 0)) & (lane < leaves), 1.0, 0.0)
        here = lane == jnp.sum(more, axis=1, keepdims=True).astype(jnp.int32) - 1
        low, high = (
            jnp.broadcast_to(jnp.sum(jnp.where(here, v, 0.0), axis=1, keepdims=True), (1, 128))
            for v in (low, high)
        )
    return high[:, :1]


def call(kernel, out, args, scratch=(), vmem=16, smem=0, loose=0, **kw):
    specs = [pl.BlockSpec(memory_space=pltpu.SMEM)] * smem
    specs += [pl.BlockSpec(memory_space=pltpu.VMEM)] * (len(args) - smem - loose)
    specs += [pl.BlockSpec(memory_space=pl.ANY)] * loose
    return pl.pallas_call(
        kernel,
        in_specs=specs,
        out_shape=out,
        scratch_shapes=list(scratch),
        compiler_params=pltpu.CompilerParams(vmem_limit_bytes=vmem << 20),
        **kw,
    )(*args)


def struct(shape, dtype):
    return jax.ShapeDtypeStruct(shape, dtype)


def estimate(m, k, n):
    return pl.CostEstimate(flops=2 * m * k * n, bytes_accessed=2 * k * n, transcendentals=0)


LN2_64 = float(np.log(2.0) / 64.0)


def valid_ranks(valid):
    i = lax.broadcasted_iota(jnp.int32, (128, 128), 0)
    j = lax.broadcasted_iota(jnp.int32, (128, 128), 1)
    mask = jnp.broadcast_to(valid[...].astype(f32), (8, 128))
    rank = jnp.dot(mask, (i < j).astype(f32), preferred_element_type=f32)
    return jnp.where(mask > 0.0, rank, -1.0)[0:1, :]


def split_kernel(at, hidden, valid, b0, b1, b2, b3):
    chip_rows = b0.shape[1]
    choose = one_hot(b0.shape[0], valid_ranks(valid))
    for s, out in enumerate((b0, b1, b2, b3)):
        to = lax.rem(at[0] + s, NX) * chip_rows
        block = hidden[:, pl.ds(pl.multiple_of(to, 128), chip_rows)]
        out[...] = jnp.dot(choose, block, preferred_element_type=f32).astype(bf16)


def table_kernel(valid, advantage, ids, after, table):
    rank = valid_ranks(valid)
    lane = lax.broadcasted_iota(jnp.int32, (128, 128), 1).astype(f32)
    place = lax.broadcasted_iota(jnp.int32, (1, 128), 1).astype(f32)
    mask = valid[...].astype(f32)
    columns = as_columns([rank, mask, advantage[...], ids[...].astype(f32), place])
    here = columns[:, 0:1] == lane
    row = lax.broadcasted_iota(jnp.int32, (8, 128), 0)
    out = jnp.broadcast_to(jnp.sum(mask, axis=1, keepdims=True), (8, 128))
    for k, to in ((1, 3), (2, 4), (3, 5), (4, 7)):
        value = jnp.sum(jnp.where(here, columns[:, k : k + 1], 0.0), axis=0, keepdims=True)
        out = jnp.where(row == to, value, out)
    table[...] = out


def turn_kernel(tick, head, turned):
    for k in range(head.shape[1] // 128):
        span = slice(k * 128, (k + 1) * 128)
        turned[span, :] = jnp.transpose(head[:, span])


def pack(block, out, to):
    step, cols = block.shape
    top = jnp.maximum(jnp.max(jnp.abs(block), axis=1, keepdims=True), 1e-30)
    power = jnp.ceil(jnp.log(top) * (1.0 / LN2_64)) + 1.0
    fixed = jnp.round(block * (jnp.exp(power * -LN2_64) * 32766.0))
    out[to, 0:cols] = fixed.astype(jnp.int32).astype(jnp.int16)
    wide_power = jnp.broadcast_to(power.astype(jnp.int32), (step, 128))
    out[to, cols : cols + 128] = wide_power.astype(jnp.int16)


def pack_rows(part, start, out):
    step = 16
    for row in range(0, out.shape[0], step):
        pack(part[start + row : start + row + step, :], out, slice(row, row + step))


def unpack(ref, at):
    cols = ref.shape[1] - 128
    power = ref[at, cols : cols + 128].astype(jnp.int32).astype(f32)[:, :1]
    return ref[at, 0:cols].astype(jnp.int32).astype(f32) * (jnp.exp(power * LN2_64) * (1.0 / 32766.0))


def over_columns(cols, tile):
    for start in range(0, cols, 256):
        tile(slice(start, min(start + 256, cols)))


def halves(at, rows):
    return (
        pl.ds(pl.multiple_of(at[1] * rows, 128), rows),
        pl.ds(pl.multiple_of((1 - at[1]) * rows, 128), rows),
    )


def own_kernel(at, block, head, other, own, kept):
    kept[...] = head[...]
    here, there = halves(at, head.shape[0])

    def tile(span):
        own[:, span] = jnp.dot(block[:, here], head[:, span], preferred_element_type=f32) + jnp.dot(
            block[:, there], other[:, span], preferred_element_type=f32
        )

    over_columns(head.shape[1], tile)


def far_kernel(at, block, head, other, low, high, tick, part):
    rows, cols = head.shape
    here, there = halves(at, rows)

    def tile(span):
        part[:, span] = jnp.dot(block[:, here], head[:, span], preferred_element_type=f32) + jnp.dot(
            block[:, there], other[:, span], preferred_element_type=f32
        )

    over_columns(cols, tile)
    tick[...] = jnp.zeros(tick.shape, f32)
    pack_rows(part, 0, low)
    pack_rows(part, LOW, high)


def near_kernel(at, tick, b0, b1, b2, b3, head, other, p1, p3, q1, q3, mine, theirs, part):
    count = b0.shape[0]
    rows, cols = head.shape
    here, there = halves(at, rows)
    for k, block in enumerate((b1, b3, b0, b2)):
        start = k * 128
        for stack, half in ((mine, here), (theirs, there)):
            stack[start : start + count, :] = block[:, half]
            stack[start + count : start + 128, :] = jnp.zeros((128 - count, rows), bf16)

    def tile(span):
        both = jnp.dot(mine[0:256, :], head[:, span], preferred_element_type=f32) + jnp.dot(
            theirs[0:256, :], other[:, span], preferred_element_type=f32
        )
        p1[:, span] = both[0:LOW, :]
        part[:, span] = both[LOW : 128 + LOW, :]
        p3[:, span] = both[128 + LOW : 128 + count, :]

    over_columns(cols, tile)
    pack_rows(part, 0, q1)
    pack_rows(part, 128 - LOW, q3)


def relay_kernel(p1, p3, low, high, q1, q3, tick):
    step = 16
    tick[...] = jnp.zeros(tick.shape, f32)
    for part, came, out in ((p1, low, q1), (p3, high, q3)):
        for start in range(0, part.shape[0], step):
            at = slice(start, start + step)
            pack(part[at, :] + unpack(came, at), out, at)


def total_kernel(own, q1_low, q1_high, q3_low, q3_high, turned, theirs, logits, sent, stats):
    count = own.shape[0]
    step = 16
    lane = lax.broadcasted_iota(jnp.int32, (step, 128), 1)
    logits[count:, :] = jnp.zeros((128 - count, own.shape[1]), f32)
    stats[count:, :] = jnp.ones((128 - count, 128), f32)
    for start in range(0, count, step):
        at = slice(start, start + step)
        q1, q3 = (q1_low, q3_low) if start < LOW else (q1_high, q3_high)
        part = slice(start % LOW, start % LOW + step)
        value = own[at, :] + unpack(q1, part) + unpack(q3, part)
        logits[at, :] = value
        high = jnp.max(value, axis=1, keepdims=True)
        shifted = jnp.exp(value - high)
        total = jnp.sum(shifted, axis=1, keepdims=True)
        moment = jnp.sum(shifted * value, axis=1, keepdims=True)
        stats[at, :] = jnp.where(lane == 0, high, jnp.where(lane == 1, total, moment))

    rows = jnp.transpose(stats[...])[0:8, :]
    for i in range(sent.shape[0]):
        sent[i] = rows


def merge_kernel(parts, table, sent):
    high = parts[0, 0:1, :]
    for i in range(1, parts.shape[0]):
        high = jnp.maximum(high, parts[i, 0:1, :])
    sums = jnp.zeros((8, 128), f32)
    for i in range(parts.shape[0]):
        sums = sums + jnp.exp(parts[i, 0:1, :] - high) * parts[i]
    row = lax.broadcasted_iota(jnp.int32, (8, 128), 0)
    out = jnp.where(row == 0, high, jnp.where(row < 3, sums, table[...]))
    for i in range(sent.shape[0]):
        sent[i] = out


def plan_kernel(start_high, parts, coef_out, normal_out, packed_out, slot_out, place_out, flag, rows):
    owners = 8
    ny = parts.shape[0] // owners
    for o in range(owners):
        high = parts[o * ny, 0:1, :]
        for y in range(1, ny):
            high = jnp.maximum(high, parts[o * ny + y, 0:1, :])
        sums = jnp.zeros((8, 128), f32)
        for y in range(ny):
            sums = sums + jnp.exp(parts[o * ny + y, 0:1, :] - high) * parts[o * ny + y]
        row = lax.broadcasted_iota(jnp.int32, (8, 128), 0)
        normal = high + jnp.log(sums[1:2, :])
        entropy = normal - sums[2:3, :] / sums[1:2, :]
        rows[o] = jnp.where(row == 0, normal, jnp.where(row == 1, entropy, parts[o * ny]))
    normal, entropy, valid, advantage, held, place = (
        jnp.concatenate([rows[o, k : k + 1, :] for o in range(owners)], axis=0) for k in (0, 1, 3, 4, 6, 7)
    )
    counted = jnp.sum(jnp.sum(valid, axis=1, keepdims=True), axis=0, keepdims=True)
    threshold = bisect(jnp.where(valid > 0.0, entropy, -jnp.inf), counted, start_high)
    gate = valid * jnp.clip((entropy - threshold) / ramp_width + 0.5, 0.0, 1.0)
    coef = -(gate * advantage)
    active = coef != 0.0
    activef = active.astype(f32)
    i = lax.broadcasted_iota(jnp.int32, (128, 128), 0)
    j = lax.broadcasted_iota(jnp.int32, (128, 128), 1)
    ahead = (i < j).astype(f32)
    rank_owner = jnp.dot(activef, ahead, preferred_element_type=f32)
    group = 128 // (32 // owners)
    start = jnp.zeros((8, 1), f32)
    slot = jnp.full((8, 128), -1.0, f32)
    over = jnp.where(active & (rank_owner >= CAP_SMALL), 1.0, 0.0)
    for g in range(128 // group):
        member = active & (place >= float(g * group)) & (place < float((g + 1) * group))
        rank_group = rank_owner - start
        slot = jnp.where(member, rank_group + float(g * CAP), slot)
        over = jnp.where(member & (rank_group >= CAP), 2.0, over)
        start = start + jnp.sum(jnp.where(member, 1.0, 0.0), axis=1, keepdims=True)
    over = jnp.where(held > float(VALID), 2.0, over)
    coef_out[...] = coef
    normal_out[...] = normal
    packed_out[...] = jnp.where(active, rank_owner, -1.0)
    slot_out[...] = slot
    place_out[...] = place
    flag[0, 0] = jnp.max(over).astype(jnp.int32)


def as_columns(rows):
    row = lax.broadcasted_iota(jnp.int32, (8, 128), 0)
    out = jnp.zeros((8, 128), f32)
    for k, value in enumerate(rows):
        out = jnp.where(row == k, value, out)
    return jnp.transpose(out)


def one_hot(count, slots):
    row = lax.broadcasted_iota(jnp.int32, (count, 128), 0).astype(f32)
    return (row == slots).astype(f32).astype(bf16)


def slopes_kernel(at, logits, coef_all, normal_all, packed_all, table, out):
    me = pl.ds(at[2], 1)
    count = out.shape[0]
    columns = as_columns([coef_all[me, :], normal_all[me, :], table[5:6, :]])
    coef, normal, token = columns[:, 0:1], columns[:, 1:2], columns[:, 2:3].astype(jnp.int32) - at[3]
    choose = one_hot(count, packed_all[me, :])
    lane = lax.broadcasted_iota(jnp.int32, (128, 128), 1)
    for k in range(logits.shape[1] // 128):
        span = slice(k * 128, (k + 1) * 128)
        hit = (lane + k * 128 == token).astype(f32)
        slopes = (coef * (hit - jnp.exp(logits[:, span] - normal))).astype(bf16)
        out[:, span] = jnp.dot(choose, slopes, preferred_element_type=f32).astype(bf16)


def owner_of(at, s, k):
    return lax.rem(at[0] - s + NX, NX) * 2 + lax.rem(at[1] + k, 2)


def product_kernel(at, mine, theirs, turned, slopes, o0, o1, o2, o3, held):
    half = mine.shape[0]
    cap = half // NX
    slopes[0:half, :] = mine[...]
    slopes[half:, :] = theirs[...]
    held[...] = jnp.dot(slopes[...], turned[...], preferred_element_type=f32).astype(bf16)
    for step, out in enumerate((o0, o1, o2, o3)):
        source = lax.rem(at[0] - at[5] - step + 2 * NX, NX) * cap
        for k in range(2):
            rows = pl.ds(pl.multiple_of(source + k * half, cap), cap)
            out[k * cap : (k + 1) * cap, :] = held[rows, :]


def outer_kernel(at, packed_all, hid_mine, hid_theirs, slopes, above, after, out, tick, held):
    half = slopes.shape[0] // 2
    cap = half // NX
    tick[...] = jnp.zeros(tick.shape, f32)
    for k, hidden in enumerate((hid_mine, hid_theirs)):
        for s in range(NX):
            choose = one_hot(cap, packed_all[pl.ds(owner_of(at, s, k), 1), :])
            to = k * half + s * cap
            held[to : to + cap, :] = jnp.dot(
                choose, hidden[ORDER[s] * 128 : (ORDER[s] + 1) * 128, :], preferred_element_type=f32
            ).astype(bf16)
    out[...] = lax.dot_general(
        held[...], slopes[...], (((0,), (0,)), ((), ())), preferred_element_type=f32
    )


def outer(at, packed_all, hid_mine, hid_theirs, slopes, first, count, above, after):
    (tokens, rows), (depth, cols) = hid_mine.shape, slopes.shape
    tile = 128
    whole_block = lambda i: (0, 0)
    in_specs = [
        pl.BlockSpec(memory_space=pltpu.SMEM),
        pl.BlockSpec(packed_all.shape, whole_block),
        pl.BlockSpec((tokens, tile), lambda i: (0, i + first)),
        pl.BlockSpec((tokens, tile), lambda i: (0, i + first)),
        pl.BlockSpec((depth, cols), whole_block),
        pl.BlockSpec(memory_space=pl.ANY),
        pl.BlockSpec(memory_space=pl.ANY),
    ]
    aliases = {5: 0} if above.shape == (rows, cols) else {}
    return pl.pallas_call(
        outer_kernel,
        grid=(count,),
        in_specs=in_specs,
        out_specs=[pl.BlockSpec((tile, cols), lambda i: (i + first, 0)), pl.BlockSpec((8, 128), whole_block)],
        out_shape=[struct((rows, cols), f32), struct((8, 128), f32)],
        scratch_shapes=[pltpu.VMEM((depth, tile), bf16)],
        input_output_aliases=aliases,
        compiler_params=pltpu.CompilerParams(vmem_limit_bytes=24 << 20),
        cost_estimate=estimate(count * tile, depth, cols),
    )(at, packed_all, hid_mine, hid_theirs, slopes, above, after)


def spread_kernel(at, before, r0, r1, r2, r3, packed_all, slot_all, out, tick):
    size = out.shape[0]
    cap = r0.shape[0] // 2
    tick[...] = jnp.zeros(tick.shape, f32)
    spread = []
    for k in range(2):
        core = lax.rem(at[1] + k, 2)
        me = pl.ds(at[5] * 2 + core, 1)
        slot = slot_all[me, :]
        slot = jnp.where(slot >= 0.0, slot + (core * (size // 2)).astype(f32), -1.0)
        part = lax.dot_general(
            one_hot(size, slot),
            one_hot(cap, packed_all[me, :]),
            (((1,), (1,)), ((), ())),
            preferred_element_type=f32,
        )
        spread.append(part.astype(bf16))
    spread = jnp.concatenate(spread, axis=1)
    total = jnp.zeros((size, r0.shape[1]), f32)
    for r in (r0, r1, r2, r3):
        total = total + jnp.dot(spread, r[...], preferred_element_type=f32)
    pack(total, out, slice(0, size))


def sum_kernel(at, parts, slot_all, place_all, out):
    total = unpack(parts, slice(0, CAP))
    for i in range(1, parts.shape[0] // CAP):
        total = total + unpack(parts, slice(i * CAP, (i + 1) * CAP))
    group = out.shape[0]
    per_owner = 128 // group
    me, block = pl.ds(at[4] // per_owner, 1), lax.rem(at[4], per_owner)
    slot, place = slot_all[me, :], place_all[me, :]
    token = lax.broadcasted_iota(jnp.int32, (group, 128), 0) + block * group
    here = (place == token.astype(f32)) & (slot >= 0.0)
    rank = jnp.sum(jnp.where(here, slot + 1.0, 0.0), axis=1, keepdims=True)
    rank = rank - 1.0 - (block * CAP).astype(f32)
    rows = jnp.zeros(out.shape, f32)
    for r in range(CAP):
        rows = rows + jnp.where(rank == float(r), total[r : r + 1, :], 0.0)
    out[...] = rows


def shards(hidden_states, head, token_ids, valid, advantage):
    tokens, width = hidden_states.shape
    rows, voc_cols = head.shape
    nx, n_voc, n_dp = lax.axis_size("x"), lax.axis_size(VOC), lax.axis_size(DP)
    x, c, block = lax.axis_index("x"), lax.axis_index("c"), lax.axis_index(VOC)
    at = jnp.stack([x, c, x * 2 + c, block * voc_cols, block, lax.axis_index("y")]).astype(jnp.int32)
    chip_rows = width // nx

    head_other = lax.ppermute(head, "c", SWAP)

    valid_row, advantage_row, id_row = (v.reshape(1, tokens) for v in (valid, advantage, token_ids))
    block_shape = struct((VALID, chip_rows), bf16)
    b0, *leave = call(split_kernel, [block_shape] * 4, [at, hidden_states, valid_row], smem=1)
    came = {s: lax.ppermute(leave[s - 1], "x", ring(nx, s)) for s in (2, 1, 3)}
    partial = struct((VALID, voc_cols), f32)
    tick_shape = struct((8, 128), f32)
    own, kept = call(
        own_kernel,
        [partial, struct((rows, voc_cols), bf16)],
        [at, b0, head, head_other],
        smem=1,
        cost_estimate=estimate(tokens, chip_rows, voc_cols),
    )
    table = call(table_kernel, tick_shape, [valid_row, advantage_row, id_row, own], loose=1)
    first = struct((LOW, voc_cols + 128), jnp.int16)
    second = struct((VALID - LOW, voc_cols + 128), jnp.int16)
    low, high, tick = call(
        far_kernel,
        [first, second, tick_shape],
        [at, came[2], kept, head_other],
        [pltpu.VMEM((VALID, voc_cols), f32)],
        smem=1,
        cost_estimate=estimate(tokens, chip_rows, voc_cols),
    )
    low, high = lax.ppermute(low, "x", ring(nx, -1)), lax.ppermute(high, "x", ring(nx, 1))
    relayed = [struct((n, voc_cols), f32) for n in (LOW, VALID - LOW)]
    p1, p3, q1_high, q3_low, hid_mine, hid_send = call(
        near_kernel,
        relayed + [second, first] + [struct((nx * tokens, rows), bf16)] * 2,
        [at, tick, b0, came[1], came[2], came[3], kept, head_other],
        [pltpu.VMEM((tokens, voc_cols), f32)],
        vmem=24,
        smem=1,
        cost_estimate=estimate(2 * tokens, chip_rows, voc_cols),
    )
    q1_high, q3_low = lax.ppermute(q1_high, "x", ring(nx, -1)), lax.ppermute(q3_low, "x", ring(nx, 1))
    q1_low, q3_high, tick = call(relay_kernel, [first, second, tick_shape], [p1, p3, low, high])
    q1_low, q3_high = lax.ppermute(q1_low, "x", ring(nx, -1)), lax.ppermute(q3_high, "x", ring(nx, 1))
    turned = call(turn_kernel, struct((voc_cols, rows), bf16), [tick, kept])
    hid_theirs = lax.ppermute(hid_send, "c", SWAP)
    logits, stats = call(
        total_kernel,
        [struct((tokens, voc_cols), f32), struct((lax.axis_size("z"), 8, 128), f32)],
        [own, q1_low, q1_high, q3_low, q3_high, turned, hid_theirs],
        [pltpu.VMEM((tokens, 128), f32)],
        loose=2,
    )

    stats = lax.all_to_all(stats, "z", 0, 0, tiled=True)
    everyone = DP + ("y",)
    stats = call(
        merge_kernel,
        struct((lax.axis_size(everyone), 8, 128), f32),
        [stats, table],
    )
    stats = lax.all_to_all(stats, everyone, 0, 0, tiled=True)
    start_high = float(np.float32(np.log(np.float32(voc_cols * n_voc))) + np.float32(1.0))
    everyones = struct((n_dp, tokens), f32)
    coef_all, normal_all, packed_all, slot_all, place_all, flag = call(
        functools.partial(plan_kernel, start_high),
        [everyones] * 5 + [struct((1, 1), jnp.int32)],
        [stats],
        [pltpu.VMEM((n_dp, 8, 128), f32)],
        out_specs=[pl.BlockSpec(memory_space=pltpu.VMEM)] * 5 + [pl.BlockSpec(memory_space=pltpu.SMEM)],
    )

    def backward(cap):
        piece = call(
            slopes_kernel,
            struct((cap, voc_cols), bf16),
            [at, logits, coef_all, normal_all, packed_all, table],
            smem=1,
        )
        pieces = {s: lax.ppermute(piece, "x", ring(nx, s)) for s in (2, 1, 3)}
        mine = jnp.concatenate([piece, pieces[1], pieces[2], pieces[3]], axis=0)
        theirs = lax.ppermute(mine, "c", SWAP)
        return call(
            product_kernel,
            [struct((2 * nx * cap, voc_cols), bf16)] + [struct((2 * cap, rows), bf16)] * nx,
            [at, mine, theirs, turned],
            [pltpu.VMEM((2 * nx * cap, rows), bf16)],
            smem=1,
        )

    def finish(slopes, *parts):
        parts = [parts[0]] + [lax.ppermute(parts[k], "y", ring(nx, k)) for k in range(1, nx)]
        sides = (at, packed_all, hid_mine, hid_theirs, slopes)
        blocks = rows // 128
        early = (blocks + 1) // 2
        head_grad, tick = outer(*sides, 0, early, packed_all, packed_all)
        spread, tick = call(
            spread_kernel,
            [struct((n_voc * CAP // nx, rows + 128), jnp.int16), tick_shape],
            [at, tick, *parts, packed_all, slot_all],
            smem=1,
        )
        spread = lax.all_to_all(spread, "z", 0, 0, tiled=True)
        head_grad, _ = outer(*sides, early, blocks - early, head_grad, tick)
        hidden_grad = call(
            sum_kernel,
            struct((tokens * n_dp // n_voc, rows), f32),
            [at, spread, slot_all, place_all],
            smem=1,
        )
        return hidden_grad, head_grad

    def whole(_):
        return dense(hidden_states, head, token_ids, valid, advantage)

    packed_rows = backward(CAP_SMALL)

    def small(_):
        return finish(*packed_rows)

    def large(_):
        return finish(*backward(CAP * n_voc // n_dp))

    return lax.switch(flag[0, 0], [small, large, whole], 0)


def solution(mesh):
    chips = Mesh(mesh.devices.reshape(4, 2, 4, 8), DP + VOC)
    placed = (P(DP, None), P(DP, VOC), P(DP), P(DP), P(DP))
    return jax.shard_map(
        shards,
        mesh=chips,
        in_specs=placed,
        out_specs=(P(VOC, DP), P(DP, VOC)),
        check_vma=False,
    )
```

```python
import functools

import jax
import jax.numpy as jnp
import numpy as np
from jax import lax
from jax.experimental import pallas as pl
from jax.experimental.pallas import tpu as pltpu
from jax.sharding import Mesh, PartitionSpec as P

ROUNDS = 24
LEVELS = 8
CAP = 16
CAP_SMALL = 32
ORDER = (2, 0, 3, 1)
NX = 4

ramp_width = 0.5
DP = ("x", "c")
VOC = ("y", "z")
f32 = jnp.float32
bf16 = jnp.bfloat16


def ring(n, shift):
    return [(i, (i + shift) % n) for i in range(n)]


SWAP = [(0, 1), (1, 0)]


def dense(hidden_states, head, token_ids, valid, advantage):
    voc_cols = head.shape[1]
    columns = lax.all_to_all(hidden_states, DP, split_axis=1, concat_axis=0, tiled=True)
    logits = lax.psum_scatter(
        jnp.dot(columns, head, preferred_element_type=f32), DP, scatter_dimension=0, tiled=True
    )
    offset = lax.axis_index(VOC) * voc_cols
    hit = jnp.arange(voc_cols, dtype=jnp.int32)[None, :] + offset == token_ids[:, None]
    highest = lax.pmax(jnp.max(logits, axis=1), VOC)
    shifted = jnp.exp(logits - highest[:, None])
    total, moment = lax.psum((jnp.sum(shifted, axis=1), jnp.sum(shifted * logits, axis=1)), VOC)
    normal = highest + jnp.log(total)
    entropy = normal - moment / total
    validf = valid.astype(f32)
    start_high = jnp.log(f32(voc_cols * lax.axis_size(VOC))) + 1.0
    counted = lax.psum(jnp.sum(validf), DP)
    quota = jnp.floor((counted + 0.5) * 0.2)

    def round_step(step, bounds):
        low, high = bounds
        middle = (low + high) * 0.5
        above = lax.psum(jnp.sum(jnp.where(entropy > middle, validf, 0.0)), DP)
        more = above > quota
        return (jnp.where(more, middle, low), jnp.where(more, high, middle))

    _, threshold = lax.fori_loop(0, ROUNDS, round_step, (f32(0.0), start_high))
    gate = validf * jnp.clip((entropy - threshold) / ramp_width + 0.5, 0.0, 1.0)
    coef = -(gate * advantage)
    probs = jnp.exp(logits - normal[:, None])
    slopes = (coef[:, None] * (hit.astype(f32) - probs)).astype(bf16)
    piece = lax.all_gather(slopes, DP, axis=0, tiled=True)
    head_grad = lax.dot_general(columns, piece, (((0,), (0,)), ((), ())), preferred_element_type=f32)
    product = lax.dot_general(piece, head, (((1,), (1,)), ((), ())), preferred_element_type=f32)
    return lax.psum_scatter(product, VOC, scatter_dimension=0, tiled=True), head_grad


def bisect(entropy, counted, start_high):
    columns = jnp.transpose(entropy)
    quota = jnp.floor((counted + 0.5) * 0.2)
    leaves = 1 << LEVELS
    lane = lax.broadcasted_iota(jnp.int32, (1, leaves), 1)
    low = jnp.zeros((1, leaves), f32)
    high = jnp.full((1, leaves), start_high, f32)
    for _ in range(ROUNDS // LEVELS):
        for level in range(LEVELS):
            middle = (low + high) * 0.5
            bit = ((lane >> (LEVELS - 1 - level)) & 1) == 1
            low, high = jnp.where(bit, middle, low), jnp.where(bit, high, middle)
        above = jnp.zeros((128, leaves), f32)
        for i in range(8):
            above = above + jnp.where(columns[:, i : i + 1] > low, 1.0, 0.0)
        above = jnp.sum(above, axis=0, keepdims=True)
        more = jnp.where((above > quota) | (lane == 0), 1.0, 0.0)
        here = lane == jnp.sum(more, axis=1, keepdims=True).astype(jnp.int32) - 1
        low, high = (
            jnp.broadcast_to(jnp.sum(jnp.where(here, v, 0.0), axis=1, keepdims=True), (1, leaves))
            for v in (low, high)
        )
    return high[:, :1]


def call(kernel, out, args, scratch=(), vmem=16, smem=0, loose=0, **kw):
    specs = [pl.BlockSpec(memory_space=pltpu.SMEM)] * smem
    specs += [pl.BlockSpec(memory_space=pltpu.VMEM)] * (len(args) - smem - loose)
    specs += [pl.BlockSpec(memory_space=pl.ANY)] * loose
    return pl.pallas_call(
        kernel,
        in_specs=specs,
        out_shape=out,
        scratch_shapes=list(scratch),
        compiler_params=pltpu.CompilerParams(vmem_limit_bytes=vmem << 20),
        **kw,
    )(*args)


def struct(shape, dtype):
    return jax.ShapeDtypeStruct(shape, dtype)


def estimate(m, k, n):
    return pl.CostEstimate(flops=2 * m * k * n, bytes_accessed=2 * k * n, transcendentals=0)


LN2_64 = float(np.log(2.0) / 64.0)


def split_kernel(at, hidden, b0, b1, b2, b3):
    chip_rows = b0.shape[1]
    nx = hidden.shape[1] // chip_rows
    for s, out in enumerate((b0, b1, b2, b3)):
        to = lax.rem(at[0] + s, nx) * chip_rows
        out[...] = hidden[:, pl.ds(pl.multiple_of(to, 128), chip_rows)]


def turn_kernel(tick, head, turned):
    for k in range(head.shape[1] // 128):
        span = slice(k * 128, (k + 1) * 128)
        turned[span, :] = jnp.transpose(head[:, span])


def pack(block, out, to):
    step, cols = block.shape
    top = jnp.maximum(jnp.max(jnp.abs(block), axis=1, keepdims=True), 1e-30)
    power = jnp.ceil(jnp.log(top) * (1.0 / LN2_64)) + 1.0
    fixed = jnp.round(block * (jnp.exp(power * -LN2_64) * 32766.0))
    out[to, 0:cols] = fixed.astype(jnp.int32).astype(jnp.int16)
    wide_power = jnp.broadcast_to(power.astype(jnp.int32), (step, 128))
    out[to, cols : cols + 128] = wide_power.astype(jnp.int16)


def pack_rows(part, start, out):
    step = 16
    for row in range(0, out.shape[0], step):
        pack(part[start + row : start + row + step, :], out, slice(row, row + step))


def unpack(ref, at):
    cols = ref.shape[1] - 128
    power = ref[at, cols : cols + 128].astype(jnp.int32).astype(f32)[:, :1]
    return ref[at, 0:cols].astype(jnp.int32).astype(f32) * (jnp.exp(power * LN2_64) * (1.0 / 32766.0))


def over_columns(cols, tile):
    for start in range(0, cols, 256):
        tile(slice(start, min(start + 256, cols)))


def halves(at, rows):
    return (
        pl.ds(pl.multiple_of(at[1] * rows, 128), rows),
        pl.ds(pl.multiple_of((1 - at[1]) * rows, 128), rows),
    )


def own_kernel(at, block, head, other, own, kept):
    kept[...] = head[...]
    here, there = halves(at, head.shape[0])

    def tile(span):
        own[:, span] = jnp.dot(block[:, here], head[:, span], preferred_element_type=f32) + jnp.dot(
            block[:, there], other[:, span], preferred_element_type=f32
        )

    over_columns(head.shape[1], tile)


def far_kernel(at, block, head, other, low, high, tick, part):
    tokens = block.shape[0]
    rows, cols = head.shape
    here, there = halves(at, rows)

    def tile(span):
        part[:, span] = jnp.dot(block[:, here], head[:, span], preferred_element_type=f32) + jnp.dot(
            block[:, there], other[:, span], preferred_element_type=f32
        )

    over_columns(cols, tile)
    tick[...] = jnp.zeros(tick.shape, f32)
    half = tokens // 2
    pack_rows(part, 0, low)
    pack_rows(part, half, high)


def near_kernel(at, tick, b0, b1, b2, b3, head, other, p1, p3, q1, q3, mine, theirs, part):
    tokens = b0.shape[0]
    half = tokens // 2
    rows, cols = head.shape
    here, there = halves(at, rows)
    for k, block in enumerate((b1, b3, b0, b2)):
        mine[k * tokens : (k + 1) * tokens, :] = block[:, here]
        theirs[k * tokens : (k + 1) * tokens, :] = block[:, there]

    def tile(span):
        both = jnp.dot(mine[0 : 2 * tokens, :], head[:, span], preferred_element_type=f32) + jnp.dot(
            theirs[0 : 2 * tokens, :], other[:, span], preferred_element_type=f32
        )
        p1[:, span] = both[0:half, :]
        part[:, span] = both[half : tokens + half, :]
        p3[:, span] = both[tokens + half :, :]

    over_columns(cols, tile)
    pack_rows(part, 0, q1)
    pack_rows(part, half, q3)


def relay_kernel(p1, p3, low, high, q1, q3, tick):
    step = 16
    tick[...] = jnp.zeros(tick.shape, f32)
    for start in range(0, p1.shape[0], step):
        at = slice(start, start + step)
        pack(p1[at, :] + unpack(low, at), q1, at)
        pack(p3[at, :] + unpack(high, at), q3, at)


def total_kernel(own, q1_low, q1_high, q3_low, q3_high, turned, theirs, logits, sent, stats):
    tokens = own.shape[0]
    step = 16
    lane = lax.broadcasted_iota(jnp.int32, (step, 128), 1)
    for start in range(0, tokens, step):
        at = slice(start, start + step)
        q1, q3 = (q1_low, q3_low) if start < tokens // 2 else (q1_high, q3_high)
        part = slice(start % (tokens // 2), start % (tokens // 2) + step)
        value = own[at, :] + unpack(q1, part) + unpack(q3, part)
        logits[at, :] = value
        high = jnp.max(value, axis=1, keepdims=True)
        shifted = jnp.exp(value - high)
        total = jnp.sum(shifted, axis=1, keepdims=True)
        moment = jnp.sum(shifted * value, axis=1, keepdims=True)
        stats[at, :] = jnp.where(lane == 0, high, jnp.where(lane == 1, total, moment))

    rows = jnp.transpose(stats[...])[0:8, :]
    for i in range(sent.shape[0]):
        sent[i] = rows


def merge_kernel(parts, valid, advantage, sent):
    high = parts[0, 0:1, :]
    for i in range(1, parts.shape[0]):
        high = jnp.maximum(high, parts[i, 0:1, :])
    sums = jnp.zeros((8, 128), f32)
    for i in range(parts.shape[0]):
        sums = sums + jnp.exp(parts[i, 0:1, :] - high) * parts[i]
    row = lax.broadcasted_iota(jnp.int32, (8, 128), 0)
    out = jnp.where(row == 0, high, sums)
    out = jnp.where(row == 3, valid[...].astype(f32), jnp.where(row == 4, advantage[...], out))
    for i in range(sent.shape[0]):
        sent[i] = out


def plan_kernel(start_high, parts, coef_out, normal_out, packed_out, slot_out, flag, rows):
    owners = 8
    ny = parts.shape[0] // owners
    for o in range(owners):
        high = parts[o * ny, 0:1, :]
        for y in range(1, ny):
            high = jnp.maximum(high, parts[o * ny + y, 0:1, :])
        sums = jnp.zeros((8, 128), f32)
        for y in range(ny):
            sums = sums + jnp.exp(parts[o * ny + y, 0:1, :] - high) * parts[o * ny + y]
        row = lax.broadcasted_iota(jnp.int32, (8, 128), 0)
        normal = high + jnp.log(sums[1:2, :])
        entropy = normal - sums[2:3, :] / sums[1:2, :]
        rows[o] = jnp.where(row == 0, normal, jnp.where(row == 1, entropy, parts[o * ny]))
    normal, entropy, valid, advantage = (
        jnp.concatenate([rows[o, k : k + 1, :] for o in range(owners)], axis=0) for k in (0, 1, 3, 4)
    )
    counted = jnp.sum(jnp.sum(valid, axis=1, keepdims=True), axis=0, keepdims=True)
    threshold = bisect(jnp.where(valid > 0.0, entropy, -jnp.inf), counted, start_high)
    gate = valid * jnp.clip((entropy - threshold) / ramp_width + 0.5, 0.0, 1.0)
    coef = -(gate * advantage)
    active = coef != 0.0
    activef = active.astype(f32)
    i = lax.broadcasted_iota(jnp.int32, (128, 128), 0)
    j = lax.broadcasted_iota(jnp.int32, (128, 128), 1)
    ahead = (i < j).astype(f32)
    group = 128 // (32 // owners)
    same = (i // group == j // group).astype(f32)
    rank_owner = jnp.dot(activef, ahead, preferred_element_type=f32)
    rank_group = jnp.dot(activef, ahead * same, preferred_element_type=f32)
    start = (lax.broadcasted_iota(jnp.int32, (8, 128), 1) // group * CAP).astype(f32)
    coef_out[...] = coef
    normal_out[...] = normal
    packed_out[...] = jnp.where(active, rank_owner, -1.0)
    slot_out[...] = jnp.where(active, rank_group + start, -1.0)
    over = jnp.where(active & (rank_owner >= CAP_SMALL), 1.0, 0.0)
    over = jnp.where(active & (rank_group >= CAP), 2.0, over)
    flag[0, 0] = jnp.max(over).astype(jnp.int32)


def as_columns(rows):
    row = lax.broadcasted_iota(jnp.int32, (8, 128), 0)
    out = jnp.zeros((8, 128), f32)
    for k, value in enumerate(rows):
        out = jnp.where(row == k, value, out)
    return jnp.transpose(out)


def one_hot(count, slots):
    row = lax.broadcasted_iota(jnp.int32, (count, 128), 0).astype(f32)
    return (row == slots).astype(f32).astype(bf16)


def slopes_kernel(at, logits, coef_all, normal_all, packed_all, ids, out):
    me = pl.ds(at[2], 1)
    count = out.shape[0]
    columns = as_columns([coef_all[me, :], normal_all[me, :], ids[...].astype(f32)])
    coef, normal, token = columns[:, 0:1], columns[:, 1:2], columns[:, 2:3].astype(jnp.int32) - at[3]
    choose = one_hot(count, packed_all[me, :])
    lane = lax.broadcasted_iota(jnp.int32, (128, 128), 1)
    for k in range(logits.shape[1] // 128):
        span = slice(k * 128, (k + 1) * 128)
        hit = (lane + k * 128 == token).astype(f32)
        slopes = (coef * (hit - jnp.exp(logits[:, span] - normal))).astype(bf16)
        out[:, span] = jnp.dot(choose, slopes, preferred_element_type=f32).astype(bf16)


def owner_of(at, s, k):
    return lax.rem(at[0] - s + NX, NX) * 2 + lax.rem(at[1] + k, 2)


def half_kernel(mine, turned, out):
    out[...] = jnp.dot(mine[...], turned[...], preferred_element_type=f32).astype(bf16)


def product_kernel(at, mine, theirs, turned, first, slopes, o0, o1, o2, o3, held):
    half = mine.shape[0]
    cap = half // NX
    slopes[0:half, :] = mine[...]
    slopes[half:, :] = theirs[...]
    held[0:half, :] = first[...]
    held[half:, :] = jnp.dot(theirs[...], turned[...], preferred_element_type=f32).astype(bf16)
    for step, out in enumerate((o0, o1, o2, o3)):
        source = lax.rem(at[0] - at[5] - step + 2 * NX, NX) * cap
        for k in range(2):
            rows = pl.ds(pl.multiple_of(source + k * half, cap), cap)
            out[k * cap : (k + 1) * cap, :] = held[rows, :]


def outer_kernel(at, packed_all, hid_mine, hid_theirs, slopes, above, after, out, tick, held):
    half = slopes.shape[0] // 2
    cap = half // NX
    tick[...] = jnp.zeros(tick.shape, f32)
    for k, hidden in enumerate((hid_mine, hid_theirs)):
        for s in range(NX):
            choose = one_hot(cap, packed_all[pl.ds(owner_of(at, s, k), 1), :])
            to = k * half + s * cap
            held[to : to + cap, :] = jnp.dot(
                choose, hidden[ORDER[s] * 128 : (ORDER[s] + 1) * 128, :], preferred_element_type=f32
            ).astype(bf16)
    out[...] = lax.dot_general(
        held[...], slopes[...], (((0,), (0,)), ((), ())), preferred_element_type=f32
    )


def outer(at, packed_all, hid_mine, hid_theirs, slopes, first, count, above, after):
    (tokens, rows), (depth, cols) = hid_mine.shape, slopes.shape
    tile = 128
    whole_block = lambda i: (0, 0)
    in_specs = [
        pl.BlockSpec(memory_space=pltpu.SMEM),
        pl.BlockSpec(packed_all.shape, whole_block),
        pl.BlockSpec((tokens, tile), lambda i: (0, i + first)),
        pl.BlockSpec((tokens, tile), lambda i: (0, i + first)),
        pl.BlockSpec((depth, cols), whole_block),
        pl.BlockSpec(memory_space=pl.ANY),
        pl.BlockSpec(memory_space=pl.ANY),
    ]
    aliases = {5: 0} if above.shape == (rows, cols) else {}
    return pl.pallas_call(
        outer_kernel,
        grid=(count,),
        in_specs=in_specs,
        out_specs=[pl.BlockSpec((tile, cols), lambda i: (i + first, 0)), pl.BlockSpec((8, 128), whole_block)],
        out_shape=[struct((rows, cols), f32), struct((8, 128), f32)],
        scratch_shapes=[pltpu.VMEM((depth, tile), bf16)],
        input_output_aliases=aliases,
        compiler_params=pltpu.CompilerParams(vmem_limit_bytes=24 << 20),
        cost_estimate=estimate(count * tile, depth, cols),
    )(at, packed_all, hid_mine, hid_theirs, slopes, above, after)


def spread_kernel(at, before, r0, r1, r2, r3, packed_all, slot_all, out, tick):
    size = out.shape[0]
    cap = r0.shape[0] // 2
    tick[...] = jnp.zeros(tick.shape, f32)
    spread = []
    for k in range(2):
        core = lax.rem(at[1] + k, 2)
        me = pl.ds(at[5] * 2 + core, 1)
        slot = slot_all[me, :]
        slot = jnp.where(slot >= 0.0, slot + (core * (size // 2)).astype(f32), -1.0)
        part = lax.dot_general(
            one_hot(size, slot),
            one_hot(cap, packed_all[me, :]),
            (((1,), (1,)), ((), ())),
            preferred_element_type=f32,
        )
        spread.append(part.astype(bf16))
    spread = jnp.concatenate(spread, axis=1)
    total = jnp.zeros((size, r0.shape[1]), f32)
    for r in (r0, r1, r2, r3):
        total = total + jnp.dot(spread, r[...], preferred_element_type=f32)
    pack(total, out, slice(0, size))


def sum_kernel(at, parts, slot_all, out, ranks):
    total = unpack(parts, slice(0, CAP))
    for i in range(1, parts.shape[0] // CAP):
        total = total + unpack(parts, slice(i * CAP, (i + 1) * CAP))
    group = out.shape[0]
    per_owner = 128 // group
    owner, place = at[4] // per_owner, lax.rem(at[4], per_owner)
    ranks[...] = as_columns([slot_all[pl.ds(owner, 1), :]])
    rank = ranks[pl.ds(pl.multiple_of(place * group, group), group), :][:, 0:1]
    rank = rank - (place * CAP).astype(f32)
    rows = jnp.zeros(out.shape, f32)
    for r in range(CAP):
        rows = rows + jnp.where(rank == float(r), total[r : r + 1, :], 0.0)
    out[...] = rows


def shards(hidden_states, head, token_ids, valid, advantage):
    tokens, width = hidden_states.shape
    rows, voc_cols = head.shape
    nx, n_voc, n_dp = lax.axis_size("x"), lax.axis_size(VOC), lax.axis_size(DP)
    x, c, block = lax.axis_index("x"), lax.axis_index("c"), lax.axis_index(VOC)
    at = jnp.stack([x, c, x * 2 + c, block * voc_cols, block, lax.axis_index("y")]).astype(jnp.int32)
    chip_rows = width // nx

    head_other = lax.ppermute(head, "c", SWAP)

    block_shape = struct((tokens, chip_rows), bf16)
    b0, *leave = call(split_kernel, [block_shape] * 4, [at, hidden_states], smem=1)
    came = {s: lax.ppermute(leave[s - 1], "x", ring(nx, s)) for s in (2, 1, 3)}
    partial = struct((tokens, voc_cols), f32)
    tick_shape = struct((8, 128), f32)
    own, kept = call(
        own_kernel,
        [partial, struct((rows, voc_cols), bf16)],
        [at, b0, head, head_other],
        smem=1,
        cost_estimate=estimate(tokens, chip_rows, voc_cols),
    )
    half = struct((tokens // 2, voc_cols + 128), jnp.int16)
    low, high, tick = call(
        far_kernel,
        [half, half, tick_shape],
        [at, came[2], kept, head_other],
        [pltpu.VMEM((tokens, voc_cols), f32)],
        smem=1,
        cost_estimate=estimate(tokens, chip_rows, voc_cols),
    )
    low, high = lax.ppermute(low, "x", ring(nx, -1)), lax.ppermute(high, "x", ring(nx, 1))
    half_partial = struct((tokens // 2, voc_cols), f32)
    p1, p3, q1_high, q3_low, hid_mine, hid_send = call(
        near_kernel,
        [half_partial] * 2 + [half] * 2 + [struct((nx * tokens, rows), bf16)] * 2,
        [at, tick, b0, came[1], came[2], came[3], kept, head_other],
        [pltpu.VMEM((tokens, voc_cols), f32)],
        vmem=24,
        smem=1,
        cost_estimate=estimate(2 * tokens, chip_rows, voc_cols),
    )
    q1_high, q3_low = lax.ppermute(q1_high, "x", ring(nx, -1)), lax.ppermute(q3_low, "x", ring(nx, 1))
    q1_low, q3_high, tick = call(relay_kernel, [half] * 2 + [tick_shape], [p1, p3, low, high])
    q1_low, q3_high = lax.ppermute(q1_low, "x", ring(nx, -1)), lax.ppermute(q3_high, "x", ring(nx, 1))
    turned = call(turn_kernel, struct((voc_cols, rows), bf16), [tick, kept])
    hid_theirs = lax.ppermute(hid_send, "c", SWAP)
    logits, stats = call(
        total_kernel,
        [partial, struct((lax.axis_size("z"), 8, 128), f32)],
        [own, q1_low, q1_high, q3_low, q3_high, turned, hid_theirs],
        [pltpu.VMEM((tokens, 128), f32)],
        loose=2,
    )

    stats = lax.all_to_all(stats, "z", 0, 0, tiled=True)
    everyone = DP + ("y",)
    stats = call(
        merge_kernel,
        struct((lax.axis_size(everyone), 8, 128), f32),
        [stats, valid.reshape(1, tokens), advantage.reshape(1, tokens)],
    )
    stats = lax.all_to_all(stats, everyone, 0, 0, tiled=True)
    start_high = float(np.float32(np.log(np.float32(voc_cols * n_voc))) + np.float32(1.0))
    table = struct((n_dp, tokens), f32)
    coef_all, normal_all, packed_all, slot_all, flag = call(
        functools.partial(plan_kernel, start_high),
        [table] * 4 + [struct((1, 1), jnp.int32)],
        [stats],
        [pltpu.VMEM((n_dp, 8, 128), f32)],
        out_specs=[pl.BlockSpec(memory_space=pltpu.VMEM)] * 4 + [pl.BlockSpec(memory_space=pltpu.SMEM)],
    )

    def backward(cap):
        piece = call(
            slopes_kernel,
            struct((cap, voc_cols), bf16),
            [at, logits, coef_all, normal_all, packed_all, token_ids.reshape(1, tokens)],
            smem=1,
        )
        pieces = {s: lax.ppermute(piece, "x", ring(nx, s)) for s in (2, 1, 3)}
        mine = jnp.concatenate([piece, pieces[1], pieces[2], pieces[3]], axis=0)
        theirs = lax.ppermute(mine, "c", SWAP)
        first = call(
            half_kernel,
            struct((nx * cap, rows), bf16),
            [mine, turned],
            cost_estimate=estimate(nx * cap, voc_cols, rows),
        )
        return call(
            product_kernel,
            [struct((2 * nx * cap, voc_cols), bf16)] + [struct((2 * cap, rows), bf16)] * nx,
            [at, mine, theirs, turned, first],
            [pltpu.VMEM((2 * nx * cap, rows), bf16)],
            smem=1,
        )

    def finish(slopes, *parts):
        parts = [parts[0]] + [lax.ppermute(parts[k], "y", ring(nx, k)) for k in range(1, nx)]
        sides = (at, packed_all, hid_mine, hid_theirs, slopes)
        blocks = rows // 128
        early = (blocks + 1) // 2
        head_grad, tick = outer(*sides, 0, early, packed_all, packed_all)
        spread, tick = call(
            spread_kernel,
            [struct((n_voc * CAP // nx, rows + 128), jnp.int16), tick_shape],
            [at, tick, *parts, packed_all, slot_all],
            smem=1,
        )
        spread = lax.all_to_all(spread, "z", 0, 0, tiled=True)
        head_grad, _ = outer(*sides, early, blocks - early, head_grad, tick)
        hidden_grad = call(
            sum_kernel,
            struct((tokens * n_dp // n_voc, rows), f32),
            [at, spread, slot_all],
            [pltpu.VMEM((tokens, 8), f32)],
            smem=1,
        )
        return hidden_grad, head_grad

    def whole(_):
        return dense(hidden_states, head, token_ids, valid, advantage)

    packed_rows = backward(CAP_SMALL)

    def small(_):
        return finish(*packed_rows)

    def large(_):
        return finish(*backward(CAP * n_voc // n_dp))

    return lax.switch(flag[0, 0], [small, large, whole], 0)


def solution(mesh):
    chips = Mesh(mesh.devices.reshape(4, 2, 4, 8), DP + VOC)
    placed = (P(DP, None), P(DP, VOC), P(DP), P(DP), P(DP))
    return jax.shard_map(
        shards,
        mesh=chips,
        in_specs=placed,
        out_specs=(P(VOC, DP), P(DP, VOC)),
        check_vma=False,
    )
```

```python
import functools

import jax
import jax.numpy as jnp
import numpy as np
from jax import lax
from jax.experimental import pallas as pl
from jax.experimental.pallas import tpu as pltpu
from jax.sharding import Mesh, PartitionSpec as P

ROUNDS = 24
LEVELS = 8
CAP = 16
CAP_SMALL = 32
ORDER = (2, 0, 3, 1)
NX = 4

ramp_width = 0.5
DP = ("x", "c")
VOC = ("y", "z")
f32 = jnp.float32
bf16 = jnp.bfloat16


def ring(n, shift):
    return [(i, (i + shift) % n) for i in range(n)]


SWAP = [(0, 1), (1, 0)]


def dense(hidden_states, head, token_ids, valid, advantage):
    voc_cols = head.shape[1]
    columns = lax.all_to_all(hidden_states, DP, split_axis=1, concat_axis=0, tiled=True)
    logits = lax.psum_scatter(
        jnp.dot(columns, head, preferred_element_type=f32), DP, scatter_dimension=0, tiled=True
    )
    offset = lax.axis_index(VOC) * voc_cols
    hit = jnp.arange(voc_cols, dtype=jnp.int32)[None, :] + offset == token_ids[:, None]
    highest = lax.pmax(jnp.max(logits, axis=1), VOC)
    shifted = jnp.exp(logits - highest[:, None])
    total, moment = lax.psum((jnp.sum(shifted, axis=1), jnp.sum(shifted * logits, axis=1)), VOC)
    normal = highest + jnp.log(total)
    entropy = normal - moment / total
    validf = valid.astype(f32)
    start_high = jnp.log(f32(voc_cols * lax.axis_size(VOC))) + 1.0
    counted = lax.psum(jnp.sum(validf), DP)
    quota = jnp.floor((counted + 0.5) * 0.2)

    def round_step(step, bounds):
        low, high = bounds
        middle = (low + high) * 0.5
        above = lax.psum(jnp.sum(jnp.where(entropy > middle, validf, 0.0)), DP)
        more = above > quota
        return (jnp.where(more, middle, low), jnp.where(more, high, middle))

    _, threshold = lax.fori_loop(0, ROUNDS, round_step, (f32(0.0), start_high))
    gate = validf * jnp.clip((entropy - threshold) / ramp_width + 0.5, 0.0, 1.0)
    coef = -(gate * advantage)
    probs = jnp.exp(logits - normal[:, None])
    slopes = (coef[:, None] * (hit.astype(f32) - probs)).astype(bf16)
    piece = lax.all_gather(slopes, DP, axis=0, tiled=True)
    head_grad = lax.dot_general(columns, piece, (((0,), (0,)), ((), ())), preferred_element_type=f32)
    product = lax.dot_general(piece, head, (((1,), (1,)), ((), ())), preferred_element_type=f32)
    return lax.psum_scatter(product, VOC, scatter_dimension=0, tiled=True), head_grad


def bisect(entropy, counted, start_high):
    columns = jnp.transpose(entropy)
    quota = jnp.floor((counted + 0.5) * 0.2)
    leaves = 1 << LEVELS
    lane = lax.broadcasted_iota(jnp.int32, (1, leaves), 1)
    low = jnp.zeros((1, leaves), f32)
    high = jnp.full((1, leaves), start_high, f32)
    for _ in range(ROUNDS // LEVELS):
        for level in range(LEVELS):
            middle = (low + high) * 0.5
            bit = ((lane >> (LEVELS - 1 - level)) & 1) == 1
            low, high = jnp.where(bit, middle, low), jnp.where(bit, high, middle)
        above = jnp.zeros((128, leaves), f32)
        for i in range(8):
            above = above + jnp.where(columns[:, i : i + 1] > low, 1.0, 0.0)
        above = jnp.sum(above, axis=0, keepdims=True)
        more = jnp.where((above > quota) | (lane == 0), 1.0, 0.0)
        here = lane == jnp.sum(more, axis=1, keepdims=True).astype(jnp.int32) - 1
        low, high = (
            jnp.broadcast_to(jnp.sum(jnp.where(here, v, 0.0), axis=1, keepdims=True), (1, leaves))
            for v in (low, high)
        )
    return high[:, :1]


def call(kernel, out, args, scratch=(), vmem=16, smem=0, loose=0, **kw):
    specs = [pl.BlockSpec(memory_space=pltpu.SMEM)] * smem
    specs += [pl.BlockSpec(memory_space=pltpu.VMEM)] * (len(args) - smem - loose)
    specs += [pl.BlockSpec(memory_space=pl.ANY)] * loose
    return pl.pallas_call(
        kernel,
        in_specs=specs,
        out_shape=out,
        scratch_shapes=list(scratch),
        compiler_params=pltpu.CompilerParams(vmem_limit_bytes=vmem << 20),
        **kw,
    )(*args)


def struct(shape, dtype):
    return jax.ShapeDtypeStruct(shape, dtype)


def estimate(m, k, n):
    return pl.CostEstimate(flops=2 * m * k * n, bytes_accessed=2 * k * n, transcendentals=0)


LN2_64 = float(np.log(2.0) / 64.0)


def split_kernel(at, hidden, b0, b1, b2, b3):
    chip_rows = b0.shape[1]
    nx = hidden.shape[1] // chip_rows
    for s, out in enumerate((b0, b1, b2, b3)):
        to = lax.rem(at[0] + s, nx) * chip_rows
        out[...] = hidden[:, pl.ds(pl.multiple_of(to, 128), chip_rows)]


def turn_kernel(tick, head, turned):
    for k in range(head.shape[1] // 128):
        span = slice(k * 128, (k + 1) * 128)
        turned[span, :] = jnp.transpose(head[:, span])


def pack(block, out, to):
    step, cols = block.shape
    top = jnp.maximum(jnp.max(jnp.abs(block), axis=1, keepdims=True), 1e-30)
    power = jnp.ceil(jnp.log(top) * (1.0 / LN2_64)) + 1.0
    fixed = jnp.round(block * (jnp.exp(power * -LN2_64) * 32766.0))
    out[to, 0:cols] = fixed.astype(jnp.int32).astype(jnp.int16)
    wide_power = jnp.broadcast_to(power.astype(jnp.int32), (step, 128))
    out[to, cols : cols + 128] = wide_power.astype(jnp.int16)


def pack_rows(part, start, out):
    step = 16
    for row in range(0, out.shape[0], step):
        pack(part[start + row : start + row + step, :], out, slice(row, row + step))


def unpack(ref, at):
    cols = ref.shape[1] - 128
    power = ref[at, cols : cols + 128].astype(jnp.int32).astype(f32)[:, :1]
    return ref[at, 0:cols].astype(jnp.int32).astype(f32) * (jnp.exp(power * LN2_64) * (1.0 / 32766.0))


def over_columns(cols, tile):
    for start in range(0, cols, 256):
        tile(slice(start, min(start + 256, cols)))


def halves(at, rows):
    return (
        pl.ds(pl.multiple_of(at[1] * rows, 128), rows),
        pl.ds(pl.multiple_of((1 - at[1]) * rows, 128), rows),
    )


def own_kernel(at, block, head, other, own, kept):
    kept[...] = head[...]
    here, there = halves(at, head.shape[0])

    def tile(span):
        own[:, span] = jnp.dot(block[:, here], head[:, span], preferred_element_type=f32) + jnp.dot(
            block[:, there], other[:, span], preferred_element_type=f32
        )

    over_columns(head.shape[1], tile)


def far_kernel(at, block, head, other, low, high, tick, part):
    tokens = block.shape[0]
    rows, cols = head.shape
    here, there = halves(at, rows)

    def tile(span):
        part[:, span] = jnp.dot(block[:, here], head[:, span], preferred_element_type=f32) + jnp.dot(
            block[:, there], other[:, span], preferred_element_type=f32
        )

    over_columns(cols, tile)
    tick[...] = jnp.zeros(tick.shape, f32)
    half = tokens // 2
    pack_rows(part, 0, low)
    pack_rows(part, half, high)


def near_kernel(at, tick, b0, b1, b2, b3, head, other, p1, p3, q1, q3, mine, theirs, part):
    tokens = b0.shape[0]
    half = tokens // 2
    rows, cols = head.shape
    here, there = halves(at, rows)
    for k, block in enumerate((b1, b3, b0, b2)):
        mine[k * tokens : (k + 1) * tokens, :] = block[:, here]
        theirs[k * tokens : (k + 1) * tokens, :] = block[:, there]

    def tile(span):
        both = jnp.dot(mine[0 : 2 * tokens, :], head[:, span], preferred_element_type=f32) + jnp.dot(
            theirs[0 : 2 * tokens, :], other[:, span], preferred_element_type=f32
        )
        p1[:, span] = both[0:half, :]
        part[:, span] = both[half : tokens + half, :]
        p3[:, span] = both[tokens + half :, :]

    over_columns(cols, tile)
    pack_rows(part, 0, q1)
    pack_rows(part, half, q3)


def relay_kernel(p1, p3, low, high, q1, q3, tick):
    step = 16
    tick[...] = jnp.zeros(tick.shape, f32)
    for start in range(0, p1.shape[0], step):
        at = slice(start, start + step)
        pack(p1[at, :] + unpack(low, at), q1, at)
        pack(p3[at, :] + unpack(high, at), q3, at)


def total_kernel(own, q1_low, q1_high, q3_low, q3_high, turned, theirs, logits, sent, stats):
    tokens = own.shape[0]
    step = 16
    lane = lax.broadcasted_iota(jnp.int32, (step, 128), 1)
    for start in range(0, tokens, step):
        at = slice(start, start + step)
        q1, q3 = (q1_low, q3_low) if start < tokens // 2 else (q1_high, q3_high)
        part = slice(start % (tokens // 2), start % (tokens // 2) + step)
        value = own[at, :] + unpack(q1, part) + unpack(q3, part)
        logits[at, :] = value
        high = jnp.max(value, axis=1, keepdims=True)
        shifted = jnp.exp(value - high)
        total = jnp.sum(shifted, axis=1, keepdims=True)
        moment = jnp.sum(shifted * value, axis=1, keepdims=True)
        stats[at, :] = jnp.where(lane == 0, high, jnp.where(lane == 1, total, moment))

    rows = jnp.transpose(stats[...])[0:8, :]
    for i in range(sent.shape[0]):
        sent[i] = rows


def merge_kernel(parts, valid, advantage, sent):
    high = parts[0, 0:1, :]
    for i in range(1, parts.shape[0]):
        high = jnp.maximum(high, parts[i, 0:1, :])
    sums = jnp.zeros((8, 128), f32)
    for i in range(parts.shape[0]):
        sums = sums + jnp.exp(parts[i, 0:1, :] - high) * parts[i]
    row = lax.broadcasted_iota(jnp.int32, (8, 128), 0)
    out = jnp.where(row == 0, high, sums)
    out = jnp.where(row == 3, valid[...].astype(f32), jnp.where(row == 4, advantage[...], out))
    for i in range(sent.shape[0]):
        sent[i] = out


def plan_kernel(start_high, parts, coef_out, normal_out, packed_out, slot_out, flag, rows):
    owners = 8
    ny = parts.shape[0] // owners
    for o in range(owners):
        high = parts[o * ny, 0:1, :]
        for y in range(1, ny):
            high = jnp.maximum(high, parts[o * ny + y, 0:1, :])
        sums = jnp.zeros((8, 128), f32)
        for y in range(ny):
            sums = sums + jnp.exp(parts[o * ny + y, 0:1, :] - high) * parts[o * ny + y]
        row = lax.broadcasted_iota(jnp.int32, (8, 128), 0)
        normal = high + jnp.log(sums[1:2, :])
        entropy = normal - sums[2:3, :] / sums[1:2, :]
        rows[o] = jnp.where(row == 0, normal, jnp.where(row == 1, entropy, parts[o * ny]))
    normal, entropy, valid, advantage = (
        jnp.concatenate([rows[o, k : k + 1, :] for o in range(owners)], axis=0) for k in (0, 1, 3, 4)
    )
    counted = jnp.sum(jnp.sum(valid, axis=1, keepdims=True), axis=0, keepdims=True)
    threshold = bisect(jnp.where(valid > 0.0, entropy, -jnp.inf), counted, start_high)
    gate = valid * jnp.clip((entropy - threshold) / ramp_width + 0.5, 0.0, 1.0)
    coef = -(gate * advantage)
    active = coef != 0.0
    activef = active.astype(f32)
    i = lax.broadcasted_iota(jnp.int32, (128, 128), 0)
    j = lax.broadcasted_iota(jnp.int32, (128, 128), 1)
    ahead = (i < j).astype(f32)
    group = 128 // (32 // owners)
    same = (i // group == j // group).astype(f32)
    rank_owner = jnp.dot(activef, ahead, preferred_element_type=f32)
    rank_group = jnp.dot(activef, ahead * same, preferred_element_type=f32)
    start = (lax.broadcasted_iota(jnp.int32, (8, 128), 1) // group * CAP).astype(f32)
    coef_out[...] = coef
    normal_out[...] = normal
    packed_out[...] = jnp.where(active, rank_owner, -1.0)
    slot_out[...] = jnp.where(active, rank_group + start, -1.0)
    over = jnp.where(active & (rank_owner >= CAP_SMALL), 1.0, 0.0)
    over = jnp.where(active & (rank_group >= CAP), 2.0, over)
    flag[0, 0] = jnp.max(over).astype(jnp.int32)


def as_columns(rows):
    row = lax.broadcasted_iota(jnp.int32, (8, 128), 0)
    out = jnp.zeros((8, 128), f32)
    for k, value in enumerate(rows):
        out = jnp.where(row == k, value, out)
    return jnp.transpose(out)


def one_hot(count, slots):
    row = lax.broadcasted_iota(jnp.int32, (count, 128), 0).astype(f32)
    return (row == slots).astype(f32).astype(bf16)


def slopes_kernel(at, logits, coef_all, normal_all, packed_all, ids, out):
    me = pl.ds(at[2], 1)
    count = out.shape[0]
    columns = as_columns([coef_all[me, :], normal_all[me, :], ids[...].astype(f32)])
    coef, normal, token = columns[:, 0:1], columns[:, 1:2], columns[:, 2:3].astype(jnp.int32) - at[3]
    choose = one_hot(count, packed_all[me, :])
    lane = lax.broadcasted_iota(jnp.int32, (128, 128), 1)
    for k in range(logits.shape[1] // 128):
        span = slice(k * 128, (k + 1) * 128)
        hit = (lane + k * 128 == token).astype(f32)
        slopes = (coef * (hit - jnp.exp(logits[:, span] - normal))).astype(bf16)
        out[:, span] = jnp.dot(choose, slopes, preferred_element_type=f32).astype(bf16)


def owner_of(at, s, k):
    return lax.rem(at[0] - s + NX, NX) * 2 + lax.rem(at[1] + k, 2)


def half_kernel(m0, m1, m2, m3, turned, slopes, out):
    cap = m0.shape[0]
    for s, rows in enumerate((m0, m1, m2, m3)):
        slopes[s * cap : (s + 1) * cap, :] = rows[...]
    out[...] = jnp.dot(slopes[...], turned[...], preferred_element_type=f32).astype(bf16)


def product_kernel(at, mine, t0, t1, t2, t3, turned, first, slopes, o0, o1, o2, o3, held):
    half = mine.shape[0]
    cap = half // NX
    slopes[0:half, :] = mine[...]
    for s, rows in enumerate((t0, t1, t2, t3)):
        slopes[half + s * cap : half + (s + 1) * cap, :] = rows[...]
    held[0:half, :] = first[...]
    held[half:, :] = jnp.dot(slopes[half:, :], turned[...], preferred_element_type=f32).astype(bf16)
    for step, out in enumerate((o0, o1, o2, o3)):
        source = lax.rem(at[0] - at[5] - step + 2 * NX, NX) * cap
        for k in range(2):
            rows = pl.ds(pl.multiple_of(source + k * half, cap), cap)
            out[k * cap : (k + 1) * cap, :] = held[rows, :]


def outer_kernel(at, packed_all, hid_mine, hid_theirs, slopes, above, after, out, tick, held):
    half = slopes.shape[0] // 2
    cap = half // NX
    tick[...] = jnp.zeros(tick.shape, f32)
    for k, hidden in enumerate((hid_mine, hid_theirs)):
        for s in range(NX):
            choose = one_hot(cap, packed_all[pl.ds(owner_of(at, s, k), 1), :])
            to = k * half + s * cap
            held[to : to + cap, :] = jnp.dot(
                choose, hidden[ORDER[s] * 128 : (ORDER[s] + 1) * 128, :], preferred_element_type=f32
            ).astype(bf16)
    out[...] = lax.dot_general(
        held[...], slopes[...], (((0,), (0,)), ((), ())), preferred_element_type=f32
    )


def outer(at, packed_all, hid_mine, hid_theirs, slopes, first, count, above, after):
    (tokens, rows), (depth, cols) = hid_mine.shape, slopes.shape
    tile = 128
    whole_block = lambda i: (0, 0)
    in_specs = [
        pl.BlockSpec(memory_space=pltpu.SMEM),
        pl.BlockSpec(packed_all.shape, whole_block),
        pl.BlockSpec((tokens, tile), lambda i: (0, i + first)),
        pl.BlockSpec((tokens, tile), lambda i: (0, i + first)),
        pl.BlockSpec((depth, cols), whole_block),
        pl.BlockSpec(memory_space=pl.ANY),
        pl.BlockSpec(memory_space=pl.ANY),
    ]
    aliases = {5: 0} if above.shape == (rows, cols) else {}
    return pl.pallas_call(
        outer_kernel,
        grid=(count,),
        in_specs=in_specs,
        out_specs=[pl.BlockSpec((tile, cols), lambda i: (i + first, 0)), pl.BlockSpec((8, 128), whole_block)],
        out_shape=[struct((rows, cols), f32), struct((8, 128), f32)],
        scratch_shapes=[pltpu.VMEM((depth, tile), bf16)],
        input_output_aliases=aliases,
        compiler_params=pltpu.CompilerParams(vmem_limit_bytes=24 << 20),
        cost_estimate=estimate(count * tile, depth, cols),
    )(at, packed_all, hid_mine, hid_theirs, slopes, above, after)


def spread_kernel(at, before, r0, r1, r2, r3, packed_all, slot_all, out, tick):
    size = out.shape[0]
    cap = r0.shape[0] // 2
    tick[...] = jnp.zeros(tick.shape, f32)
    spread = []
    for k in range(2):
        core = lax.rem(at[1] + k, 2)
        me = pl.ds(at[5] * 2 + core, 1)
        slot = slot_all[me, :]
        slot = jnp.where(slot >= 0.0, slot + (core * (size // 2)).astype(f32), -1.0)
        part = lax.dot_general(
            one_hot(size, slot),
            one_hot(cap, packed_all[me, :]),
            (((1,), (1,)), ((), ())),
            preferred_element_type=f32,
        )
        spread.append(part.astype(bf16))
    spread = jnp.concatenate(spread, axis=1)
    total = jnp.zeros((size, r0.shape[1]), f32)
    for r in (r0, r1, r2, r3):
        total = total + jnp.dot(spread, r[...], preferred_element_type=f32)
    pack(total, out, slice(0, size))


def sum_kernel(at, parts, slot_all, out, ranks):
    total = unpack(parts, slice(0, CAP))
    for i in range(1, parts.shape[0] // CAP):
        total = total + unpack(parts, slice(i * CAP, (i + 1) * CAP))
    group = out.shape[0]
    per_owner = 128 // group
    owner, place = at[4] // per_owner, lax.rem(at[4], per_owner)
    ranks[...] = as_columns([slot_all[pl.ds(owner, 1), :]])
    rank = ranks[pl.ds(pl.multiple_of(place * group, group), group), :][:, 0:1]
    rank = rank - (place * CAP).astype(f32)
    rows = jnp.zeros(out.shape, f32)
    for r in range(CAP):
        rows = rows + jnp.where(rank == float(r), total[r : r + 1, :], 0.0)
    out[...] = rows


def shards(hidden_states, head, token_ids, valid, advantage):
    tokens, width = hidden_states.shape
    rows, voc_cols = head.shape
    nx, n_voc, n_dp = lax.axis_size("x"), lax.axis_size(VOC), lax.axis_size(DP)
    x, c, block = lax.axis_index("x"), lax.axis_index("c"), lax.axis_index(VOC)
    at = jnp.stack([x, c, x * 2 + c, block * voc_cols, block, lax.axis_index("y")]).astype(jnp.int32)
    chip_rows = width // nx

    head_other = lax.ppermute(head, "c", SWAP)

    block_shape = struct((tokens, chip_rows), bf16)
    b0, *leave = call(split_kernel, [block_shape] * 4, [at, hidden_states], smem=1)
    came = {s: lax.ppermute(leave[s - 1], "x", ring(nx, s)) for s in (2, 1, 3)}
    partial = struct((tokens, voc_cols), f32)
    tick_shape = struct((8, 128), f32)
    own, kept = call(
        own_kernel,
        [partial, struct((rows, voc_cols), bf16)],
        [at, b0, head, head_other],
        smem=1,
        cost_estimate=estimate(tokens, chip_rows, voc_cols),
    )
    half = struct((tokens // 2, voc_cols + 128), jnp.int16)
    low, high, tick = call(
        far_kernel,
        [half, half, tick_shape],
        [at, came[2], kept, head_other],
        [pltpu.VMEM((tokens, voc_cols), f32)],
        smem=1,
        cost_estimate=estimate(tokens, chip_rows, voc_cols),
    )
    low, high = lax.ppermute(low, "x", ring(nx, -1)), lax.ppermute(high, "x", ring(nx, 1))
    half_partial = struct((tokens // 2, voc_cols), f32)
    p1, p3, q1_high, q3_low, hid_mine, hid_send = call(
        near_kernel,
        [half_partial] * 2 + [half] * 2 + [struct((nx * tokens, rows), bf16)] * 2,
        [at, tick, b0, came[1], came[2], came[3], kept, head_other],
        [pltpu.VMEM((tokens, voc_cols), f32)],
        vmem=24,
        smem=1,
        cost_estimate=estimate(2 * tokens, chip_rows, voc_cols),
    )
    q1_high, q3_low = lax.ppermute(q1_high, "x", ring(nx, -1)), lax.ppermute(q3_low, "x", ring(nx, 1))
    q1_low, q3_high, tick = call(relay_kernel, [half] * 2 + [tick_shape], [p1, p3, low, high])
    q1_low, q3_high = lax.ppermute(q1_low, "x", ring(nx, -1)), lax.ppermute(q3_high, "x", ring(nx, 1))
    turned = call(turn_kernel, struct((voc_cols, rows), bf16), [tick, kept])
    hid_theirs = lax.ppermute(hid_send, "c", SWAP)
    logits, stats = call(
        total_kernel,
        [partial, struct((lax.axis_size("z"), 8, 128), f32)],
        [own, q1_low, q1_high, q3_low, q3_high, turned, hid_theirs],
        [pltpu.VMEM((tokens, 128), f32)],
        loose=2,
    )

    stats = lax.all_to_all(stats, "z", 0, 0, tiled=True)
    everyone = DP + ("y",)
    stats = call(
        merge_kernel,
        struct((lax.axis_size(everyone), 8, 128), f32),
        [stats, valid.reshape(1, tokens), advantage.reshape(1, tokens)],
    )
    stats = lax.all_to_all(stats, everyone, 0, 0, tiled=True)
    start_high = float(np.float32(np.log(np.float32(voc_cols * n_voc))) + np.float32(1.0))
    table = struct((n_dp, tokens), f32)
    coef_all, normal_all, packed_all, slot_all, flag = call(
        functools.partial(plan_kernel, start_high),
        [table] * 4 + [struct((1, 1), jnp.int32)],
        [stats],
        [pltpu.VMEM((n_dp, 8, 128), f32)],
        out_specs=[pl.BlockSpec(memory_space=pltpu.VMEM)] * 4 + [pl.BlockSpec(memory_space=pltpu.SMEM)],
    )

    def backward(cap):
        piece = call(
            slopes_kernel,
            struct((cap, voc_cols), bf16),
            [at, logits, coef_all, normal_all, packed_all, token_ids.reshape(1, tokens)],
            smem=1,
        )
        pieces = {s: lax.ppermute(piece, "x", ring(nx, s)) for s in (2, 1, 3)}
        pieces[0] = piece
        theirs = {s: lax.ppermute(pieces[s], "c", SWAP) for s in (0, 2, 1, 3)}
        mine, first = call(
            half_kernel,
            [struct((nx * cap, voc_cols), bf16), struct((nx * cap, rows), bf16)],
            [pieces[s] for s in range(nx)] + [turned],
            cost_estimate=estimate(nx * cap, voc_cols, rows),
        )
        return call(
            product_kernel,
            [struct((2 * nx * cap, voc_cols), bf16)] + [struct((2 * cap, rows), bf16)] * nx,
            [at, mine, *[theirs[s] for s in range(nx)], turned, first],
            [pltpu.VMEM((2 * nx * cap, rows), bf16)],
            smem=1,
        )

    def finish(slopes, *parts):
        parts = [parts[0]] + [lax.ppermute(parts[k], "y", ring(nx, k)) for k in range(1, nx)]
        sides = (at, packed_all, hid_mine, hid_theirs, slopes)
        blocks = rows // 128
        early = blocks // 2
        head_grad, tick = outer(*sides, 0, early, packed_all, packed_all)
        spread, tick = call(
            spread_kernel,
            [struct((n_voc * CAP // nx, rows + 128), jnp.int16), tick_shape],
            [at, tick, *parts, packed_all, slot_all],
            smem=1,
        )
        spread = lax.all_to_all(spread, "z", 0, 0, tiled=True)
        head_grad, _ = outer(*sides, early, blocks - early, head_grad, tick)
        hidden_grad = call(
            sum_kernel,
            struct((tokens * n_dp // n_voc, rows), f32),
            [at, spread, slot_all],
            [pltpu.VMEM((tokens, 8), f32)],
            smem=1,
        )
        return hidden_grad, head_grad

    def whole(_):
        return dense(hidden_states, head, token_ids, valid, advantage)

    packed_rows = backward(CAP_SMALL)

    def small(_):
        return finish(*packed_rows)

    def large(_):
        return finish(*backward(CAP * n_voc // n_dp))

    return lax.switch(flag[0, 0], [small, large, whole], 0)


def solution(mesh):
    chips = Mesh(mesh.devices.reshape(4, 2, 4, 8), DP + VOC)
    placed = (P(DP, None), P(DP, VOC), P(DP), P(DP), P(DP))
    return jax.shard_map(
        shards,
        mesh=chips,
        in_specs=placed,
        out_specs=(P(VOC, DP), P(DP, VOC)),
        check_vma=False,
    )
```
